32 devices in a mesh: tm: 8 (over y, x, core), space: 4 (over z).
Axes of the slice: x: 2, y: 2, z: 4, core: 2. Of those that a mesh axis runs over, the one named last changes fastest.
Arguments:
- frames_in: bfloat16 [8, 128, 128, 256], P('tm', 'space'), may hold values from -6 to 6
- w_input: bfloat16 [3, 3, 256, 256], replicated, may hold values from -0.125 to 0.125
- decay_rate: float32 [128], replicated, may hold values from 0.001 to 0.2
- phase: float32 [128], replicated, may hold values from -3.140625 to 3.140625
- w_output: bfloat16 [3, 3, 256, 256], replicated, may hold values from -0.125 to 0.125
Outputs:
- frames_out: bfloat16 [8, 128, 128, 256], P('tm', 'space')
The draws below stay inside these ranges and needn't reach their ends.
All inputs are finite; a program needn't handle non-finite values.
Results may differ from the reference program's by a relative error of at most 0.0029.
Values may be sent and summed in bfloat16 or wider, within the bound.
No kernel may reach another device: no remote copies, remote signals or barrier semaphores. Data moves between devices by JAX's collectives and lax.ppermute only.
A program may use at most 192 MiB of HBM per device.

```python
import math
import jax
import jax.numpy as jnp
from jax import lax

C = 256
P_SIZE = 128
HEIGHT = 128
W = 128
FRAMES = 8


def shard_levels(stream_key, extent, cuts, least, largest):
    level = 1.0
    for position, shards_of in cuts:
        steps = jax.random.uniform(jax.random.fold_in(jax.random.fold_in(stream_key, 6), position), (shards_of,), jnp.float32, least / len(cuts), largest / len(cuts))
        level = level * jnp.repeat(jnp.exp(steps), extent[position] // shards_of).reshape((-1,) + (1,) * (len(extent) - 1 - position))
    return level


def gaussian(stream_key, extent, spread, most, cuts=(), dtype=jnp.bfloat16):
    values = spread * jax.random.normal(stream_key, extent, jnp.float32)
    if cuts:
        values = values * shard_levels(stream_key, extent, cuts, -0.22, 0.18)
    return jnp.clip(values, -most, most).astype(dtype)


def setup_inputs(seed: int = 0) -> dict:
    key_list = jax.random.split(jax.random.key(seed), 6)
    frames_in = gaussian(key_list[0], (FRAMES, HEIGHT, W, C), 1.0, 6.0, ((0, 8), (1, 4)))
    w_input = gaussian(key_list[1], (3, 3, C, 2 * P_SIZE), (9 * C) ** -0.5, 0.125)
    decay_rate = jnp.clip(jnp.exp(jax.random.uniform(key_list[2], (P_SIZE,), jnp.float32, math.log(0.001), math.log(0.2))), 0.001, 0.2)
    phase = jnp.clip(jax.random.uniform(key_list[3], (P_SIZE,), jnp.float32, -3.140625, 3.140625), -3.140625, 3.140625)
    w_output = gaussian(key_list[4], (3, 3, 2 * P_SIZE, C), (18 * P_SIZE) ** -0.5, 0.125)
    return dict(frames_in=frames_in, w_input=w_input, decay_rate=decay_rate, phase=phase, w_output=w_output)


def convolve(data, kernel):
    return lax.conv_general_dilated(data.astype(jnp.float32), kernel.astype(jnp.float32), (1, 1), ((1, 1), (1, 1)), dimension_numbers=('NHWC', 'HWIO', 'NHWC'), precision=lax.Precision.HIGHEST)

def reference(frames_in, w_input, decay_rate, phase, w_output):
    drive = convolve(frames_in, w_input)
    magnitude = jnp.exp(-decay_rate)
    lam_re = magnitude * jnp.cos(phase)
    lam_im = magnitude * jnp.sin(phase)
    factor = jnp.sqrt(1.0 - magnitude * magnitude)
    feed = drive * jnp.concatenate([factor, factor])

    def advance(carry, item):
        prev_re, prev_im = carry
        new_re = lam_re * prev_re - lam_im * prev_im + item[..., :P_SIZE]
        new_im = lam_re * prev_im + lam_im * prev_re + item[..., P_SIZE:]
        return ((new_re, new_im), jnp.concatenate([new_re, new_im], axis=-1).astype(jnp.bfloat16))
    start = jnp.zeros(feed.shape[1:3] + (P_SIZE,), jnp.float32)
    final, state_b = lax.scan(advance, (start, start), feed)
    mixed = convolve(state_b, w_output)
    return (frames_in.astype(jnp.float32) + jax.nn.gelu(mixed, approximate=False)).astype(jnp.bfloat16)
```

```python
import functools

import numpy as np
import jax
import jax.numpy as jnp
from jax import lax
from jax.experimental import pallas as pl
from jax.experimental.pallas import tpu as pltpu
from jax.sharding import PartitionSpec as P

F32 = jnp.float32
BF16 = jnp.bfloat16
VMEM = pl.BlockSpec(memory_space=pltpu.VMEM)
SMEM = pl.BlockSpec(memory_space=pltpu.SMEM)
PARAMS = pltpu.CompilerParams(vmem_limit_bytes=48 * 1024 * 1024)


def cmul(coef, z):
    n = z.shape[-1] // 2
    re, im = z[..., :n], z[..., n:]
    cr, ci = coef
    return jnp.concatenate([cr * re - ci * im, cr * im + ci * re], axis=-1)


def widen(row):
    w = row.shape[0]
    col = lax.broadcasted_iota(jnp.int32, row.shape, 0)
    left = jnp.where(col == 0, 0.0, pltpu.roll(row, 1, 0))
    right = jnp.where(col == w - 1, 0.0, pltpu.roll(row, w - 1, 0))
    return jnp.concatenate([left, row, right], axis=-1).astype(BF16)


def conv_block(wide, w_ref, start, count):
    w, k = wide.shape[1], wide.shape[2]
    lhs = jnp.concatenate(
        [wide[start + d : start + d + count].reshape(count * w, k) for d in range(3)], axis=-1
    )
    return jnp.dot(lhs, w_ref[...], preferred_element_type=F32)


def blocks(total, size):
    return [(s, min(size, total - s)) for s in range(0, total, size)]


def coefficient(tab_ref, i):
    return tab_ref[2 * i : 2 * i + 1, :], tab_ref[2 * i + 1 : 2 * i + 2, :]


def drive_kernel(pieces, segments, step, *refs):
    idx, edge, decay, w_ref = refs[:4]
    xs = refs[4 : 4 + len(pieces)]
    feed, send, wide = refs[4 + len(pieces) :]
    n_states = decay.shape[1]
    mag = jnp.exp(-decay[...])
    factor = jnp.sqrt(1.0 - mag * mag)
    factor = jnp.concatenate([factor, factor], axis=-1)
    at = 0
    for ref, (lo, hi) in zip(xs, pieces):
        for r in range(lo, hi):
            wide[at] = widen(ref[r].astype(F32))
            at += 1
    quarters = feed.shape[1]
    half = quarters // 2
    other = (1 - idx[0]) * half
    out = 0
    for first, count, mask in segments:
        for s, size in blocks(count, step):
            acc = conv_block(wide, w_ref, first + s, size) * factor
            acc = acc.reshape((size,) + feed.shape[1:])
            for r in range(size):
                row = acc[r]
                if mask is not None and mask[0] == s + r:
                    row = row * edge[mask[1]]
                feed[out + r] = row
            out += size
    send[...] = feed[:, pl.ds(other, half)].astype(BF16)


def drive(xs, pieces, segments, rows, idx, edge, decay, w_in, quarters, step):
    w, c = xs[0].shape[1:]
    n_wide = sum(hi - lo for lo, hi in pieces)
    flops = 2 * rows * w * w_in.shape[0] * w_in.shape[1]
    return pl.pallas_call(
        functools.partial(drive_kernel, pieces, segments, step),
        out_shape=(
            jax.ShapeDtypeStruct((rows, quarters, w // quarters, c), F32),
            jax.ShapeDtypeStruct((rows, quarters // 2, w // quarters, c), BF16),
        ),
        in_specs=[SMEM, SMEM, VMEM, VMEM] + [VMEM] * len(xs),
        out_specs=(VMEM, VMEM),
        scratch_shapes=[pltpu.VMEM((n_wide, w, 3 * c), BF16)],
        compiler_params=PARAMS,
        cost_estimate=pl.CostEstimate(flops=flops, bytes_accessed=rows * w * c * 8, transcendentals=0),
        name="drive",
    )(idx, edge, decay, w_in, *xs)


def mix_kernel(terms, outs, *refs):
    idx, tab = refs[:2]
    srcs = refs[2 : 2 + len(terms)]
    dsts = refs[2 + len(terms) :]
    rows = srcs[0].shape[0]
    picks = []
    for plan in outs:
        picks.append([(coefficient(tab, k), srcs[s], idx[p] if isinstance(p, int) else None, p) for k, s, p in plan])

    def one(r, _):
        for dst, plan in zip(dsts, picks):
            total = None
            for coef, src, where, p in plan:
                if p == "all":
                    z = src[r]
                elif isinstance(p, tuple):
                    z = src[r, p[0] : p[0] + p[1]]
                else:
                    z = src[r, pl.ds(where, dst.shape[1])]
                part = cmul(coef, z.astype(F32))
                total = part if total is None else total + part
            dst[r] = total.astype(dst.dtype)
        return 0

    lax.fori_loop(0, rows, one, 0, unroll=False)


def mix(idx, tab, srcs, outs, name):
    size = sum(int(np.prod(s.shape)) for s in srcs)
    return pl.pallas_call(
        functools.partial(mix_kernel, srcs, [plan for _, _, plan in outs]),
        out_shape=tuple(jax.ShapeDtypeStruct(shape, dtype) for shape, dtype, _ in outs),
        in_specs=[SMEM, VMEM] + [VMEM] * len(srcs),
        out_specs=tuple(VMEM for _ in outs),
        compiler_params=PARAMS,
        cost_estimate=pl.CostEstimate(flops=8 * size, bytes_accessed=2 * size, transcendentals=0),
        name=name,
    )(idx, tab, *srcs)


def carry_kernel(half, idx, tab, r1, r2, r3, feed, got, pay, own):
    a2, a3, b1, b2, b3 = (coefficient(tab, k) for k in range(6, 11))
    pc, pf, qc, qg = (coefficient(tab, k) for k in range(11, 15))
    mine = idx[0] * half

    def one(r, _):
        x1, x2, x3 = (ref[r].astype(F32) for ref in (r1, r2, r3))
        first = cmul(a2, x2) + cmul(a3, x3)
        second = cmul(b1, x1) + cmul(b2, x2) + cmul(b3, x3)
        carry = jnp.stack([first, second])
        f = feed[r, pl.ds(mine, half)]
        g = got[r].astype(F32)
        pay[r] = (cmul(pc, carry) + cmul(pf, f)).astype(BF16)
        own[r] = (cmul(qc, carry) + cmul(qg, g)).astype(BF16)
        return 0

    lax.fori_loop(0, r1.shape[0], one, 0)


def carry_mix(idx, tab, r1, r2, r3, feed, got):
    shape = got.shape
    return pl.pallas_call(
        functools.partial(carry_kernel, shape[1]),
        out_shape=(jax.ShapeDtypeStruct(shape, BF16), jax.ShapeDtypeStruct(shape, BF16)),
        in_specs=[SMEM] + [VMEM] * 6,
        out_specs=(VMEM, VMEM),
        compiler_params=PARAMS,
        cost_estimate=pl.CostEstimate(flops=40 * got.size, bytes_accessed=12 * got.size, transcendentals=0),
        name="carry",
    )(idx, tab, r1, r2, r3, feed, got)


def output_kernel(plan, step, *refs):
    keep_rows, strips, aliased = plan
    idx, tab, w_ref, feed, own, other, frames = refs[:7]
    refs = refs[7:]
    if aliased:
        kept, _, out = refs[:3]
        refs = refs[3:]
    else:
        out, kept_out = refs[:2]
        refs = refs[2:]
    prev, wide, block, sem = refs
    rows, quarters = prev.shape[0], prev.shape[1]
    half = quarters // 2
    w, c = frames.shape[1:]
    lam = coefficient(tab, 15)
    prev[:, pl.ds(idx[0] * half, half)] = own[...]
    prev[:, pl.ds((1 - idx[0]) * half, half)] = other[...]

    def state(i):
        z = cmul(lam, prev[i].astype(F32)) + feed[i]
        return z.reshape(w, c)

    at = 0
    jobs = []
    for sources, first, count in strips:
        base = at
        for kind, i in sources:
            if kind == "new":
                row = state(i)
                if not aliased and i in keep_rows:
                    kept_out[keep_rows.index(i)] = row.astype(BF16)
                wide[at] = widen(row)
            else:
                wide[at] = widen(kept[i].astype(F32))
            at += 1
        jobs += [(base + s, first + s, size) for s, size in blocks(count, step)]
    copies = []
    for j, (base, first, size) in enumerate(jobs):
        mixed = conv_block(wide, w_ref, base, size).reshape(size, w, c)
        act = 0.5 * mixed * (1.0 + lax.erf(mixed * np.float32(0.5**0.5)))
        lo = sum(s for _, _, s in jobs[:j])
        block[lo : lo + size] = (frames[first : first + size].astype(F32) + act).astype(BF16)
        copy = pltpu.make_async_copy(block.at[pl.ds(lo, size)], out.at[pl.ds(first, size)], sem.at[j])
        copy.start()
        copies.append(copy)
    for copy in copies:
        copy.wait()


def output(idx, tab, w_out, feed, own, other, frames, plan, step, previous=None, kept=None):
    keep_rows, strips, aliased = plan
    rows, quarters = feed.shape[:2]
    w, c = frames.shape[1:]
    n_wide = sum(len(s) for s, _, _ in strips)
    n_out = sum(n for _, _, n in strips)
    n_jobs = sum(len(blocks(n, step)) for _, _, n in strips)
    hbm = pl.BlockSpec(memory_space=pl.ANY)
    whole = jax.ShapeDtypeStruct(frames.shape, BF16)
    args = [idx, tab, w_out, feed, own, other, frames]
    specs = [SMEM] + [VMEM] * 6
    if aliased:
        args += [kept, previous]
        specs += [VMEM, hbm]
        out_shape, out_specs, alias = whole, hbm, {8: 0}
    else:
        out_shape = (whole, jax.ShapeDtypeStruct((len(keep_rows), w, c), BF16))
        out_specs, alias = (hbm, VMEM), {}
    return pl.pallas_call(
        functools.partial(output_kernel, plan, step),
        out_shape=out_shape,
        in_specs=specs,
        out_specs=out_specs,
        input_output_aliases=alias,
        scratch_shapes=[
            pltpu.VMEM((rows, quarters, w // quarters, c), BF16),
            pltpu.VMEM((n_wide, w, 3 * c), BF16),
            pltpu.VMEM((n_out, w, c), BF16),
            pltpu.SemaphoreType.DMA((n_jobs,)),
        ],
        compiler_params=PARAMS,
        cost_estimate=pl.CostEstimate(
            flops=2 * n_out * w * w_out.shape[0] * w_out.shape[1], bytes_accessed=n_out * w * c * 8, transcendentals=0
        ),
        name="output",
    )(*args)


def role_table(n):
    expo, gate = np.zeros((n, 16)), np.zeros((n, 16))

    def put(dev, k, e):
        expo[dev, k], gate[dev, k] = e, 1.0

    for dev in range(n):
        q, core = divmod(dev, 2)
        put(dev, 0, 1 - core)
        put(dev, 1, core)
        if n == 8:
            if q == 0:
                put(dev, 2, 2), put(dev, 3, 0), put(dev, 4, 0)
            if q == 1:
                put(dev, 2, 0), put(dev, 3, 2), put(dev, 7, 0), put(dev, 8, 0)
            if q == 2:
                put(dev, 4, 0), put(dev, 5, 2), put(dev, 6, 0), put(dev, 10, 0)
            if q == 3:
                put(dev, 5, 0), put(dev, 7, 0), put(dev, 8, 0), put(dev, 9, 2)
        else:
            put(dev, 7, 0), put(dev, 8, 0)
        put(dev, 11, 1 - core)
        if core == 0:
            put(dev, 12, 0)
        put(dev, 13, core)
        if core == 1:
            put(dev, 14, 0)
        put(dev, 15, 1)
    return expo.astype(np.float32), gate.astype(np.float32)


def powers(expo, gate, decay, phase):
    size = gate[:, None] * jnp.exp(-expo[:, None] * decay)
    angle = expo[:, None] * phase
    return jnp.stack([size * jnp.cos(angle), size * jnp.sin(angle)], axis=1).reshape(2 * expo.shape[0], -1)


def both_cores(pairs):
    return [(2 * a + k, 2 * b + k) for a, b in pairs for k in range(2)]


def on_device(n, n_space, frames_in, w_input, decay_rate, phase, w_output):
    frames = frames_in[0]
    rows, w, c = frames.shape
    quarters = 4
    me = lax.axis_index("tm")
    core = me % 2
    chip = me // 2
    expo, gate = role_table(n)
    tab = powers(jnp.asarray(expo)[me], jnp.asarray(gate)[me], decay_rate, phase)
    idx = jnp.stack([core, jnp.where(chip == 1, 0, 1), jnp.where(chip == 0, 0, 1)]).astype(jnp.int32)
    space = lax.axis_index("space")
    edge = jnp.stack([space > 0, space < n_space - 1]).astype(F32)
    decay = decay_rate[None]
    w_in = w_input.reshape(-1, w_input.shape[-1])
    w_out = w_output.reshape(-1, w_output.shape[-1])
    swap = [(i, i ^ 1) for i in range(n)]

    up = [(i, i + 1) for i in range(n_space - 1)]
    down = [(b, a) for a, b in up]
    above = lax.ppermute(frames[rows - 2 :], "space", up)
    below = lax.ppermute(frames[:2], "space", down)

    m = rows // 4
    inner = rows - 2 * m
    feeds, gots = [], []
    first = drive(
        [frames], [(m - 1, rows - m + 1)], [(0, inner, None)], inner, idx, edge, decay, w_in, quarters, 8
    )
    second = drive(
        [above, frames, frames, below],
        [(0, 2), (0, m + 1), (rows - m - 1, rows), (0, 2)],
        [(0, m + 1, (0, 0)), (m + 3, m + 1, (m, 1))],
        2 * (m + 1), idx, edge, decay, w_in, quarters, 9,
    )

    def exchange(feed, send):
        got = lax.ppermute(send, "tm", swap)
        n_rows, half = got.shape[:2]
        quarter = (n_rows, 1) + got.shape[2:]
        if n == 8:
            pair, pay = pair_sum(idx, tab, feed, got)
            r1 = lax.ppermute(pay, "tm", both_cores([(0, 1), (1, 0), (2, 3)]))
            (pay,) = mix(idx, tab, [pair, r1], [(quarter, BF16, [(2, 0, 2), (3, 1, "all")])], "second")
            r2 = lax.ppermute(pay, "tm", both_cores([(0, 2), (1, 3)]))
            (pay,) = mix(idx, tab, [pair, r2], [(quarter, BF16, [(4, 0, (0, 1)), (5, 1, "all")])], "third")
            r3 = lax.ppermute(pay, "tm", both_cores([(0, 1), (2, 3), (3, 2)]))
        else:
            pair, _ = pair_sum(idx, tab, feed, got)
            chips = n // 2
            stride = 1
            while stride < chips:
                moved = lax.ppermute(
                    pair.astype(BF16), "tm", both_cores([(i, i + stride) for i in range(chips - stride)])
                ).astype(F32)
                power = powers(jnp.asarray([2.0 * stride], F32), jnp.ones((1,), F32), decay_rate, phase)
                pair = pair + cmul((power[0], power[1]), moved)
                stride *= 2
            carry = lax.ppermute(pair.astype(BF16), "tm", both_cores([(i, i + 1) for i in range(chips - 1)]))
            r1, r3 = carry[:, 1:], carry[:, :1]
            r2 = jnp.zeros_like(r1)
        pay, own = carry_mix(idx, tab, r1[:, 0], r2[:, 0], r3[:, 0], feed, got)
        return own, lax.ppermute(pay, "tm", swap)

    own1, other1 = exchange(*first)
    own2, other2 = exchange(*second)
    top = [("new", i) for i in range(m + 1)] + [("kept", 0), ("kept", 1)]
    bottom = [("kept", 2), ("kept", 3)] + [("new", i) for i in range(m + 1, 2 * (m + 1))]
    keep = [0, 1, inner - 2, inner - 1]
    result, kept = output(
        idx, tab, w_out, first[0], own1, other1, frames,
        (keep, [([("new", i) for i in range(inner)], m + 1, inner - 2)], False), 7,
    )
    result = output(
        idx, tab, w_out, second[0], own2, other2, frames,
        (keep, [(top, 0, m + 1), (bottom, rows - m - 1, m + 1)], True), 9,
        previous=result, kept=kept,
    )
    return result[None]


def pair_kernel(half, idx, tab, feed, got, pair, pay):
    cm, cr = coefficient(tab, 0), coefficient(tab, 1)
    mine = idx[0] * half

    def one(r, _):
        pair[r] = cmul(cm, feed[r, pl.ds(mine, half)]) + cmul(cr, got[r].astype(F32))
        pay[r] = pair[r, pl.ds(idx[1], 1)].astype(BF16)
        return 0

    lax.fori_loop(0, got.shape[0], one, 0)


def pair_sum(idx, tab, feed, got):
    n_rows, half, w, c = got.shape
    return pl.pallas_call(
        functools.partial(pair_kernel, half),
        out_shape=(jax.ShapeDtypeStruct(got.shape, F32), jax.ShapeDtypeStruct((n_rows, 1, w, c), BF16)),
        in_specs=[SMEM, VMEM, VMEM, VMEM],
        out_specs=(VMEM, VMEM),
        compiler_params=PARAMS,
        cost_estimate=pl.CostEstimate(flops=16 * got.size, bytes_accessed=10 * got.size, transcendentals=0),
        name="pair",
    )(idx, tab, feed, got)


def solution(mesh):
    in_specs = (P("tm", "space", None, None), P(), P(), P(), P())
    out_specs = P("tm", "space", None, None)
    body = functools.partial(on_device, mesh.shape["tm"], mesh.shape["space"])
    return jax.shard_map(body, mesh=mesh, in_specs=in_specs, out_specs=out_specs, check_vma=False)
```

```python
import functools

import numpy as np
import jax
import jax.numpy as jnp
from jax import lax
from jax.experimental import pallas as pl
from jax.experimental.pallas import tpu as pltpu
from jax.sharding import PartitionSpec as P

F32 = jnp.float32
BF16 = jnp.bfloat16
VMEM = pl.BlockSpec(memory_space=pltpu.VMEM)
HBM = pl.BlockSpec(memory_space=pltpu.HBM)
PARAMS = pltpu.CompilerParams(vmem_limit_bytes=24 * 1024 * 1024)
SLOTS = 16


def cmul(coef, z):
    n = z.shape[-1] // 2
    re, im = z[..., :n], z[..., n:]
    cr, ci = coef
    return jnp.concatenate([cr * re - ci * im, cr * im + ci * re], axis=-1)


def coefficient(tab, i):
    return tab[i : i + 1, :], tab[SLOTS + i : SLOTS + i + 1, :]


def widen(row):
    w = row.shape[0]
    col = lax.broadcasted_iota(jnp.int32, row.shape, 0)
    left = jnp.where(col == 0, 0.0, pltpu.roll(row, 1, 0))
    right = jnp.where(col == w - 1, 0.0, pltpu.roll(row, w - 1, 0))
    return jnp.concatenate([left, row, right], axis=-1).astype(BF16)


def conv_block(wide, weights, start, count):
    w, k = wide.shape[1], wide.shape[2]
    lhs = jnp.concatenate(
        [wide[start + d : start + d + count].reshape(count * w, k) for d in range(3)], axis=-1
    )
    return jnp.dot(lhs, weights[...].reshape(3 * k, -1), preferred_element_type=F32)


def load_weights(core, hbm, vmem, sem):
    copies = []
    for d in range(3):
        source = jnp.where(core == 1, 2 - d, d)
        copies.append(pltpu.make_async_copy(hbm.at[source], vmem.at[d], sem.at[d]))
        copies[-1].start()
    return copies


def my_core():
    return lax.rem(lax.axis_index("tm"), 2)


def convolve(weights, wide, row_of, n, step, finish):
    ready = 0
    for s in range(0, n, step):
        size = min(step, n - s)
        while ready < s + size + 2:
            wide[ready] = widen(row_of(ready))
            ready += 1
        finish(s, size, conv_block(wide, weights, s, size))


def lead_kernel(entries, lo, hi, step, own, w_hbm, decay, phase, feed, frame, weights, tab, factor, wide, dvec, sem):
    core, chip = my_core(), lax.div(lax.axis_index("tm"), 2)
    rows = own.shape[0]
    n = hi - lo
    vectors = [pltpu.make_async_copy(ref, dvec.at[pl.ds(k, 1)], sem.at[3 + k]) for k, ref in enumerate((decay, phase))]
    for copy in vectors:
        copy.start()
    source = jnp.where(core == 1, rows - 1 - hi, lo - 1)
    near = pltpu.make_async_copy(own.at[pl.ds(source, n + 2)], frame.at[pl.ds(source, n + 2)], sem.at[5])
    near.start()
    wcopies = load_weights(core, w_hbm, weights, sem)
    rest = []
    for k, (begin, end) in enumerate(((0, lo - 1), (hi + 1, rows))):
        at = jnp.where(core == 1, rows - end, begin)
        rest.append(
            pltpu.make_async_copy(own.at[pl.ds(at, end - begin)], frame.at[pl.ds(at, end - begin)], sem.at[6 + k])
        )
        rest[-1].start()
    for copy in vectors:
        copy.wait()
    expo, gate = [jnp.float32(0.0)] * SLOTS, [jnp.float32(0.0)] * SLOTS
    for q, slot, power in entries:
        expo[slot] = jnp.where(chip == q, jnp.float32(power), expo[slot])
        gate[slot] = jnp.where(chip == q, jnp.float32(1.0), gate[slot])
    for slot, power in ((8, 1), (9, 1 - core), (10, core)):
        expo[slot], gate[slot] = jnp.asarray(power).astype(F32), jnp.float32(1.0)
    spread = lambda values: jnp.concatenate([jnp.full((1, dvec.shape[1]), v, F32) for v in values], axis=0)
    expo = spread(expo)
    size = spread(gate) * jnp.exp(-expo * dvec[0:1])
    angle = expo * dvec[1:2]
    tab[...] = jnp.concatenate([size * jnp.cos(angle), size * jnp.sin(angle)], axis=0)
    mag = jnp.exp(-dvec[0:1])
    scale = jnp.sqrt(1.0 - mag * mag)
    factor[...] = jnp.concatenate([scale, scale], axis=-1)
    near.wait()
    for copy in wcopies:
        copy.wait()

    def row_of(p):
        return frame[source + jnp.where(core == 1, n + 1 - p, p)].astype(F32)

    def finish(s, count, acc):
        feed[s : s + count] = (acc * factor[...]).reshape((count,) + feed.shape[1:])

    convolve(weights, wide, row_of, n, step, finish)
    for copy in rest:
        copy.wait()


def lead(entries, own, w_in, decay, phase, lo, hi, step):
    rows, w, c = own.shape
    n = hi - lo
    return pl.pallas_call(
        functools.partial(lead_kernel, entries, lo, hi, step),
        out_shape=[
            jax.ShapeDtypeStruct((n, w, c), F32),
            jax.ShapeDtypeStruct(own.shape, BF16),
            jax.ShapeDtypeStruct(w_in.shape, BF16),
            jax.ShapeDtypeStruct((2 * SLOTS, decay.shape[1]), F32),
            jax.ShapeDtypeStruct((1, 2 * decay.shape[1]), F32),
        ],
        in_specs=[HBM] * 4,
        out_specs=[VMEM] * 5,
        scratch_shapes=[
            pltpu.VMEM((n + 2, w, 3 * c), BF16),
            pltpu.VMEM((2, decay.shape[1]), F32),
            pltpu.SemaphoreType.DMA((8,)),
        ],
        compiler_params=PARAMS,
        cost_estimate=pl.CostEstimate(flops=18 * n * w * c * c, bytes_accessed=2 * own.size, transcendentals=0),
        name="lead",
    )(own, w_in, decay, phase)


def pair_kernel(lo, hi, step, frame, oth, weights, tab, factor, feed_own, feed, pay, border, wide):
    core = my_core()
    rows = frame.shape[0]
    n = hi - lo
    source = jnp.where(core == 1, rows - 1 - hi, lo - 1)
    for r in range(2):
        border[0, r] = frame[core * (rows - 2) + r]
        border[1, r] = oth[core * (rows - 2) + r]

    def row_of(p):
        return oth[source + jnp.where(core == 1, n + 1 - p, p)].astype(F32)

    def finish(s, count, acc):
        value = (acc * factor[...]).reshape((count,) + feed.shape[1:])
        feed[s : s + count] = value
        for r in range(count):
            pair = cmul(coefficient(tab, 9), feed_own[s + r]) + cmul(coefficient(tab, 10), value[r])
            pay[s + r] = pair.astype(BF16)

    convolve(weights, wide, row_of, n, step, finish)


def pair_up(frame, oth, weights, tab, factor, feed_own, lo, hi, step):
    rows, w, c = frame.shape
    n = hi - lo
    return pl.pallas_call(
        functools.partial(pair_kernel, lo, hi, step),
        out_shape=[
            jax.ShapeDtypeStruct((n, w, c), F32),
            jax.ShapeDtypeStruct((n, w, c), BF16),
            jax.ShapeDtypeStruct((2, 2, w, c), BF16),
        ],
        in_specs=[VMEM] * 6,
        out_specs=[VMEM] * 3,
        scratch_shapes=[pltpu.VMEM((n + 2, w, 3 * c), BF16)],
        compiler_params=PARAMS,
        cost_estimate=pl.CostEstimate(flops=18 * n * w * c * c, bytes_accessed=2 * oth.size, transcendentals=0),
        name="pair",
    )(frame, oth, weights, tab, factor, feed_own)


def drive_kernel(lo, hi, step, edge, last, *refs):
    refs = list(refs)
    take = lambda k: [refs.pop(0) for _ in range(k)]
    frame, oth, weights, tab, factor = take(5)
    if edge:
        (halo,) = take(1)
    if last:
        (w_hbm,) = take(1)
    feed_own, feed_oth, pay = take(3)
    if last:
        (w_next,) = take(1)
    (wide,) = take(1)
    core = my_core()
    rows = frame.shape[0]
    n = hi - lo
    copies = load_weights(core, w_hbm, w_next, take(1)[0]) if last else []
    if edge:
        space = lax.axis_index("space")
        outer = jnp.where(core == 1, lax.axis_size("space") - 1, 0)
        inside = jnp.where(space == outer, 0.0, 1.0)
    for f, (ref, feed) in enumerate(((frame, feed_own), (oth, feed_oth))):

        def row_of(p):
            depth = lo - 1 + p
            if depth < 0:
                return halo[1 - f, jnp.where(core == 1, -1 - depth, 2 + depth)].astype(F32)
            return ref[jnp.where(core == 1, rows - 1 - depth, depth)].astype(F32)

        def finish(s, count, acc):
            value = (acc * factor[...]).reshape((count,) + feed.shape[1:])
            for r in range(count):
                row = value[r]
                if edge and s + r == 0:
                    row = row * inside
                feed[s + r] = row
                if f == 1:
                    pair = cmul(coefficient(tab, 9), feed_own[s + r]) + cmul(coefficient(tab, 10), row)
                    pay[s + r] = pair.astype(BF16)

        convolve(weights, wide.at[f], row_of, n, step, finish)
    for copy in copies:
        copy.wait()


def drive(frame, oth, weights, tab, factor, lo, hi, step, halo=None, w_out=None):
    rows, w, c = frame.shape
    n = hi - lo
    edge, last = halo is not None, w_out is not None
    args, specs = [frame, oth, weights, tab, factor], [VMEM] * 5
    if edge:
        args, specs = args + [halo], specs + [VMEM]
    if last:
        args, specs = args + [w_out], specs + [HBM]
    shapes = [jax.ShapeDtypeStruct((n, w, c), F32)] * 2 + [jax.ShapeDtypeStruct((n, w, c), BF16)]
    scratch = [pltpu.VMEM((2, n + 2, w, 3 * c), BF16)]
    if last:
        shapes += [jax.ShapeDtypeStruct(w_out.shape, BF16)]
        scratch += [pltpu.SemaphoreType.DMA((3,))]
    return pl.pallas_call(
        functools.partial(drive_kernel, lo, hi, step, edge, last),
        out_shape=shapes,
        in_specs=specs,
        out_specs=[VMEM] * len(shapes),
        scratch_shapes=scratch,
        compiler_params=PARAMS,
        cost_estimate=pl.CostEstimate(flops=36 * n * w * c * c, bytes_accessed=20 * n * w * c, transcendentals=0),
        name="drive",
    )(*args)


def relay_kernel(slot, tab, pair, got, pay):
    cp, cr = coefficient(tab, slot), coefficient(tab, slot + 1)
    for r in range(pair.shape[0]):
        pay[r] = (cmul(cp, pair[r].astype(F32)) + cmul(cr, got[r].astype(F32))).astype(BF16)


def relay(slot, tab, pair, got):
    return pl.pallas_call(
        functools.partial(relay_kernel, slot),
        out_shape=jax.ShapeDtypeStruct(pair.shape, BF16),
        in_specs=[VMEM] * 3,
        out_specs=VMEM,
        compiler_params=PARAMS,
        cost_estimate=pl.CostEstimate(flops=16 * pair.size, bytes_accessed=6 * pair.size, transcendentals=0),
        name="relay",
    )(tab, pair, got)


def output_kernel(lo, hi, begin, end, slot, step, keep, *refs):
    refs = list(refs)
    take = lambda k: [refs.pop(0) for _ in range(k)]
    tab, weights, feed_own, feed_oth, r1, r2, own, oth = take(8)
    kept = None
    if hi < end + 1:
        kept, _ = take(2)
    out, pay = take(2)
    if keep:
        (kept_out,) = take(1)
    wide, block, sem = take(3)
    core = my_core()
    first_core = core == 0
    n, n_out = hi - lo, end - begin
    w, c = own.shape[1:]
    rows = own.shape[0]
    lam = coefficient(tab, 8)
    e1, e2 = coefficient(tab, slot + 2), coefficient(tab, slot + 3)

    def states(r):
        f_own, f_oth = feed_own[r], feed_oth[r]
        carry = cmul(e1, r1[r].astype(F32)) + cmul(e2, r2[r].astype(F32))
        s0 = cmul(lam, carry) + jnp.where(first_core, f_own, f_oth)
        s1 = cmul(lam, s0) + jnp.where(first_core, f_oth, f_own)
        return jnp.where(first_core, s1, s0), jnp.where(first_core, s0, s1)

    ready = 0
    copies = []
    for s in range(0, n_out, step):
        size = min(step, n_out - s)
        while ready < s + size + 2:
            if ready < n:
                pair = states(ready)
                if keep and ready < 2:
                    for f in range(2):
                        kept_out[f, ready] = pair[f].astype(BF16)
            else:
                pair = [kept[f, ready - n].astype(F32) for f in range(2)]
            for f in range(2):
                wide[f, ready] = widen(pair[f])
            ready += 1
        for f, (frame, dst) in enumerate(((oth, pay), (own, block))):
            mixed = conv_block(wide.at[f], weights, s, size).reshape(size, w, c)
            act = 0.5 * mixed * (1.0 + lax.erf(mixed * np.float32(0.5**0.5)))
            for r in range(s, s + size):
                depth = begin + r
                at = jnp.where(core == 1, rows - 1 - depth, depth)
                dst[r] = (frame[at].astype(F32) + act[r - s]).astype(BF16)
                if f == 1:
                    copies.append(pltpu.make_async_copy(block.at[r], out.at[at], sem.at[r]))
                    copies[-1].start()
    for copy in copies:
        copy.wait()


def output(tab, weights, feeds, arrived, own, oth, lo, hi, begin, end, slot, step, keep, kept=None, result=None):
    rows, w, c = own.shape
    n, n_out = hi - lo, end - begin
    args = [tab, weights, *feeds, *arrived, own, oth]
    specs = [VMEM] * len(args)
    alias = {}
    if kept is not None:
        args += [kept, result]
        specs += [VMEM, HBM]
        alias = {len(args) - 1: 0}
    shapes = [jax.ShapeDtypeStruct(own.shape, BF16), jax.ShapeDtypeStruct((n_out, w, c), BF16)]
    out_specs = [HBM, VMEM]
    if keep:
        shapes.append(jax.ShapeDtypeStruct((2, 2, w, c), BF16))
        out_specs.append(VMEM)
    return pl.pallas_call(
        functools.partial(output_kernel, lo, hi, begin, end, slot, step, keep),
        out_shape=shapes,
        in_specs=specs,
        out_specs=out_specs,
        input_output_aliases=alias,
        scratch_shapes=[
            pltpu.VMEM((2, n_out + 2, w, 3 * c), BF16),
            pltpu.VMEM((n_out, w, c), BF16),
            pltpu.SemaphoreType.DMA((n_out,)),
        ],
        compiler_params=PARAMS,
        cost_estimate=pl.CostEstimate(flops=36 * n_out * w * c * c, bytes_accessed=20 * n * w * c, transcendentals=0),
        name="output",
    )(*args)


def place_kernel(spans, *refs):
    parts, out, sem = refs[: len(spans)], refs[-2], refs[-1]
    core = my_core()
    rows = out.shape[0]
    copies = []
    for part, (begin, end) in zip(parts, spans):
        for r in range(end - begin):
            at = jnp.where(core == 1, begin + r, rows - 1 - begin - r)
            copies.append(pltpu.make_async_copy(part.at[r], out.at[at], sem.at[len(copies)]))
            copies[-1].start()
    for copy in copies:
        copy.wait()


def place(parts, spans, result):
    return pl.pallas_call(
        functools.partial(place_kernel, spans),
        out_shape=jax.ShapeDtypeStruct(result.shape, result.dtype),
        in_specs=[VMEM] * len(parts) + [HBM],
        out_specs=HBM,
        input_output_aliases={len(parts): 0},
        scratch_shapes=[pltpu.SemaphoreType.DMA((sum(end - begin for begin, end in spans),))],
        compiler_params=PARAMS,
        name="place",
    )(*parts, result)


ALONG_X = [(0, 1), (1, 0), (2, 3)], [(0, 2), (1, 3)]
ALONG_Y = [(0, 2), (1, 3)], [(0, 1), (2, 3), (3, 2)]


def roles(n):
    if n != 8:
        return [(q, slot, 0) for q in range(n // 2) for slot in (2, 6)]
    along_x = [(0, 0, 2), (0, 1, 0), (1, 0, 0), (1, 1, 2), (1, 2, 0), (2, 3, 0), (3, 2, 0), (3, 3, 2)]
    along_y = [(0, 4, 0), (2, 4, 0), (2, 5, 4), (3, 5, 0), (1, 7, 0), (2, 6, 2), (2, 7, 0), (3, 6, 2), (3, 7, 0)]
    return along_x + along_y


def both_cores(pairs):
    return [(2 * a + k, 2 * b + k) for a, b in pairs for k in range(2)]


def exchange(n, slot, tab, pair, decay, phase):
    if n == 8:
        one, two = ALONG_X if slot == 0 else ALONG_Y
        r1 = lax.ppermute(pair, "tm", both_cores(one))
        r2 = lax.ppermute(relay(slot, tab, pair, r1), "tm", both_cores(two))
        return r1, r2
    chips, stride, total = n // 2, 1, pair.astype(F32)
    while stride < chips:
        steps = both_cores([(i, i + stride) for i in range(chips - stride)])
        moved = lax.ppermute(total.astype(BF16), "tm", steps).astype(F32)
        size, angle = jnp.exp(-2.0 * stride * decay), 2.0 * stride * phase
        total = total + cmul((size * jnp.cos(angle), size * jnp.sin(angle)), moved)
        stride *= 2
    carry = lax.ppermute(total.astype(BF16), "tm", both_cores([(i, i + 1) for i in range(chips - 1)]))
    return carry, jnp.zeros_like(carry)


def on_device(n, n_space, frames_in, w_input, decay_rate, phase, w_output):
    own = frames_in[0]
    rows, w, c = own.shape
    decay, phase = decay_rate[None], phase[None]
    w_in = w_input.reshape(3, 3 * c, -1)
    w_out = w_output.reshape(3, -1, c)
    swap = [(i, i ^ 1) for i in range(n)]
    step = 3
    oth = lax.ppermute(own, "tm", swap)

    half = rows // 2
    cut = half // 2
    own1, frame, weights, tab, factor = lead(roles(n), own, w_in, decay, phase, cut, half + 1, step)
    oth1, pair1, border = pair_up(frame, oth, weights, tab, factor, own1, cut, half + 1, step)
    links = [
        ((t ^ 1) * n_space + s, t * n_space + s + 1) if t % 2 == 0 else ((t ^ 1) * n_space + s + 1, t * n_space + s)
        for t in range(n)
        for s in range(n_space - 1)
    ]
    halo = lax.ppermute(border, ("tm", "space"), links)
    arrived1 = exchange(n, 0, tab, pair1, decay, phase)
    own2, oth2, pair2, weights = drive(frame, oth, weights, tab, factor, -1, cut, step, halo=halo, w_out=w_out)
    arrived2 = exchange(n, 4, tab, pair2, decay, phase)
    result, pay1, kept = output(
        tab, weights, (own1, oth1), arrived1, frame, oth, cut, half + 1, cut + 1, half, 0, step, True
    )
    got1 = lax.ppermute(pay1, "tm", swap)
    result, pay2 = output(
        tab, weights, (own2, oth2), arrived2, frame, oth, -1, cut, 0, cut + 1, 4, step, False, kept=kept, result=result
    )
    got2 = lax.ppermute(pay2, "tm", swap)
    return place([got1, got2], [(cut + 1, half), (0, cut + 1)], result)[None]


def solution(mesh):
    in_specs = (P("tm", "space", None, None), P(), P(), P(), P())
    out_specs = P("tm", "space", None, None)
    body = functools.partial(on_device, mesh.shape["tm"], mesh.shape["space"])
    return jax.shard_map(body, mesh=mesh, in_specs=in_specs, out_specs=out_specs, check_vma=False)
```

```python
import functools

import numpy as np
import jax
import jax.numpy as jnp
from jax import lax
from jax.experimental import pallas as pl
from jax.experimental.pallas import tpu as pltpu
from jax.sharding import PartitionSpec as P

F32 = jnp.float32
BF16 = jnp.bfloat16
VMEM = pl.BlockSpec(memory_space=pltpu.VMEM)
HBM = pl.BlockSpec(memory_space=pltpu.HBM)
PARAMS = pltpu.CompilerParams(vmem_limit_bytes=24 * 1024 * 1024)
SLOTS = 16


def cmul(coef, z):
    n = z.shape[-1] // 2
    re, im = z[..., :n], z[..., n:]
    cr, ci = coef
    return jnp.concatenate([cr * re - ci * im, cr * im + ci * re], axis=-1)


def coefficient(tab, i):
    return tab[i : i + 1, :], tab[SLOTS + i : SLOTS + i + 1, :]


def widen(row):
    w = row.shape[0]
    col = lax.broadcasted_iota(jnp.int32, row.shape, 0)
    left = jnp.where(col == 0, 0.0, pltpu.roll(row, 1, 0))
    right = jnp.where(col == w - 1, 0.0, pltpu.roll(row, w - 1, 0))
    return jnp.concatenate([left, row, right], axis=-1).astype(BF16)


def conv_block(wide, weights, start, count):
    w, k = wide.shape[1], wide.shape[2]
    lhs = jnp.concatenate(
        [wide[start + d : start + d + count].reshape(count * w, k) for d in range(3)], axis=-1
    )
    return jnp.dot(lhs, weights[...].reshape(3 * k, -1), preferred_element_type=F32)


def load_weights(core, hbm, vmem, sem):
    copies = []
    for d in range(3):
        source = jnp.where(core == 1, 2 - d, d)
        copies.append(pltpu.make_async_copy(hbm.at[source], vmem.at[d], sem.at[d]))
        copies[-1].start()
    return copies


def my_core():
    return lax.rem(lax.axis_index("tm"), 2)


def convolve(weights, wide, row_of, n, step, finish):
    ready = 0
    for s in range(0, n, step):
        size = min(step, n - s)
        while ready < s + size + 2:
            wide[ready] = widen(row_of(ready))
            ready += 1
        finish(s, size, conv_block(wide, weights, s, size))


def lead_kernel(entries, lo, hi, step, own, w_hbm, decay, phase, feed, frame, weights, tab, factor, wide, dvec, sem):
    core, chip = my_core(), lax.div(lax.axis_index("tm"), 2)
    rows = own.shape[0]
    n = hi - lo
    vectors = [pltpu.make_async_copy(ref, dvec.at[pl.ds(k, 1)], sem.at[3 + k]) for k, ref in enumerate((decay, phase))]
    for copy in vectors:
        copy.start()
    source = jnp.where(core == 1, rows - 1 - hi, lo - 1)
    near = pltpu.make_async_copy(own.at[pl.ds(source, n + 2)], frame.at[pl.ds(source, n + 2)], sem.at[5])
    near.start()
    wcopies = load_weights(core, w_hbm, weights, sem)
    rest = []
    for k, (begin, end) in enumerate(((0, lo - 1), (hi + 1, rows))):
        at = jnp.where(core == 1, rows - end, begin)
        rest.append(
            pltpu.make_async_copy(own.at[pl.ds(at, end - begin)], frame.at[pl.ds(at, end - begin)], sem.at[6 + k])
        )
        rest[-1].start()
    for copy in vectors:
        copy.wait()
    expo, gate = [jnp.float32(0.0)] * SLOTS, [jnp.float32(0.0)] * SLOTS
    for q, slot, power in entries:
        expo[slot] = jnp.where(chip == q, jnp.float32(power), expo[slot])
        gate[slot] = jnp.where(chip == q, jnp.float32(1.0), gate[slot])
    for slot, power in ((8, 1), (9, 1 - core), (10, core)):
        expo[slot], gate[slot] = jnp.asarray(power).astype(F32), jnp.float32(1.0)
    spread = lambda values: jnp.concatenate([jnp.full((1, dvec.shape[1]), v, F32) for v in values], axis=0)
    expo = spread(expo)
    size = spread(gate) * jnp.exp(-expo * dvec[0:1])
    angle = expo * dvec[1:2]
    tab[...] = jnp.concatenate([size * jnp.cos(angle), size * jnp.sin(angle)], axis=0)
    mag = jnp.exp(-dvec[0:1])
    scale = jnp.sqrt(1.0 - mag * mag)
    factor[...] = jnp.concatenate([scale, scale], axis=-1)
    near.wait()
    for copy in wcopies:
        copy.wait()

    def row_of(p):
        return frame[source + jnp.where(core == 1, n + 1 - p, p)].astype(F32)

    def finish(s, count, acc):
        feed[s : s + count] = (acc * factor[...]).reshape((count,) + feed.shape[1:])

    convolve(weights, wide, row_of, n, step, finish)
    for copy in rest:
        copy.wait()


def lead(entries, own, w_in, decay, phase, lo, hi, step):
    rows, w, c = own.shape
    n = hi - lo
    return pl.pallas_call(
        functools.partial(lead_kernel, entries, lo, hi, step),
        out_shape=[
            jax.ShapeDtypeStruct((n, w, c), F32),
            jax.ShapeDtypeStruct(own.shape, BF16),
            jax.ShapeDtypeStruct(w_in.shape, BF16),
            jax.ShapeDtypeStruct((2 * SLOTS, decay.shape[1]), F32),
            jax.ShapeDtypeStruct((1, 2 * decay.shape[1]), F32),
        ],
        in_specs=[HBM] * 4,
        out_specs=[VMEM] * 5,
        scratch_shapes=[
            pltpu.VMEM((n + 2, w, 3 * c), BF16),
            pltpu.VMEM((2, decay.shape[1]), F32),
            pltpu.SemaphoreType.DMA((8,)),
        ],
        compiler_params=PARAMS,
        cost_estimate=pl.CostEstimate(flops=18 * n * w * c * c, bytes_accessed=2 * own.size, transcendentals=0),
        name="lead",
    )(*(pltpu.with_memory_space_constraint(x, pltpu.HBM) for x in (own, w_in, decay, phase)))


def pair_kernel(lo, hi, step, frame, oth, weights, tab, factor, feed_own, feed, pay, wide):
    core = my_core()
    rows = frame.shape[0]
    n = hi - lo
    source = jnp.where(core == 1, rows - 1 - hi, lo - 1)

    def row_of(p):
        return oth[source + jnp.where(core == 1, n + 1 - p, p)].astype(F32)

    def finish(s, count, acc):
        value = (acc * factor[...]).reshape((count,) + feed.shape[1:])
        feed[s : s + count] = value
        for r in range(count):
            pair = cmul(coefficient(tab, 9), feed_own[s + r]) + cmul(coefficient(tab, 10), value[r])
            pay[s + r] = pair.astype(BF16)

    convolve(weights, wide, row_of, n, step, finish)


def pair_up(frame, oth, weights, tab, factor, feed_own, lo, hi, step):
    rows, w, c = frame.shape
    n = hi - lo
    return pl.pallas_call(
        functools.partial(pair_kernel, lo, hi, step),
        out_shape=[
            jax.ShapeDtypeStruct((n, w, c), F32),
            jax.ShapeDtypeStruct((n, w, c), BF16),
        ],
        in_specs=[VMEM] * 6,
        out_specs=[VMEM] * 2,
        scratch_shapes=[pltpu.VMEM((n + 2, w, 3 * c), BF16)],
        compiler_params=PARAMS,
        cost_estimate=pl.CostEstimate(flops=18 * n * w * c * c, bytes_accessed=2 * oth.size, transcendentals=0),
        name="pair",
    )(frame, oth, weights, tab, factor, feed_own)


def drive_kernel(lo, hi, step, edge, second, *refs):
    refs = list(refs)
    take = lambda k: [refs.pop(0) for _ in range(k)]
    frame, oth, weights, tab, factor = take(5)
    if edge:
        (halo,) = take(1)
    if second:
        (w_hbm,) = take(1)
    feed_own, feed_oth, pay = take(3)
    if second:
        w_next, border = take(2)
    (wide,) = take(1)
    core = my_core()
    rows = frame.shape[0]
    n = hi - lo
    copies = []
    if second:
        copies = load_weights(core, w_hbm, w_next, take(1)[0])
        for f, ref in enumerate((frame, oth)):
            for r in range(2):
                border[f, r] = ref[core * (rows - 2) + r]
    if edge:
        space = lax.axis_index("space")
        outer = jnp.where(core == 1, lax.axis_size("space") - 1, 0)
        inside = jnp.where(space == outer, 0.0, 1.0)
    for f, (ref, feed) in enumerate(((frame, feed_own), (oth, feed_oth))):

        def row_of(p):
            depth = lo - 1 + p
            if depth < 0:
                return halo[1 - f, jnp.where(core == 1, -1 - depth, 2 + depth)].astype(F32)
            return ref[jnp.where(core == 1, rows - 1 - depth, depth)].astype(F32)

        def finish(s, count, acc):
            value = (acc * factor[...]).reshape((count,) + feed.shape[1:])
            for r in range(count):
                row = value[r]
                if edge and s + r == 0:
                    row = row * inside
                feed[s + r] = row
                if f == 1:
                    pair = cmul(coefficient(tab, 9), feed_own[s + r]) + cmul(coefficient(tab, 10), row)
                    pay[s + r] = pair.astype(BF16)

        convolve(weights, wide.at[f], row_of, n, step, finish)
    for copy in copies:
        copy.wait()


def drive(frame, oth, weights, tab, factor, lo, hi, step, halo=None, w_out=None):
    rows, w, c = frame.shape
    n = hi - lo
    edge, second = halo is not None, w_out is not None
    args, specs = [frame, oth, weights, tab, factor], [VMEM] * 5
    if edge:
        args, specs = args + [halo], specs + [VMEM]
    if second:
        args, specs = args + [w_out], specs + [HBM]
    shapes = [jax.ShapeDtypeStruct((n, w, c), F32)] * 2 + [jax.ShapeDtypeStruct((n, w, c), BF16)]
    scratch = [pltpu.VMEM((2, n + 2, w, 3 * c), BF16)]
    if second:
        shapes += [jax.ShapeDtypeStruct(w_out.shape, BF16), jax.ShapeDtypeStruct((2, 2, w, c), BF16)]
        scratch += [pltpu.SemaphoreType.DMA((3,))]
    return pl.pallas_call(
        functools.partial(drive_kernel, lo, hi, step, edge, second),
        out_shape=shapes,
        in_specs=specs,
        out_specs=[VMEM] * len(shapes),
        scratch_shapes=scratch,
        compiler_params=PARAMS,
        cost_estimate=pl.CostEstimate(flops=36 * n * w * c * c, bytes_accessed=20 * n * w * c, transcendentals=0),
        name="drive",
    )(*args)


def relay_kernel(slot, tab, pair, got, pay):
    cp, cr = coefficient(tab, slot), coefficient(tab, slot + 1)
    for r in range(pair.shape[0]):
        pay[r] = (cmul(cp, pair[r].astype(F32)) + cmul(cr, got[r].astype(F32))).astype(BF16)


def relay(slot, tab, pair, got):
    return pl.pallas_call(
        functools.partial(relay_kernel, slot),
        out_shape=jax.ShapeDtypeStruct(pair.shape, BF16),
        in_specs=[VMEM] * 3,
        out_specs=VMEM,
        compiler_params=PARAMS,
        cost_estimate=pl.CostEstimate(flops=16 * pair.size, bytes_accessed=6 * pair.size, transcendentals=0),
        name="relay",
    )(tab, pair, got)


def output_kernel(lo, hi, begin, end, slot, step, keep, which, *refs):
    refs = list(refs)
    take = lambda k: [refs.pop(0) for _ in range(k)]
    tab, weights, feed_own, feed_oth, r1, r2, own, oth = take(8)
    kept = out = pay = block = None
    if hi < end + 1:
        (kept,) = take(1)
        if 1 in which:
            take(1)
    if 1 in which:
        (out,) = take(1)
    if 0 in which:
        (pay,) = take(1)
    if keep:
        (kept_out,) = take(1)
    (wide,) = take(1)
    if 1 in which:
        block, sem = take(2)
    core = my_core()
    first_core = core == 0
    n, n_out = hi - lo, end - begin
    w, c = own.shape[1:]
    rows = own.shape[0]
    lam = coefficient(tab, 8)
    e1, e2 = coefficient(tab, slot + 2), coefficient(tab, slot + 3)

    def states(r):
        f_own, f_oth = feed_own[r], feed_oth[r]
        carry = cmul(e1, r1[r].astype(F32)) + cmul(e2, r2[r].astype(F32))
        s0 = cmul(lam, carry) + jnp.where(first_core, f_own, f_oth)
        s1 = cmul(lam, s0) + jnp.where(first_core, f_oth, f_own)
        return jnp.where(first_core, s1, s0), jnp.where(first_core, s0, s1)

    ready = 0
    copies = []
    for s in range(0, n_out, step):
        size = min(step, n_out - s)
        while ready < s + size + 2:
            if ready < n:
                pair = states(ready)
                if keep and ready < 2:
                    for f in range(2):
                        kept_out[f, ready] = pair[f].astype(BF16)
            else:
                pair = [kept[f, ready - n].astype(F32) for f in range(2)]
            for f in which:
                wide[f, ready] = widen(pair[f])
            ready += 1
        for f in which:
            frame, dst = ((oth, pay), (own, block))[f]
            mixed = conv_block(wide.at[f], weights, s, size).reshape(size, w, c)
            act = 0.5 * mixed * (1.0 + lax.erf(mixed * np.float32(0.5**0.5)))
            for r in range(s, s + size):
                depth = begin + r
                at = jnp.where(core == 1, rows - 1 - depth, depth)
                dst[r] = (frame[at].astype(F32) + act[r - s]).astype(BF16)
                if f == 1:
                    copies.append(pltpu.make_async_copy(block.at[r], out.at[at], sem.at[r]))
                    copies[-1].start()
    for copy in copies:
        copy.wait()


def output(tab, weights, feeds, arrived, own, oth, lo, hi, begin, end, slot, step, keep, which=(0, 1), kept=None, result=None):
    rows, w, c = own.shape
    n, n_out = hi - lo, end - begin
    args = [tab, weights, *feeds, *arrived, own, oth]
    specs = [VMEM] * len(args)
    alias = {}
    if kept is not None:
        args += [kept]
        specs += [VMEM]
        if 1 in which:
            args += [result]
            specs += [HBM]
            alias = {len(args) - 1: 0}
    shapes, out_specs = [], []
    scratch = [pltpu.VMEM((2, n_out + 2, w, 3 * c), BF16)]
    if 1 in which:
        shapes += [jax.ShapeDtypeStruct(own.shape, BF16)]
        out_specs += [HBM]
        scratch += [pltpu.VMEM((n_out, w, c), BF16), pltpu.SemaphoreType.DMA((n_out,))]
    if 0 in which:
        shapes += [jax.ShapeDtypeStruct((n_out, w, c), BF16)]
        out_specs += [VMEM]
    if keep:
        shapes.append(jax.ShapeDtypeStruct((2, 2, w, c), BF16))
        out_specs.append(VMEM)
    return pl.pallas_call(
        functools.partial(output_kernel, lo, hi, begin, end, slot, step, keep, which),
        out_shape=shapes,
        in_specs=specs,
        out_specs=out_specs,
        input_output_aliases=alias,
        scratch_shapes=scratch,
        compiler_params=PARAMS,
        cost_estimate=pl.CostEstimate(
            flops=18 * len(which) * n_out * w * c * c, bytes_accessed=20 * n * w * c, transcendentals=0
        ),
        name="output",
    )(*args)


def place_kernel(spans, *refs):
    parts, out, sem = refs[: len(spans)], refs[-2], refs[-1]
    core = my_core()
    rows = out.shape[0]
    copies = []
    for part, (begin, end) in zip(parts, spans):
        for r in range(end - begin):
            at = jnp.where(core == 1, begin + r, rows - 1 - begin - r)
            copies.append(pltpu.make_async_copy(part.at[r], out.at[at], sem.at[len(copies)]))
            copies[-1].start()
    for copy in copies:
        copy.wait()


def place(parts, spans, result):
    return pl.pallas_call(
        functools.partial(place_kernel, spans),
        out_shape=jax.ShapeDtypeStruct(result.shape, result.dtype),
        in_specs=[VMEM] * len(parts) + [HBM],
        out_specs=HBM,
        input_output_aliases={len(parts): 0},
        scratch_shapes=[pltpu.SemaphoreType.DMA((sum(end - begin for begin, end in spans),))],
        compiler_params=PARAMS,
        name="place",
    )(*parts, result)


ALONG_X = [(0, 1), (1, 0), (2, 3)], [(0, 2), (1, 3)]
ALONG_Y = [(0, 2), (1, 3)], [(0, 1), (2, 3), (3, 2)]


def roles(n):
    if n != 8:
        return [(q, slot, 0) for q in range(n // 2) for slot in (2, 6)]
    along_x = [(0, 0, 2), (0, 1, 0), (1, 0, 0), (1, 1, 2), (1, 2, 0), (2, 3, 0), (3, 2, 0), (3, 3, 2)]
    along_y = [(0, 4, 0), (2, 4, 0), (2, 5, 4), (3, 5, 0), (1, 7, 0), (2, 6, 2), (2, 7, 0), (3, 6, 2), (3, 7, 0)]
    return along_x + along_y


def both_cores(pairs):
    return [(2 * a + k, 2 * b + k) for a, b in pairs for k in range(2)]


def exchange(n, slot, tab, pair, decay, phase):
    if n == 8:
        one, two = ALONG_X if slot == 0 else ALONG_Y
        r1 = lax.ppermute(pair, "tm", both_cores(one))
        r2 = lax.ppermute(relay(slot, tab, pair, r1), "tm", both_cores(two))
        return r1, r2
    chips, stride, total = n // 2, 1, pair.astype(F32)
    while stride < chips:
        steps = both_cores([(i, i + stride) for i in range(chips - stride)])
        moved = lax.ppermute(total.astype(BF16), "tm", steps).astype(F32)
        size, angle = jnp.exp(-2.0 * stride * decay), 2.0 * stride * phase
        total = total + cmul((size * jnp.cos(angle), size * jnp.sin(angle)), moved)
        stride *= 2
    carry = lax.ppermute(total.astype(BF16), "tm", both_cores([(i, i + 1) for i in range(chips - 1)]))
    return carry, jnp.zeros_like(carry)


def on_device(n, n_space, frames_in, w_input, decay_rate, phase, w_output):
    own = frames_in[0]
    rows, w, c = own.shape
    decay, phase = decay_rate[None], phase[None]
    w_in = w_input.reshape(3, 3 * c, -1)
    w_out = w_output.reshape(3, -1, c)
    swap = [(i, i ^ 1) for i in range(n)]
    step = 3
    oth = lax.ppermute(own, "tm", swap)

    half = rows // 2
    total, parts = half + 2, 3
    sizes = [total // parts + (k < total % parts) for k in range(parts)]
    bounds = [half + 1 - sum(sizes[:k]) for k in range(parts + 1)]
    spans = [(bounds[k + 1], bounds[k]) for k in range(parts)]
    links = [
        ((t ^ 1) * n_space + s, t * n_space + s + 1) if t % 2 == 0 else ((t ^ 1) * n_space + s + 1, t * n_space + s)
        for t in range(n)
        for s in range(n_space - 1)
    ]
    feeds, arrived = [], []
    for k, (lo, hi) in enumerate(spans):
        if k == 0:
            mine, frame, weights, tab, factor = lead(roles(n), own, w_in, decay, phase, lo, hi, step)
            theirs, pair = pair_up(frame, oth, weights, tab, factor, mine, lo, hi, step)
        elif k == 1:
            mine, theirs, pair, weights_out, border = drive(
                frame, oth, weights, tab, factor, lo, hi, step, w_out=w_out
            )
            halo = lax.ppermute(border, ("tm", "space"), links)
        else:
            mine, theirs, pair = drive(frame, oth, weights, tab, factor, lo, hi, step, halo=halo)
        feeds.append((mine, theirs))
        arrived.append(exchange(n, 4 * (k % 2), tab, pair, decay, phase))
    got, outs, result, kept = [], [], None, None
    for k, (lo, hi) in enumerate(spans):
        begin, end = lo + 1, min(hi + 1, half)
        args = (tab, weights_out, feeds[k], arrived[k], frame, oth, lo, hi, begin, end, 4 * (k % 2), step)
        if k < parts - 1:
            result, pay, kept_next = output(*args, True, kept=kept, result=result)
        else:
            (pay,) = output(*args, False, which=(0,), kept=kept)
            (result,) = output(*args, False, which=(1,), kept=kept, result=result)
        kept = kept_next
        got.append(lax.ppermute(pay, "tm", swap))
        outs.append((begin, end))
    return place(got, outs, result)[None]


def solution(mesh):
    in_specs = (P("tm", "space", None, None), P(), P(), P(), P())
    out_specs = P("tm", "space", None, None)
    body = functools.partial(on_device, mesh.shape["tm"], mesh.shape["space"])
    return jax.shard_map(body, mesh=mesh, in_specs=in_specs, out_specs=out_specs, check_vma=False)
```

```python
import functools

import numpy as np
import jax
import jax.numpy as jnp
from jax import lax
from jax.experimental import pallas as pl
from jax.experimental.pallas import tpu as pltpu
from jax.sharding import PartitionSpec as P

F32 = jnp.float32
BF16 = jnp.bfloat16
VMEM = pl.BlockSpec(memory_space=pltpu.VMEM)
HBM = pl.BlockSpec(memory_space=pltpu.HBM)
PARAMS = pltpu.CompilerParams(vmem_limit_bytes=24 * 1024 * 1024)
SLOTS = 16


def cmul(coef, z):
    n = z.shape[-1] // 2
    re, im = z[..., :n], z[..., n:]
    cr, ci = coef
    return jnp.concatenate([cr * re - ci * im, cr * im + ci * re], axis=-1)


def coefficient(tab, i):
    return tab[i : i + 1, :], tab[SLOTS + i : SLOTS + i + 1, :]


def widen(row):
    w = row.shape[0]
    col = lax.broadcasted_iota(jnp.int32, row.shape, 0)
    left = jnp.where(col == 0, 0.0, pltpu.roll(row, 1, 0))
    right = jnp.where(col == w - 1, 0.0, pltpu.roll(row, w - 1, 0))
    return jnp.concatenate([left, row, right], axis=-1).astype(BF16)


def conv_block(wide, weights, start, count, order=(0, 1, 2)):
    w, k = wide.shape[1], wide.shape[2]
    lhs = jnp.concatenate(
        [wide[start + d : start + d + count].reshape(count * w, k) for d in range(3)], axis=-1
    )
    rhs = jnp.concatenate([weights[d] for d in order], axis=0)
    return jnp.dot(lhs, rhs, preferred_element_type=F32)


def load_weights(core, hbm, vmem, sem):
    copies = []
    for d in range(3):
        source = jnp.where(core == 1, 2 - d, d)
        copies.append(pltpu.make_async_copy(hbm.at[source], vmem.at[d], sem.at[d]))
        copies[-1].start()
    return copies


def my_core():
    return lax.rem(lax.axis_index("tm"), 2)


def convolve(weights, wide, row_of, n, step, finish):
    ready = 0
    for s in range(0, n, step):
        size = min(step, n - s)
        while ready < s + size + 2:
            wide[ready] = widen(row_of(ready))
            ready += 1
        finish(s, size, conv_block(wide, weights, s, size))


def lead_kernel(
    entries, lo, mid, hi, step, own, w_hbm, decay, phase, feed, feed_next, frame, weights, tab, factor, wide, dvec, sem
):
    core, chip = my_core(), lax.div(lax.axis_index("tm"), 2)
    rows = own.shape[0]
    n = hi - lo
    vectors = [pltpu.make_async_copy(ref, dvec.at[pl.ds(k, 1)], sem.at[3 + k]) for k, ref in enumerate((decay, phase))]
    for copy in vectors:
        copy.start()
    source = jnp.where(core == 1, rows - 1 - hi, lo - 1)
    near = pltpu.make_async_copy(own.at[pl.ds(source, n + 2)], frame.at[pl.ds(source, n + 2)], sem.at[5])
    near.start()
    wcopies = load_weights(core, w_hbm, weights, sem)
    for copy in vectors:
        copy.wait()
    expo, gate = [jnp.float32(0.0)] * SLOTS, [jnp.float32(0.0)] * SLOTS
    for q, slot, power in entries:
        expo[slot] = jnp.where(chip == q, jnp.float32(power), expo[slot])
        gate[slot] = jnp.where(chip == q, jnp.float32(1.0), gate[slot])
    for slot, power in ((8, 1), (9, 1 - core), (10, core)):
        expo[slot], gate[slot] = jnp.asarray(power).astype(F32), jnp.float32(1.0)
    spread = lambda values: jnp.concatenate([jnp.full((1, dvec.shape[1]), v, F32) for v in values], axis=0)
    expo = spread(expo)
    size = spread(gate) * jnp.exp(-expo * dvec[0:1])
    angle = expo * dvec[1:2]
    tab[...] = jnp.concatenate([size * jnp.cos(angle), size * jnp.sin(angle)], axis=0)
    mag = jnp.exp(-dvec[0:1])
    scale = jnp.sqrt(1.0 - mag * mag)
    factor[...] = jnp.concatenate([scale, scale], axis=-1)
    for copy in (*wcopies, near):
        copy.wait()
    rest = []
    for k, (begin, end) in enumerate(((0, lo - 1), (hi + 1, rows))):
        at = jnp.where(core == 1, rows - end, begin)
        rest.append(
            pltpu.make_async_copy(own.at[pl.ds(at, end - begin)], frame.at[pl.ds(at, end - begin)], sem.at[6 + k])
        )
        rest[-1].start()

    def row_of(p):
        return frame[source + jnp.where(core == 1, n + 1 - p, p)].astype(F32)

    def finish(s, count, acc):
        value = (acc * factor[...]).reshape((count,) + feed.shape[1:])
        for r in range(count):
            depth = lo + s + r
            if depth < mid:
                feed_next[depth - lo] = value[r]
            else:
                feed[depth - mid] = value[r]

    convolve(weights, wide, row_of, n, step, finish)
    for copy in rest:
        copy.wait()


def lead(entries, own, w_in, decay, phase, lo, mid, hi, step):
    rows, w, c = own.shape
    n = hi - lo
    return pl.pallas_call(
        functools.partial(lead_kernel, entries, lo, mid, hi, step),
        out_shape=[
            jax.ShapeDtypeStruct((hi - mid, w, c), F32),
            jax.ShapeDtypeStruct((mid - lo, w, c), F32),
            jax.ShapeDtypeStruct(own.shape, BF16),
            jax.ShapeDtypeStruct(w_in.shape, BF16),
            jax.ShapeDtypeStruct((2 * SLOTS, decay.shape[1]), F32),
            jax.ShapeDtypeStruct((1, 2 * decay.shape[1]), F32),
        ],
        in_specs=[HBM] * 4,
        out_specs=[VMEM] * 6,
        scratch_shapes=[
            pltpu.VMEM((n + 2, w, 3 * c), BF16),
            pltpu.VMEM((2, decay.shape[1]), F32),
            pltpu.SemaphoreType.DMA((8,)),
        ],
        compiler_params=PARAMS,
        cost_estimate=pl.CostEstimate(flops=18 * n * w * c * c, bytes_accessed=2 * own.size, transcendentals=0),
        name="lead",
    )(*(pltpu.with_memory_space_constraint(x, pltpu.HBM) for x in (own, w_in, decay, phase)))


def pair_kernel(lo, hi, step, frame, oth, weights, tab, factor, feed_own, feed, pay, factor_next, *refs):
    *border, wide = refs
    core = my_core()
    rows = oth.shape[0]
    n = hi - lo
    factor_next[...] = factor[...]
    for out in border:
        for f, ref in enumerate((frame, oth)):
            for r in range(2):
                out[f, r] = ref[core * (rows - 2) + r]
    source = jnp.where(core == 1, rows - 1 - hi, lo - 1)

    def row_of(p):
        return oth[source + jnp.where(core == 1, n + 1 - p, p)].astype(F32)

    def finish(s, count, acc):
        value = (acc * factor[...]).reshape((count,) + feed.shape[1:])
        feed[s : s + count] = value
        for r in range(count):
            pair = cmul(coefficient(tab, 9), feed_own[s + r]) + cmul(coefficient(tab, 10), value[r])
            pay[s + r] = pair.astype(BF16)

    convolve(weights, wide, row_of, n, step, finish)


def pair_up(frame, oth, weights, tab, factor, feed_own, lo, hi, step, border):
    rows, w, c = oth.shape
    n = hi - lo
    return pl.pallas_call(
        functools.partial(pair_kernel, lo, hi, step),
        out_shape=[
            jax.ShapeDtypeStruct((n, w, c), F32),
            jax.ShapeDtypeStruct((n, w, c), BF16),
            jax.ShapeDtypeStruct(factor.shape, F32),
        ]
        + [jax.ShapeDtypeStruct((2, 2, w, c), BF16)] * border,
        in_specs=[VMEM] * 6,
        out_specs=[VMEM] * (3 + border),
        scratch_shapes=[pltpu.VMEM((n + 2, w, 3 * c), BF16)],
        compiler_params=PARAMS,
        cost_estimate=pl.CostEstimate(flops=18 * n * w * c * c, bytes_accessed=2 * oth.size, transcendentals=0),
        name="pair",
    )(frame, oth, weights, tab, factor, feed_own)


def edge_kernel(
    lo, hi, step, frame, oth, weights, tab, factor, halo, feed_own, feed_oth, pay, tab_next, wide
):
    core = my_core()
    rows = frame.shape[0]
    n = hi - lo
    tab_next[...] = tab[...]
    outer = jnp.where(core == 1, lax.axis_size("space") - 1, 0)
    inside = jnp.where(lax.axis_index("space") == outer, 0.0, 1.0)
    for f, (ref, feed) in enumerate(((frame, feed_own), (oth, feed_oth))):

        def row_of(p):
            depth = lo - 1 + p
            if depth < 0:
                return halo[1 - f, jnp.where(core == 1, -1 - depth, 2 + depth)].astype(F32)
            return ref[jnp.where(core == 1, rows - 1 - depth, depth)].astype(F32)

        def finish(s, count, acc):
            value = (acc * factor[...]).reshape((count,) + feed.shape[1:])
            for r in range(count):
                row = value[r]
                if lo + s + r < 0:
                    row = row * inside
                feed[s + r] = row
                if f == 1:
                    pair = cmul(coefficient(tab, 9), feed_own[s + r]) + cmul(coefficient(tab, 10), row)
                    pay[s + r] = pair.astype(BF16)

        convolve(weights, wide.at[f], row_of, n, step, finish)


def edge_chunk(frame, oth, weights, tab, factor, halo, lo, hi, step):
    rows, w, c = frame.shape
    n = hi - lo
    return pl.pallas_call(
        functools.partial(edge_kernel, lo, hi, step),
        out_shape=[
            jax.ShapeDtypeStruct((n, w, c), F32),
            jax.ShapeDtypeStruct((n, w, c), F32),
            jax.ShapeDtypeStruct((n, w, c), BF16),
            jax.ShapeDtypeStruct(tab.shape, F32),
        ],
        in_specs=[VMEM] * 6,
        out_specs=[VMEM] * 4,
        scratch_shapes=[pltpu.VMEM((2, n + 2, w, 3 * c), BF16)],
        compiler_params=PARAMS,
        cost_estimate=pl.CostEstimate(flops=36 * n * w * c * c, bytes_accessed=20 * n * w * c, transcendentals=0),
        name="edge",
    )(frame, oth, weights, tab, factor, halo)


def relay_kernel(slot, tab, pair, got, pay):
    cp, cr = coefficient(tab, slot), coefficient(tab, slot + 1)
    for r in range(pair.shape[0]):
        pay[r] = (cmul(cp, pair[r].astype(F32)) + cmul(cr, got[r].astype(F32))).astype(BF16)


def relay(slot, tab, pair, got):
    return pl.pallas_call(
        functools.partial(relay_kernel, slot),
        out_shape=jax.ShapeDtypeStruct(pair.shape, BF16),
        in_specs=[VMEM] * 3,
        out_specs=VMEM,
        compiler_params=PARAMS,
        cost_estimate=pl.CostEstimate(flops=16 * pair.size, bytes_accessed=6 * pair.size, transcendentals=0),
        name="relay",
    )(tab, pair, got)


def output_kernel(lo, hi, begin, end, slot, step, which, keep, n_feeds, n_parts, more, *refs):
    refs = list(refs)
    take = lambda k: [refs.pop(0) for _ in range(k)]
    tab, weights, r1, r2, own, oth = take(6)
    feeds = [take(2) for _ in range(n_feeds)]
    kept = take(1)[0] if hi < end + 1 else None
    parts = take(n_parts)
    take(1 if more else 0)
    parcel = take(1)[0] if 0 in which else None
    result = take(1)[0] if 1 in which else None
    kept_out = take(1)[0] if keep else None
    wide, block, sem = refs
    core = my_core()
    first_core = core == 0
    order = [jnp.where(first_core, d, 2 - d) for d in range(3)]
    n, n_out = hi - lo, end - begin
    w, c = own.shape[1:]
    rows = own.shape[0]
    lam = coefficient(tab, 8)
    e1, e2 = coefficient(tab, slot + 2), coefficient(tab, slot + 3)
    feed_rows = [(pair, r) for pair in feeds for r in range(pair[0].shape[0])]
    at = n_out
    for part in parts:
        parcel[at : at + part.shape[0]] = part[...]
        at += part.shape[0]

    def states(r):
        pair, at = feed_rows[r]
        f_own, f_oth = pair[0][at], pair[1][at]
        carry = cmul(e1, r1[r].astype(F32)) + cmul(e2, r2[r].astype(F32))
        s0 = cmul(lam, carry) + jnp.where(first_core, f_own, f_oth)
        s1 = cmul(lam, s0) + jnp.where(first_core, f_oth, f_own)
        return jnp.where(first_core, s1, s0), jnp.where(first_core, s0, s1)

    ready = 0
    copies = []
    for s in range(0, n_out, step):
        size = min(step, n_out - s)
        while ready < s + size + 2:
            if ready < n:
                pair = states(ready)
                if keep and ready < 2:
                    for f in range(2):
                        kept_out[f, ready] = pair[f].astype(BF16)
            else:
                pair = [kept[f, ready - n].astype(F32) for f in range(2)]
            for f in which:
                wide[f, ready] = widen(pair[f])
            ready += 1
        for f in which:
            frame, dst = ((oth, parcel), (own, block))[f]
            mixed = conv_block(wide.at[f], weights, s, size, order).reshape(size, w, c)
            act = 0.5 * mixed * (1.0 + lax.erf(mixed * np.float32(0.5**0.5)))
            for r in range(s, s + size):
                depth = begin + r
                at = jnp.where(core == 1, rows - 1 - depth, depth)
                dst[r] = (frame[at].astype(F32) + act[r - s]).astype(BF16)
                if f == 1:
                    copies.append(pltpu.make_async_copy(block.at[r], result.at[at], sem.at[r]))
                    copies[-1].start()
    for copy in copies:
        copy.wait()


def output(
    tab, weights, feeds, arrived, own, oth, lo, hi, begin, end, slot, step, which, keep, kept=None, parts=(), result=None
):
    rows, w, c = own.shape
    n, n_out = hi - lo, end - begin
    args = [tab, weights, *arrived, own, oth, *(x for pair in feeds for x in pair)]
    args += ([] if kept is None else [kept]) + list(parts)
    specs = [VMEM] * len(args)
    alias = {}
    if result is not None:
        alias[len(args)] = 0
        args, specs = args + [result], specs + [HBM]
    shapes, out_specs = [], []
    if 0 in which:
        n_parcel = n_out + sum(part.shape[0] for part in parts)
        shapes, out_specs = shapes + [jax.ShapeDtypeStruct((n_parcel, w, c), BF16)], out_specs + [VMEM]
    if 1 in which:
        if result is not None:
            alias = {len(args) - 1: len(shapes)}
        shapes, out_specs = shapes + [jax.ShapeDtypeStruct(own.shape, BF16)], out_specs + [HBM]
    if keep:
        shapes, out_specs = shapes + [jax.ShapeDtypeStruct((2, 2, w, c), BF16)], out_specs + [VMEM]
    return pl.pallas_call(
        functools.partial(
            output_kernel, lo, hi, begin, end, slot, step, which, keep, len(feeds), len(parts), result is not None
        ),
        out_shape=shapes,
        in_specs=specs,
        out_specs=out_specs,
        input_output_aliases=alias,
        scratch_shapes=[
            pltpu.VMEM((2, n_out + 2, w, 3 * c), BF16),
            pltpu.VMEM((n_out, w, c), BF16),
            pltpu.SemaphoreType.DMA((n_out,)),
        ],
        compiler_params=PARAMS,
        cost_estimate=pl.CostEstimate(
            flops=18 * len(which) * n_out * w * c * c, bytes_accessed=20 * n * w * c, transcendentals=0
        ),
        name="output",
    )(*args)


def place_kernel(parcel, _, result, sem):
    core = my_core()
    rows = result.shape[0]
    copies = []
    for depth in range(parcel.shape[0]):
        at = jnp.where(core == 1, depth, rows - 1 - depth)
        copies.append(pltpu.make_async_copy(parcel.at[depth], result.at[at], sem.at[depth]))
        copies[-1].start()
    for copy in copies:
        copy.wait()


def place(parcel, result):
    return pl.pallas_call(
        place_kernel,
        out_shape=jax.ShapeDtypeStruct(result.shape, result.dtype),
        in_specs=[VMEM, HBM],
        out_specs=HBM,
        input_output_aliases={1: 0},
        scratch_shapes=[pltpu.SemaphoreType.DMA((parcel.shape[0],))],
        compiler_params=PARAMS,
        name="place",
    )(parcel, result)


ALONG_X = [(0, 1), (1, 0), (2, 3)], [(0, 2), (1, 3)]
ALONG_Y = [(0, 2), (1, 3)], [(0, 1), (2, 3), (3, 2)]


def roles(n):
    if n != 8:
        return [(q, slot, 0) for q in range(n // 2) for slot in (2, 6)]
    along_x = [(0, 0, 2), (0, 1, 0), (1, 0, 0), (1, 1, 2), (1, 2, 0), (2, 3, 0), (3, 2, 0), (3, 3, 2)]
    along_y = [(0, 4, 0), (2, 4, 0), (2, 5, 4), (3, 5, 0), (1, 7, 0), (2, 6, 2), (2, 7, 0), (3, 6, 2), (3, 7, 0)]
    return along_x + along_y


def both_cores(pairs):
    return [(2 * a + k, 2 * b + k) for a, b in pairs for k in range(2)]


def exchange(n, slot, tab, pair, decay, phase):
    if n == 8:
        one, two = ALONG_X if slot == 0 else ALONG_Y
        r1 = lax.ppermute(pair, "tm", both_cores(one))
        r2 = lax.ppermute(relay(slot, tab, pair, r1), "tm", both_cores(two))
        return r1, r2
    chips, stride, total = n // 2, 1, pair.astype(F32)
    while stride < chips:
        steps = both_cores([(i, i + stride) for i in range(chips - stride)])
        moved = lax.ppermute(total.astype(BF16), "tm", steps).astype(F32)
        size, angle = jnp.exp(-2.0 * stride * decay), 2.0 * stride * phase
        total = total + cmul((size * jnp.cos(angle), size * jnp.sin(angle)), moved)
        stride *= 2
    carry = lax.ppermute(total.astype(BF16), "tm", both_cores([(i, i + 1) for i in range(chips - 1)]))
    return carry, jnp.zeros_like(carry)


def on_device(n, n_space, frames_in, w_input, decay_rate, phase, w_output):
    own = frames_in[0]
    rows, w, c = own.shape
    decay, phase = decay_rate[None], phase[None]
    w_in = w_input.reshape(3, 3 * c, -1)
    w_out = w_output.reshape(3, -1, c)
    swap = [(i, i ^ 1) for i in range(n)]
    step = 3
    oth = lax.ppermute(own, "tm", swap)

    half = rows // 2
    last = max(2, (half + 2) * 6 // 18)
    middle = (half + 2 - last) // 2
    spans = [(last - 1 + middle, half + 1), (last - 1, last - 1 + middle), (-1, last - 1)]
    links = [
        ((t ^ 1) * n_space + s, t * n_space + s + 1) if t % 2 == 0 else ((t ^ 1) * n_space + s + 1, t * n_space + s)
        for t in range(n)
        for s in range(n_space - 1)
    ]
    (lo1, hi1), (lo2, hi2), (lo3, hi3) = spans
    mine1, mine2, frame, weights, tab, factor = lead(roles(n), own, w_in, decay, phase, lo2, lo1, hi1, step)
    theirs1, pair1, factor, border = pair_up(frame, oth, weights, tab, factor, mine1, lo1, hi1, step, True)
    halo = lax.ppermute(border, ("tm", "space"), links)
    theirs2, pair2, factor = pair_up(frame, oth, weights, tab, factor, mine2, lo2, hi2, step, False)
    mine3, theirs3, pair3, tab = edge_chunk(frame, oth, weights, tab, factor, halo, lo3, hi3, step)
    arrived1 = exchange(n, 0, tab, pair1, decay, phase)
    arrived2 = exchange(n, 4, tab, pair2, decay, phase)
    arrived3 = exchange(n, 0, tab, pair3, decay, phase)
    parcel1, result, kept = output(
        tab, w_out, [(mine1, theirs1)], arrived1, frame, oth, lo1, hi1, lo1 + 1, half, 0, step, (0, 1), True
    )
    parcel2, result, kept = output(
        tab, w_out, [(mine2, theirs2)], arrived2, frame, oth, lo2, hi2, lo2 + 1, hi2 + 1, 4, step, (0, 1), True,
        kept=kept, result=result,
    )
    rest = (tab, w_out, [(mine3, theirs3)], arrived3, frame, oth, lo3, hi3, lo3 + 1, hi3 + 1, 0, step)
    (parcel,) = output(*rest, (0,), False, kept=kept, parts=(parcel2, parcel1))
    (result,) = output(*rest, (1,), False, kept=kept, result=result)
    return place(lax.ppermute(parcel, "tm", swap), result)[None]


def solution(mesh):
    in_specs = (P("tm", "space", None, None), P(), P(), P(), P())
    out_specs = P("tm", "space", None, None)
    body = functools.partial(on_device, mesh.shape["tm"], mesh.shape["space"])
    return jax.shard_map(body, mesh=mesh, in_specs=in_specs, out_specs=out_specs, check_vma=False)
```

```python
import functools

import numpy as np
import jax
import jax.numpy as jnp
from jax import lax
from jax.experimental import pallas as pl
from jax.experimental.pallas import tpu as pltpu
from jax.sharding import PartitionSpec as P

F32 = jnp.float32
BF16 = jnp.bfloat16
VMEM = pl.BlockSpec(memory_space=pltpu.VMEM)
HBM = pl.BlockSpec(memory_space=pltpu.HBM)
PARAMS = pltpu.CompilerParams(vmem_limit_bytes=24 * 1024 * 1024)
SHORT = pl.CostEstimate(flops=1, bytes_accessed=1, transcendentals=0)
LONG = pl.CostEstimate(flops=1, bytes_accessed=1, transcendentals=0)
SLOTS = 16


def cmul(coef, z):
    n = z.shape[-1] // 2
    re, im = z[..., :n], z[..., n:]
    cr, ci = coef
    return jnp.concatenate([cr * re - ci * im, cr * im + ci * re], axis=-1)


def coefficient(tab, i):
    return tab[i : i + 1, :], tab[SLOTS + i : SLOTS + i + 1, :]


def widen(row):
    w = row.shape[0]
    col = lax.broadcasted_iota(jnp.int32, row.shape, 0)
    left = jnp.where(col == 0, 0.0, pltpu.roll(row, 1, 0))
    right = jnp.where(col == w - 1, 0.0, pltpu.roll(row, w - 1, 0))
    return jnp.concatenate([left, row, right], axis=-1).astype(BF16)


def conv_block(wide, weights, start, count, order=(0, 1, 2)):
    w, k = wide.shape[1], wide.shape[2]
    lhs = jnp.concatenate(
        [wide[start + d : start + d + count].reshape(count * w, k) for d in range(3)], axis=-1
    )
    rhs = jnp.concatenate([weights[d] for d in order], axis=0)
    return jnp.dot(lhs, rhs, preferred_element_type=F32)


def load_weights(core, hbm, vmem, sem):
    copies = []
    for d in range(3):
        source = jnp.where(core == 1, 2 - d, d)
        copies.append(pltpu.make_async_copy(hbm.at[source], vmem.at[d], sem.at[d]))
        copies[-1].start()
    return copies


def my_core():
    return lax.rem(lax.axis_index("tm"), 2)


def convolve(weights, wide, row_of, n, step, finish):
    ready = 0
    for s in range(0, n, step):
        size = min(step, n - s)
        while ready < s + size + 2:
            wide[ready] = widen(row_of(ready))
            ready += 1
        finish(s, size, conv_block(wide, weights, s, size))


def lead_kernel(
    entries, lo, mid, hi, step, own, w_hbm, decay, phase, feed, feed_next, frame, weights, tab, factor, wide, dvec, sem
):
    core, chip = my_core(), lax.div(lax.axis_index("tm"), 2)
    rows = own.shape[0]
    n = hi - lo
    vectors = [pltpu.make_async_copy(ref, dvec.at[pl.ds(k, 1)], sem.at[3 + k]) for k, ref in enumerate((decay, phase))]
    for copy in vectors:
        copy.start()
    source = jnp.where(core == 1, rows - 1 - hi, lo - 1)
    near = pltpu.make_async_copy(own.at[pl.ds(source, n + 2)], frame.at[pl.ds(source, n + 2)], sem.at[5])
    near.start()
    wcopies = load_weights(core, w_hbm, weights, sem)
    for copy in vectors:
        copy.wait()
    expo, gate = [jnp.float32(0.0)] * SLOTS, [jnp.float32(0.0)] * SLOTS
    for q, slot, power in entries:
        expo[slot] = jnp.where(chip == q, jnp.float32(power), expo[slot])
        gate[slot] = jnp.where(chip == q, jnp.float32(1.0), gate[slot])
    for slot, power in ((8, 1), (9, 1 - core), (10, core)):
        expo[slot], gate[slot] = jnp.asarray(power).astype(F32), jnp.float32(1.0)
    spread = lambda values: jnp.concatenate([jnp.full((1, dvec.shape[1]), v, F32) for v in values], axis=0)
    expo = spread(expo)
    size = spread(gate) * jnp.exp(-expo * dvec[0:1])
    angle = expo * dvec[1:2]
    tab[...] = jnp.concatenate([size * jnp.cos(angle), size * jnp.sin(angle)], axis=0)
    mag = jnp.exp(-dvec[0:1])
    scale = jnp.sqrt(1.0 - mag * mag)
    factor[...] = jnp.concatenate([scale, scale], axis=-1)
    for copy in (*wcopies, near):
        copy.wait()
    rest = []
    for k, (begin, end) in enumerate(((0, lo - 1), (hi + 1, rows))):
        at = jnp.where(core == 1, rows - end, begin)
        rest.append(
            pltpu.make_async_copy(own.at[pl.ds(at, end - begin)], frame.at[pl.ds(at, end - begin)], sem.at[6 + k])
        )
        rest[-1].start()

    def row_of(p):
        return frame[source + jnp.where(core == 1, n + 1 - p, p)].astype(F32)

    def finish(s, count, acc):
        value = (acc * factor[...]).reshape((count,) + feed.shape[1:])
        for r in range(count):
            depth = lo + s + r
            if depth < mid:
                feed_next[depth - lo] = value[r]
            else:
                feed[depth - mid] = value[r]

    convolve(weights, wide, row_of, n, step, finish)
    for copy in rest:
        copy.wait()


def lead(entries, own, w_in, decay, phase, lo, mid, hi, step):
    rows, w, c = own.shape
    n = hi - lo
    return pl.pallas_call(
        functools.partial(lead_kernel, entries, lo, mid, hi, step),
        out_shape=[
            jax.ShapeDtypeStruct((hi - mid, w, c), F32),
            jax.ShapeDtypeStruct((mid - lo, w, c), F32),
            jax.ShapeDtypeStruct(own.shape, BF16),
            jax.ShapeDtypeStruct(w_in.shape, BF16),
            jax.ShapeDtypeStruct((2 * SLOTS, decay.shape[1]), F32),
            jax.ShapeDtypeStruct((1, 2 * decay.shape[1]), F32),
        ],
        in_specs=[HBM] * 4,
        out_specs=[VMEM] * 6,
        scratch_shapes=[
            pltpu.VMEM((n + 2, w, 3 * c), BF16),
            pltpu.VMEM((2, decay.shape[1]), F32),
            pltpu.SemaphoreType.DMA((8,)),
        ],
        compiler_params=PARAMS,
        cost_estimate=SHORT,
        name="lead",
    )(*(pltpu.with_memory_space_constraint(x, pltpu.HBM) for x in (own, w_in, decay, phase)))


def pair_kernel(lo, hi, step, oth, weights, tab, factor, feed_own, feed, pay, tab_next, wide):
    core = my_core()
    rows = oth.shape[0]
    n = hi - lo
    tab_next[...] = tab[...]
    source = jnp.where(core == 1, rows - 1 - hi, lo - 1)

    def row_of(p):
        return oth[source + jnp.where(core == 1, n + 1 - p, p)].astype(F32)

    def finish(s, count, acc):
        value = (acc * factor[...]).reshape((count,) + feed.shape[1:])
        feed[s : s + count] = value
        for r in range(count):
            pair = cmul(coefficient(tab, 9), feed_own[s + r]) + cmul(coefficient(tab, 10), value[r])
            pay[s + r] = pair.astype(BF16)

    convolve(weights, wide, row_of, n, step, finish)


def pair_up(oth, weights, tab, factor, feed_own, lo, hi, step):
    rows, w, c = oth.shape
    n = hi - lo
    return pl.pallas_call(
        functools.partial(pair_kernel, lo, hi, step),
        out_shape=[
            jax.ShapeDtypeStruct((n, w, c), F32),
            jax.ShapeDtypeStruct((n, w, c), BF16),
            jax.ShapeDtypeStruct(tab.shape, F32),
        ],
        in_specs=[VMEM] * 5,
        out_specs=[VMEM] * 3,
        scratch_shapes=[pltpu.VMEM((n + 2, w, 3 * c), BF16)],
        compiler_params=PARAMS,
        cost_estimate=SHORT,
        name="pair",
    )(oth, weights, tab, factor, feed_own)


def border_kernel(frame, oth, tab, border, tab_next):
    tab_next[...] = tab[...]
    at = my_core() * (frame.shape[0] - 2)
    for f, ref in enumerate((frame, oth)):
        for r in range(2):
            border[f, r] = ref[at + r]


def outer_rows(frame, oth, tab):
    return pl.pallas_call(
        border_kernel,
        out_shape=[
            jax.ShapeDtypeStruct((2, 2) + frame.shape[1:], BF16),
            jax.ShapeDtypeStruct(tab.shape, F32),
        ],
        in_specs=[VMEM] * 3,
        out_specs=[VMEM] * 2,
        compiler_params=PARAMS,
        cost_estimate=SHORT,
        name="border",
    )(frame, oth, tab)


def edge_kernel(
    lo, hi, step, frame, oth, weights, tab, factor, halo, feed_own, feed_oth, pay, tab_next, wide
):
    core = my_core()
    rows = frame.shape[0]
    n = hi - lo
    tab_next[...] = tab[...]
    outer = jnp.where(core == 1, lax.axis_size("space") - 1, 0)
    inside = jnp.where(lax.axis_index("space") == outer, 0.0, 1.0)
    for f, (ref, feed) in enumerate(((frame, feed_own), (oth, feed_oth))):

        def row_of(p):
            depth = lo - 1 + p
            if depth < 0:
                return halo[1 - f, jnp.where(core == 1, -1 - depth, 2 + depth)].astype(F32)
            return ref[jnp.where(core == 1, rows - 1 - depth, depth)].astype(F32)

        def finish(s, count, acc):
            value = (acc * factor[...]).reshape((count,) + feed.shape[1:])
            for r in range(count):
                row = value[r]
                if lo + s + r < 0:
                    row = row * inside
                feed[s + r] = row
                if f == 1:
                    pair = cmul(coefficient(tab, 9), feed_own[s + r]) + cmul(coefficient(tab, 10), row)
                    pay[s + r] = pair.astype(BF16)

        convolve(weights, wide.at[f], row_of, n, step, finish)


def edge_chunk(frame, oth, weights, tab, factor, halo, lo, hi, step):
    rows, w, c = frame.shape
    n = hi - lo
    return pl.pallas_call(
        functools.partial(edge_kernel, lo, hi, step),
        out_shape=[
            jax.ShapeDtypeStruct((n, w, c), F32),
            jax.ShapeDtypeStruct((n, w, c), F32),
            jax.ShapeDtypeStruct((n, w, c), BF16),
            jax.ShapeDtypeStruct(tab.shape, F32),
        ],
        in_specs=[VMEM] * 6,
        out_specs=[VMEM] * 4,
        scratch_shapes=[pltpu.VMEM((2, n + 2, w, 3 * c), BF16)],
        compiler_params=PARAMS,
        cost_estimate=SHORT,
        name="edge",
    )(frame, oth, weights, tab, factor, halo)


def relay_kernel(slot, tab, pair, got, pay, tab_next):
    tab_next[...] = tab[...]
    cp, cr = coefficient(tab, slot), coefficient(tab, slot + 1)
    for r in range(pair.shape[0]):
        pay[r] = (cmul(cp, pair[r].astype(F32)) + cmul(cr, got[r].astype(F32))).astype(BF16)


def relay(slot, tab, pair, got):
    return pl.pallas_call(
        functools.partial(relay_kernel, slot),
        out_shape=[jax.ShapeDtypeStruct(pair.shape, BF16), jax.ShapeDtypeStruct(tab.shape, F32)],
        in_specs=[VMEM] * 3,
        out_specs=[VMEM] * 2,
        compiler_params=PARAMS,
        cost_estimate=SHORT,
        name="relay",
    )(tab, pair, got)


def output_kernel(lo, hi, begin, end, slot, step, which, seam, closing, n_parts, blocks_at, more, *refs):
    refs = list(refs)
    take = lambda k: [refs.pop(0) for _ in range(k)]
    tab, weights, r1, r2, own, oth, feed_own, feed_oth = take(8)
    kept = take(1)[0] if not seam else None
    near, far = take(2) if closing else (None, None)
    parts = take(n_parts)
    blocks = take(len(blocks_at))
    take(1 if more else 0)
    parcel = take(1)[0] if 0 in which else None
    block = take(1)[0] if 1 in which else None
    result = take(1)[0] if blocks_at else None
    kept_out = take(1)[0] if not closing else None
    near_out, send = take(2) if seam else (None, None)
    tab_next = take(1)[0] if 0 in which else None
    wide = take(1)[0]
    core = my_core()
    first_core = core == 0
    order = [jnp.where(first_core, d, 2 - d) for d in range(3)]
    n, n_out = hi - lo, end - begin
    w, c = own.shape[1:]
    rows = own.shape[0]
    copies = []
    for ref, depth in zip(blocks, blocks_at):
        copies += start_rows(ref, result, core, depth, refs[0], len(copies))
    if tab_next is not None:
        tab_next[...] = tab[...]
    lam = coefficient(tab, 8)
    e1, e2 = coefficient(tab, slot + 2), coefficient(tab, slot + 3)
    at = n_out
    for part in parts:
        parcel[at : at + part.shape[0]] = part[...]
        at += part.shape[0]

    def states(r):
        f_own, f_oth = feed_own[r], feed_oth[r]
        carry = cmul(e1, r1[r].astype(F32)) + cmul(e2, r2[r].astype(F32))
        s0 = cmul(lam, carry) + jnp.where(first_core, f_own, f_oth)
        s1 = cmul(lam, s0) + jnp.where(first_core, f_oth, f_own)
        return jnp.where(first_core, s1, s0), jnp.where(first_core, s0, s1)

    def emit(f, first_wide, size, depth, place):
        frame, dst = ((oth, parcel), (own, block))[f]
        mixed = conv_block(wide.at[f], weights, first_wide, size, order).reshape(size, w, c)
        act = 0.5 * mixed * (1.0 + lax.erf(mixed * np.float32(0.5**0.5)))
        for r in range(size):
            row = jnp.where(core == 1, rows - 1 - depth - r, depth + r)
            dst[place + r] = (frame[row].astype(F32) + act[r]).astype(BF16)

    if closing:
        top = n_out + 2
        for f in which:
            for k, z in enumerate((near[f, 0], near[f, 1], far[1 - f])):
                wide[f, top + k] = widen(z.astype(F32))
            emit(f, top, 1, rows // 2 - 1, (parcel if f == 0 else block).shape[0] - 1)
    ready = 0
    for s in range(0, n_out, step):
        size = min(step, n_out - s)
        while ready < s + size + 2:
            if ready < n:
                pair = states(ready)
                for f in range(2):
                    if not closing and ready < 2:
                        kept_out[f, ready] = pair[f].astype(BF16)
                    if seam and ready >= n - 2:
                        near_out[f, ready - (n - 2)] = pair[f].astype(BF16)
                    if seam and ready == n - 1:
                        send[f] = pair[f].astype(BF16)
            else:
                pair = [kept[f, ready - n].astype(F32) for f in range(2)]
            for f in which:
                wide[f, ready] = widen(pair[f])
            ready += 1
        for f in which:
            emit(f, s, size, begin + s, s)
    for copy in copies:
        copy.wait()


def start_rows(block, result, side, depth, sem, at=0):
    copies = []
    for r in range(block.shape[0]):
        row = jnp.where(side == 1, result.shape[0] - 1 - depth - r, depth + r)
        copies.append(pltpu.make_async_copy(block.at[r], result.at[row], sem.at[at + r]))
        copies[-1].start()
    return copies


def output(
    tab, weights, feeds, arrived, own, oth, lo, hi, begin, end, slot, step, which, kept=None, seam=None, parts=(),
    blocks=(), blocks_at=(), result=None,
):
    rows, w, c = own.shape
    n, n_out = hi - lo, end - begin
    first, closing = kept is None, seam is not None
    args = [tab, weights, *arrived, own, oth, *feeds]
    args += ([] if first else [kept]) + (list(seam) if closing else []) + list(parts) + list(blocks)
    specs = [VMEM] * len(args)
    alias = {}
    shapes, out_specs = [], []
    extra = 1 if closing else 0
    if 0 in which:
        n_parcel = n_out + extra + sum(part.shape[0] for part in parts)
        shapes, out_specs = shapes + [jax.ShapeDtypeStruct((n_parcel, w, c), BF16)], out_specs + [VMEM]
    if 1 in which:
        shapes = shapes + [jax.ShapeDtypeStruct((n_out + extra, w, c), BF16)]
        out_specs = out_specs + [VMEM]
    scratch = [pltpu.VMEM((2, n_out + (5 if closing else 2), w, 3 * c), BF16)]
    if blocks:
        scratch += [pltpu.SemaphoreType.DMA((sum(ref.shape[0] for ref in blocks),))]
        if result is not None:
            alias = {len(args): len(shapes)}
            args, specs = args + [result], specs + [HBM]
        shapes, out_specs = shapes + [jax.ShapeDtypeStruct(own.shape, BF16)], out_specs + [HBM]
    if not closing:
        shapes, out_specs = shapes + [jax.ShapeDtypeStruct((2, 2, w, c), BF16)], out_specs + [VMEM]
    if first:
        shapes = shapes + [jax.ShapeDtypeStruct((2, 2, w, c), BF16), jax.ShapeDtypeStruct((2, w, c), BF16)]
        out_specs = out_specs + [VMEM, VMEM]
    if 0 in which:
        shapes, out_specs = shapes + [jax.ShapeDtypeStruct(tab.shape, F32)], out_specs + [VMEM]
    return pl.pallas_call(
        functools.partial(
            output_kernel, lo, hi, begin, end, slot, step, which, first, closing, len(parts), blocks_at, result is not None
        ),
        out_shape=shapes,
        in_specs=specs,
        out_specs=out_specs,
        input_output_aliases=alias,
        scratch_shapes=scratch,
        compiler_params=PARAMS,
        cost_estimate=LONG if first else SHORT,
        name="output",
    )(*args)


def place_kernel(depth, n_two, parcel, block, _, result, sem):
    core = my_core()
    inner = result.shape[0] // 2 - 1
    n = block.shape[0] - 1
    at = 0
    copies = []
    for ref, side, start, count in ((parcel, 1 - core, 0, n + n_two), (block, core, depth, n)):
        for r in range(count + 1):
            to = inner if r == count else start + r
            row = jnp.where(side == 1, result.shape[0] - 1 - to, to)
            copies.append(pltpu.make_async_copy(ref.at[r], result.at[row], sem.at[at]))
            copies[-1].start()
            at += 1
    for copy in copies:
        copy.wait()


def place(parcel, block, depth, result):
    return pl.pallas_call(
        functools.partial(place_kernel, depth, parcel.shape[0] - block.shape[0]),
        out_shape=jax.ShapeDtypeStruct(result.shape, result.dtype),
        in_specs=[VMEM, VMEM, HBM],
        out_specs=HBM,
        input_output_aliases={2: 0},
        scratch_shapes=[pltpu.SemaphoreType.DMA((parcel.shape[0] + block.shape[0],))],
        compiler_params=PARAMS,
        name="place",
    )(parcel, block, result)


ALONG_X = [(0, 1), (1, 0), (2, 3)], [(0, 2), (1, 3)]
ALONG_Y = [(0, 2), (1, 3)], [(0, 1), (2, 3), (3, 2)]


def roles(n):
    if n != 8:
        return [(q, slot, 0) for q in range(n // 2) for slot in (2, 6)]
    along_x = [(0, 0, 2), (0, 1, 0), (1, 0, 0), (1, 1, 2), (1, 2, 0), (2, 3, 0), (3, 2, 0), (3, 3, 2)]
    along_y = [(0, 4, 0), (2, 4, 0), (2, 5, 4), (3, 5, 0), (1, 7, 0), (2, 6, 2), (2, 7, 0), (3, 6, 2), (3, 7, 0)]
    return along_x + along_y


def both_cores(pairs):
    return [(2 * a + k, 2 * b + k) for a, b in pairs for k in range(2)]


def first_stage(n, slot, pair, decay, phase):
    if n == 8:
        return lax.ppermute(pair, "tm", both_cores((ALONG_X if slot == 0 else ALONG_Y)[0]))
    chips, stride, total = n // 2, 1, pair.astype(F32)
    while stride < chips:
        steps = both_cores([(i, i + stride) for i in range(chips - stride)])
        moved = lax.ppermute(total.astype(BF16), "tm", steps).astype(F32)
        size, angle = jnp.exp(-2.0 * stride * decay), 2.0 * stride * phase
        total = total + cmul((size * jnp.cos(angle), size * jnp.sin(angle)), moved)
        stride *= 2
    return lax.ppermute(total.astype(BF16), "tm", both_cores([(i, i + 1) for i in range(chips - 1)]))


def second_stage(n, slot, tab, pair, got):
    if n != 8:
        return jnp.zeros_like(got), tab
    pay, tab = relay(slot, tab, pair, got)
    return lax.ppermute(pay, "tm", both_cores((ALONG_X if slot == 0 else ALONG_Y)[1])), tab


def on_device(n, n_space, frames_in, w_input, decay_rate, phase, w_output):
    own = frames_in[0]
    rows, w, c = own.shape
    decay, phase = decay_rate[None], phase[None]
    w_in = w_input.reshape(3, 3 * c, -1)
    w_out = w_output.reshape(3, -1, c)
    swap = [(i, i ^ 1) for i in range(n)]
    step = 3
    oth = lax.ppermute(own, "tm", swap)

    half = rows // 2
    total = half + 1
    last = max(2, total * 5 // 17)
    middle = max(2, total * 5 // 17)
    spans = [(last - 1 + middle, half), (last - 1, last - 1 + middle), (-1, last - 1)]
    links = [
        ((t ^ 1) * n_space + s, t * n_space + s + 1) if t % 2 == 0 else ((t ^ 1) * n_space + s + 1, t * n_space + s)
        for t in range(n)
        for s in range(n_space - 1)
    ]
    (lo1, hi1), (lo2, hi2), (lo3, hi3) = spans
    mine1, mine2, frame, weights, tab, factor = lead(roles(n), own, w_in, decay, phase, lo2, lo1, hi1, step)
    border, tab = outer_rows(frame, oth, tab)
    halo = lax.ppermute(border, ("tm", "space"), links)
    theirs1, pair1, tab = pair_up(oth, weights, tab, factor, mine1, lo1, hi1, step)
    got1 = first_stage(n, 0, pair1, decay, phase)
    theirs2, pair2, tab = pair_up(oth, weights, tab, factor, mine2, lo2, hi2, step)
    got2 = first_stage(n, 4, pair2, decay, phase)
    mine3, theirs3, pair3, tab = edge_chunk(frame, oth, weights, tab, factor, halo, lo3, hi3, step)
    got3 = first_stage(n, 0, pair3, decay, phase)
    also1, tab = second_stage(n, 0, tab, pair1, got1)
    also2, tab = second_stage(n, 4, tab, pair2, got2)
    also3, tab = second_stage(n, 0, tab, pair3, got3)
    args = (w_out, (mine1, theirs1), (got1, also1), frame, oth, lo1, hi1, lo1 + 1, half - 1, 0, 2)
    parcel1, block1, kept, near, send, tab = output(tab, *args, (0, 1))
    far = lax.ppermute(send, "tm", swap)
    args = (w_out, (mine2, theirs2), (got2, also2), frame, oth, lo2, hi2, lo2 + 1, hi2 + 1, 4, 2)
    parcel2, block2, result, kept, tab = output(
        tab, *args, (0, 1), kept=kept, blocks=(block1,), blocks_at=(lo1 + 1,)
    )
    args = (w_out, (mine3, theirs3), (got3, also3), frame, oth, lo3, hi3, lo3 + 1, hi3 + 1, 0, 2)
    parcel, tab = output(tab, *args, (0,), kept=kept, seam=(near, far), parts=(parcel2, parcel1))
    block3, result = output(
        tab, *args, (1,), kept=kept, seam=(near, far), blocks=(block2,), blocks_at=(lo2 + 1,), result=result
    )
    return place(lax.ppermute(parcel, "tm", swap), block3, lo3 + 1, result)[None]


def solution(mesh):
    in_specs = (P("tm", "space", None, None), P(), P(), P(), P())
    out_specs = P("tm", "space", None, None)
    body = functools.partial(on_device, mesh.shape["tm"], mesh.shape["space"])
    return jax.shard_map(body, mesh=mesh, in_specs=in_specs, out_specs=out_specs, check_vma=False)
```

```python
import functools

import numpy as np
import jax
import jax.numpy as jnp
from jax import lax
from jax.experimental import pallas as pl
from jax.experimental.pallas import tpu as pltpu
from jax.sharding import PartitionSpec as P

F32 = jnp.float32
BF16 = jnp.bfloat16
VMEM = pl.BlockSpec(memory_space=pltpu.VMEM)
HBM = pl.BlockSpec(memory_space=pltpu.HBM)
PARAMS = pltpu.CompilerParams(vmem_limit_bytes=24 * 1024 * 1024)
SHORT = pl.CostEstimate(flops=1, bytes_accessed=1, transcendentals=0)
CLOSING = pl.CostEstimate(flops=4000000000, bytes_accessed=1, transcendentals=0)
LONG = pl.CostEstimate(flops=1, bytes_accessed=1, transcendentals=0)
SLOTS = 16


def cmul(coef, z):
    n = z.shape[-1] // 2
    re, im = z[..., :n], z[..., n:]
    cr, ci = coef
    return jnp.concatenate([cr * re - ci * im, cr * im + ci * re], axis=-1)


def coefficient(tab, i):
    return tab[i : i + 1, :], tab[SLOTS + i : SLOTS + i + 1, :]


def widen(row):
    w = row.shape[0]
    col = lax.broadcasted_iota(jnp.int32, row.shape, 0)
    left = jnp.where(col == 0, 0.0, pltpu.roll(row, 1, 0))
    right = jnp.where(col == w - 1, 0.0, pltpu.roll(row, w - 1, 0))
    return jnp.concatenate([left, row, right], axis=-1).astype(BF16)


def conv_block(wide, weights, start, count, order=(0, 1, 2)):
    w, k = wide.shape[1], wide.shape[2]
    lhs = jnp.concatenate(
        [wide[start + d : start + d + count].reshape(count * w, k) for d in range(3)], axis=-1
    )
    rhs = jnp.concatenate([weights[d] for d in order], axis=0)
    return jnp.dot(lhs, rhs, preferred_element_type=F32)


def load_weights(core, hbm, vmem, sem):
    copies = []
    for d in range(3):
        source = jnp.where(core == 1, 2 - d, d)
        copies.append(pltpu.make_async_copy(hbm.at[source], vmem.at[d], sem.at[d]))
        copies[-1].start()
    return copies


def my_core():
    return lax.rem(lax.axis_index("tm"), 2)


def convolve(weights, wide, row_of, n, step, finish):
    ready = 0
    for s in range(0, n, step):
        size = min(step, n - s)
        while ready < s + size + 2:
            wide[ready] = widen(row_of(ready))
            ready += 1
        finish(s, size, conv_block(wide, weights, s, size))


def lead_kernel(
    entries, lo, mid, hi, step, own, w_hbm, decay, phase, feed, feed_next, frame, weights, tab, factor, wide, dvec, sem
):
    core, chip = my_core(), lax.div(lax.axis_index("tm"), 2)
    rows = own.shape[0]
    n = hi - lo
    vectors = [pltpu.make_async_copy(ref, dvec.at[pl.ds(k, 1)], sem.at[3 + k]) for k, ref in enumerate((decay, phase))]
    for copy in vectors:
        copy.start()
    source = jnp.where(core == 1, rows - 1 - hi, lo - 1)
    near = pltpu.make_async_copy(own.at[pl.ds(source, n + 2)], frame.at[pl.ds(source, n + 2)], sem.at[5])
    near.start()
    wcopies = load_weights(core, w_hbm, weights, sem)
    for copy in vectors:
        copy.wait()
    expo, gate = [jnp.float32(0.0)] * SLOTS, [jnp.float32(0.0)] * SLOTS
    for q, slot, power in entries:
        expo[slot] = jnp.where(chip == q, jnp.float32(power), expo[slot])
        gate[slot] = jnp.where(chip == q, jnp.float32(1.0), gate[slot])
    for slot, power in ((8, 1), (9, 1 - core), (10, core)):
        expo[slot], gate[slot] = jnp.asarray(power).astype(F32), jnp.float32(1.0)
    spread = lambda values: jnp.concatenate([jnp.full((1, dvec.shape[1]), v, F32) for v in values], axis=0)
    expo = spread(expo)
    size = spread(gate) * jnp.exp(-expo * dvec[0:1])
    angle = expo * dvec[1:2]
    tab[...] = jnp.concatenate([size * jnp.cos(angle), size * jnp.sin(angle)], axis=0)
    mag = jnp.exp(-dvec[0:1])
    scale = jnp.sqrt(1.0 - mag * mag)
    factor[...] = jnp.concatenate([scale, scale], axis=-1)
    for copy in (*wcopies, near):
        copy.wait()
    rest = []
    for k, (begin, end) in enumerate(((0, lo - 1), (hi + 1, rows))):
        at = jnp.where(core == 1, rows - end, begin)
        rest.append(
            pltpu.make_async_copy(own.at[pl.ds(at, end - begin)], frame.at[pl.ds(at, end - begin)], sem.at[6 + k])
        )
        rest[-1].start()

    def row_of(p):
        return frame[source + jnp.where(core == 1, n + 1 - p, p)].astype(F32)

    def finish(s, count, acc):
        value = (acc * factor[...]).reshape((count,) + feed.shape[1:])
        for r in range(count):
            depth = lo + s + r
            if depth < mid:
                feed_next[depth - lo] = value[r]
            else:
                feed[depth - mid] = value[r]

    convolve(weights, wide, row_of, n, step, finish)
    for copy in rest:
        copy.wait()


def lead(entries, own, w_in, decay, phase, lo, mid, hi, step):
    rows, w, c = own.shape
    n = hi - lo
    return pl.pallas_call(
        functools.partial(lead_kernel, entries, lo, mid, hi, step),
        out_shape=[
            jax.ShapeDtypeStruct((hi - mid, w, c), F32),
            jax.ShapeDtypeStruct((mid - lo, w, c), F32),
            jax.ShapeDtypeStruct(own.shape, BF16),
            jax.ShapeDtypeStruct(w_in.shape, BF16),
            jax.ShapeDtypeStruct((2 * SLOTS, decay.shape[1]), F32),
            jax.ShapeDtypeStruct((1, 2 * decay.shape[1]), F32),
        ],
        in_specs=[HBM] * 4,
        out_specs=[VMEM] * 6,
        scratch_shapes=[
            pltpu.VMEM((n + 2, w, 3 * c), BF16),
            pltpu.VMEM((2, decay.shape[1]), F32),
            pltpu.SemaphoreType.DMA((8,)),
        ],
        compiler_params=PARAMS,
        cost_estimate=SHORT,
        name="lead",
    )(*(pltpu.with_memory_space_constraint(x, pltpu.HBM) for x in (own, w_in, decay, phase)))


def pair_kernel(lo, hi, step, oth, weights, tab, factor, feed_own, feed, pay, tab_next, wide):
    core = my_core()
    rows = oth.shape[0]
    n = hi - lo
    tab_next[...] = tab[...]
    source = jnp.where(core == 1, rows - 1 - hi, lo - 1)

    def row_of(p):
        return oth[source + jnp.where(core == 1, n + 1 - p, p)].astype(F32)

    def finish(s, count, acc):
        value = (acc * factor[...]).reshape((count,) + feed.shape[1:])
        feed[s : s + count] = value
        for r in range(count):
            pair = cmul(coefficient(tab, 9), feed_own[s + r]) + cmul(coefficient(tab, 10), value[r])
            pay[s + r] = pair.astype(BF16)

    convolve(weights, wide, row_of, n, step, finish)


def pair_up(oth, weights, tab, factor, feed_own, lo, hi, step):
    rows, w, c = oth.shape
    n = hi - lo
    return pl.pallas_call(
        functools.partial(pair_kernel, lo, hi, step),
        out_shape=[
            jax.ShapeDtypeStruct((n, w, c), F32),
            jax.ShapeDtypeStruct((n, w, c), BF16),
            jax.ShapeDtypeStruct(tab.shape, F32),
        ],
        in_specs=[VMEM] * 5,
        out_specs=[VMEM] * 3,
        scratch_shapes=[pltpu.VMEM((n + 2, w, 3 * c), BF16)],
        compiler_params=PARAMS,
        cost_estimate=SHORT,
        name="pair",
    )(oth, weights, tab, factor, feed_own)


def border_kernel(frame, oth, tab, border, tab_next):
    tab_next[...] = tab[...]
    at = my_core() * (frame.shape[0] - 2)
    for f, ref in enumerate((frame, oth)):
        for r in range(2):
            border[f, r] = ref[at + r]


def outer_rows(frame, oth, tab):
    return pl.pallas_call(
        border_kernel,
        out_shape=[
            jax.ShapeDtypeStruct((2, 2) + frame.shape[1:], BF16),
            jax.ShapeDtypeStruct(tab.shape, F32),
        ],
        in_specs=[VMEM] * 3,
        out_specs=[VMEM] * 2,
        compiler_params=PARAMS,
        cost_estimate=SHORT,
        name="border",
    )(frame, oth, tab)


def edge_kernel(
    lo, hi, step, frame, oth, weights, tab, factor, halo, feed_own, feed_oth, pay, tab_next, wide
):
    core = my_core()
    rows = frame.shape[0]
    n = hi - lo
    tab_next[...] = tab[...]
    outer = jnp.where(core == 1, lax.axis_size("space") - 1, 0)
    inside = jnp.where(lax.axis_index("space") == outer, 0.0, 1.0)
    for f, (ref, feed) in enumerate(((frame, feed_own), (oth, feed_oth))):

        def row_of(p):
            depth = lo - 1 + p
            if depth < 0:
                return halo[1 - f, jnp.where(core == 1, -1 - depth, 2 + depth)].astype(F32)
            return ref[jnp.where(core == 1, rows - 1 - depth, depth)].astype(F32)

        def finish(s, count, acc):
            value = (acc * factor[...]).reshape((count,) + feed.shape[1:])
            for r in range(count):
                row = value[r]
                if lo + s + r < 0:
                    row = row * inside
                feed[s + r] = row
                if f == 1:
                    pair = cmul(coefficient(tab, 9), feed_own[s + r]) + cmul(coefficient(tab, 10), row)
                    pay[s + r] = pair.astype(BF16)

        convolve(weights, wide.at[f], row_of, n, step, finish)


def edge_chunk(frame, oth, weights, tab, factor, halo, lo, hi, step):
    rows, w, c = frame.shape
    n = hi - lo
    return pl.pallas_call(
        functools.partial(edge_kernel, lo, hi, step),
        out_shape=[
            jax.ShapeDtypeStruct((n, w, c), F32),
            jax.ShapeDtypeStruct((n, w, c), F32),
            jax.ShapeDtypeStruct((n, w, c), BF16),
            jax.ShapeDtypeStruct(tab.shape, F32),
        ],
        in_specs=[VMEM] * 6,
        out_specs=[VMEM] * 4,
        scratch_shapes=[pltpu.VMEM((2, n + 2, w, 3 * c), BF16)],
        compiler_params=PARAMS,
        cost_estimate=pl.CostEstimate(flops=1, bytes_accessed=1, transcendentals=0),
        name="edge",
    )(frame, oth, weights, tab, factor, halo)


def relay_kernel(slot, tab, pair, got, pay, tab_next):
    tab_next[...] = tab[...]
    cp, cr = coefficient(tab, slot), coefficient(tab, slot + 1)
    for r in range(pair.shape[0]):
        pay[r] = (cmul(cp, pair[r].astype(F32)) + cmul(cr, got[r].astype(F32))).astype(BF16)


def relay(slot, tab, pair, got, hint=SHORT):
    return pl.pallas_call(
        functools.partial(relay_kernel, slot),
        out_shape=[jax.ShapeDtypeStruct(pair.shape, BF16), jax.ShapeDtypeStruct(tab.shape, F32)],
        in_specs=[VMEM] * 3,
        out_specs=[VMEM] * 2,
        compiler_params=PARAMS,
        cost_estimate=hint,
        name="relay",
    )(tab, pair, got)


def output_kernel(lo, hi, begin, end, slot, step, which, seam, closing, n_parts, blocks_at, more, *refs):
    refs = list(refs)
    take = lambda k: [refs.pop(0) for _ in range(k)]
    tab, weights, r1, r2, own, oth, feed_own, feed_oth = take(8)
    kept = take(1)[0] if not seam else None
    near, far = take(2) if closing else (None, None)
    parts = take(n_parts)
    blocks = take(len(blocks_at))
    take(1 if more else 0)
    parcel = take(1)[0] if 0 in which else None
    block = take(1)[0] if 1 in which else None
    result = take(1)[0] if blocks_at else None
    kept_out = take(1)[0] if not closing else None
    near_out, send = take(2) if seam else (None, None)
    tab_next = take(1)[0] if 0 in which else None
    wide = take(1)[0]
    core = my_core()
    first_core = core == 0
    order = [jnp.where(first_core, d, 2 - d) for d in range(3)]
    n, n_out = hi - lo, end - begin
    w, c = own.shape[1:]
    rows = own.shape[0]
    copies = []
    for ref, (depth, mine) in zip(blocks, blocks_at):
        copies.append(start_rows(ref, result, core if mine else 1 - core, depth, refs[0].at[len(copies)]))
    if tab_next is not None:
        tab_next[...] = tab[...]
    lam = coefficient(tab, 8)
    e1, e2 = coefficient(tab, slot + 2), coefficient(tab, slot + 3)
    for part in parts:
        parcel[pl.ds(jnp.where(first_core, n_out, 0), part.shape[0])] = part[...]

    def states(r):
        f_own, f_oth = feed_own[r], feed_oth[r]
        carry = cmul(e1, r1[r].astype(F32)) + cmul(e2, r2[r].astype(F32))
        s0 = cmul(lam, carry) + jnp.where(first_core, f_own, f_oth)
        s1 = cmul(lam, s0) + jnp.where(first_core, f_oth, f_own)
        return jnp.where(first_core, s1, s0), jnp.where(first_core, s0, s1)

    def emit(f, first_wide, size, depth, place, span):
        frame, dst = ((oth, parcel), (own, block))[f]
        mixed = conv_block(wide.at[f], weights, first_wide, size, order).reshape(size, w, c)
        act = 0.5 * mixed * (1.0 + lax.erf(mixed * np.float32(0.5**0.5)))
        for r in range(size):
            row = jnp.where(core == 1, rows - 1 - depth - r, depth + r)
            to = jnp.where(first_core, place + r, span - 1 - place - r) if span else place + r
            dst[to] = (frame[row].astype(F32) + act[r]).astype(BF16)

    if closing:
        top = n_out + 2
        for f in which:
            for k, z in enumerate((near[f, 0], near[f, 1], far[1 - f])):
                wide[f, top + k] = widen(z.astype(F32))
            emit(f, top, 1, rows // 2 - 1, (parcel if f == 0 else block).shape[0] - 1, 0)
    ready = 0
    for s in range(0, n_out, step):
        size = min(step, n_out - s)
        while ready < s + size + 2:
            if ready < n:
                pair = states(ready)
                for f in range(2):
                    if not closing and ready < 2:
                        kept_out[f, ready] = pair[f].astype(BF16)
                    if seam and ready >= n - 2:
                        near_out[f, ready - (n - 2)] = pair[f].astype(BF16)
                    if seam and ready == n - 1:
                        send[f] = pair[f].astype(BF16)
            else:
                pair = [kept[f, ready - n].astype(F32) for f in range(2)]
            for f in which:
                wide[f, ready] = widen(pair[f])
            ready += 1
        for f in which:
            emit(f, s, size, begin + s, s, (parcel if f == 0 else block).shape[0] - (1 if closing else 0))
    for copy in copies:
        copy.wait()


def start_rows(block, result, side, depth, sem):
    n = block.shape[0]
    start = jnp.where(side == 1, result.shape[0] - depth - n, depth)
    copy = pltpu.make_async_copy(block, result.at[pl.ds(start, n)], sem)
    copy.start()
    return copy


def output(
    tab, weights, feeds, arrived, own, oth, lo, hi, begin, end, slot, step, which, kept=None, seam=None, parts=(),
    blocks=(), blocks_at=(), result=None,
):
    rows, w, c = own.shape
    n, n_out = hi - lo, end - begin
    first, closing = kept is None, seam is not None
    args = [tab, weights, *arrived, own, oth, *feeds]
    args += ([] if first else [kept]) + (list(seam) if closing else []) + list(parts) + list(blocks)
    specs = [VMEM] * len(args)
    alias = {}
    shapes, out_specs = [], []
    extra = 1 if closing else 0
    if 0 in which:
        n_parcel = n_out + extra + sum(part.shape[0] for part in parts)
        shapes, out_specs = shapes + [jax.ShapeDtypeStruct((n_parcel, w, c), BF16)], out_specs + [VMEM]
    if 1 in which:
        shapes = shapes + [jax.ShapeDtypeStruct((n_out + extra, w, c), BF16)]
        out_specs = out_specs + [VMEM]
    scratch = [pltpu.VMEM((2, n_out + (5 if closing else 2), w, 3 * c), BF16)]
    if blocks:
        scratch += [pltpu.SemaphoreType.DMA((len(blocks),))]
        if result is not None:
            alias = {len(args): len(shapes)}
            args, specs = args + [result], specs + [HBM]
        shapes, out_specs = shapes + [jax.ShapeDtypeStruct(own.shape, BF16)], out_specs + [HBM]
    if not closing:
        shapes, out_specs = shapes + [jax.ShapeDtypeStruct((2, 2, w, c), BF16)], out_specs + [VMEM]
    if first:
        shapes = shapes + [jax.ShapeDtypeStruct((2, 2, w, c), BF16), jax.ShapeDtypeStruct((2, w, c), BF16)]
        out_specs = out_specs + [VMEM, VMEM]
    if 0 in which:
        shapes, out_specs = shapes + [jax.ShapeDtypeStruct(tab.shape, F32)], out_specs + [VMEM]
    return pl.pallas_call(
        functools.partial(
            output_kernel, lo, hi, begin, end, slot, step, which, first, closing, len(parts), blocks_at, result is not None
        ),
        out_shape=shapes,
        in_specs=specs,
        out_specs=out_specs,
        input_output_aliases=alias,
        scratch_shapes=scratch,
        compiler_params=PARAMS,
        cost_estimate=LONG if first else CLOSING if closing and 0 in which else SHORT,
        name="output",
    )(*args)


def place_kernel(depth, parcel, block, _, result, sem):
    core = my_core()
    inner = result.shape[0] // 2 - 1
    copies = []
    for k, (ref, side) in enumerate(((parcel, 1 - core), (block, core))):
        n = ref.shape[0] - 1
        copies.append(start_rows(ref.at[pl.ds(0, n)], result, side, depth, sem.at[2 * k]))
        copies.append(start_rows(ref.at[pl.ds(n, 1)], result, side, inner, sem.at[2 * k + 1]))
    for copy in copies:
        copy.wait()


def place(parcel, block, depth, result):
    return pl.pallas_call(
        functools.partial(place_kernel, depth),
        out_shape=jax.ShapeDtypeStruct(result.shape, result.dtype),
        in_specs=[VMEM, VMEM, HBM],
        out_specs=HBM,
        input_output_aliases={2: 0},
        scratch_shapes=[pltpu.SemaphoreType.DMA((4,))],
        compiler_params=PARAMS,
        name="place",
    )(parcel, block, result)


ALONG_X = [(0, 1), (1, 0), (2, 3)], [(0, 2), (1, 3)]
ALONG_Y = [(0, 2), (1, 3)], [(0, 1), (2, 3), (3, 2)]


def roles(n):
    if n != 8:
        return [(q, slot, 0) for q in range(n // 2) for slot in (2, 6)]
    along_x = [(0, 0, 2), (0, 1, 0), (1, 0, 0), (1, 1, 2), (1, 2, 0), (2, 3, 0), (3, 2, 0), (3, 3, 2)]
    along_y = [(0, 4, 0), (2, 4, 0), (2, 5, 4), (3, 5, 0), (1, 7, 0), (2, 6, 2), (2, 7, 0), (3, 6, 2), (3, 7, 0)]
    return along_x + along_y


def both_cores(pairs):
    return [(2 * a + k, 2 * b + k) for a, b in pairs for k in range(2)]


def first_stage(n, slot, pair, decay, phase):
    if n == 8:
        return lax.ppermute(pair, "tm", both_cores((ALONG_X if slot == 0 else ALONG_Y)[0]))
    chips, stride, total = n // 2, 1, pair.astype(F32)
    while stride < chips:
        steps = both_cores([(i, i + stride) for i in range(chips - stride)])
        moved = lax.ppermute(total.astype(BF16), "tm", steps).astype(F32)
        size, angle = jnp.exp(-2.0 * stride * decay), 2.0 * stride * phase
        total = total + cmul((size * jnp.cos(angle), size * jnp.sin(angle)), moved)
        stride *= 2
    return lax.ppermute(total.astype(BF16), "tm", both_cores([(i, i + 1) for i in range(chips - 1)]))


def second_stage(n, slot, tab, pair, got, hint=SHORT):
    if n != 8:
        return jnp.zeros_like(got), tab
    pay, tab = relay(slot, tab, pair, got, hint)
    return lax.ppermute(pay, "tm", both_cores((ALONG_X if slot == 0 else ALONG_Y)[1])), tab


def on_device(n, n_space, frames_in, w_input, decay_rate, phase, w_output):
    own = frames_in[0]
    rows, w, c = own.shape
    decay, phase = decay_rate[None], phase[None]
    w_in = w_input.reshape(3, 3 * c, -1)
    w_out = w_output.reshape(3, -1, c)
    swap = [(i, i ^ 1) for i in range(n)]
    step = 3
    oth = lax.ppermute(own, "tm", swap)

    half = rows // 2
    total = half + 1
    last = max(3, total * 5 // 17)
    middle = max(2, total * 5 // 17)
    spans = [(last - 1 + middle, half), (last - 1, last - 1 + middle), (-1, last - 1)]
    links = [
        ((t ^ 1) * n_space + s, t * n_space + s + 1) if t % 2 == 0 else ((t ^ 1) * n_space + s + 1, t * n_space + s)
        for t in range(n)
        for s in range(n_space - 1)
    ]
    (lo1, hi1), (lo2, hi2), (lo3, hi3) = spans
    mine1, mine2, frame, weights, tab, factor = lead(roles(n), own, w_in, decay, phase, lo2, lo1, hi1, step)
    border, tab = outer_rows(frame, oth, tab)
    halo = lax.ppermute(border, ("tm", "space"), links)
    theirs1, pair1, tab = pair_up(oth, weights, tab, factor, mine1, lo1, hi1, step)
    got1 = first_stage(n, 0, pair1, decay, phase)
    theirs2, pair2, tab = pair_up(oth, weights, tab, factor, mine2, lo2, hi2, step)
    got2 = first_stage(n, 4, pair2, decay, phase)
    mine3, theirs3, pair3, tab = edge_chunk(frame, oth, weights, tab, factor, halo, lo3, hi3, step)
    got3 = first_stage(n, 0, pair3, decay, phase)
    also1, tab = second_stage(n, 0, tab, pair1, got1)
    also2, tab = second_stage(n, 4, tab, pair2, got2)
    also3, tab = second_stage(n, 0, tab, pair3, got3, pl.CostEstimate(flops=1, bytes_accessed=1, transcendentals=0))
    args = (w_out, (mine1, theirs1), (got1, also1), frame, oth, lo1, hi1, lo1 + 1, half - 1, 0, 2)
    parcel1, block1, kept, near, send, tab = output(tab, *args, (0, 1))
    far = lax.ppermute(send, "tm", swap)
    args = (w_out, (mine2, theirs2), (got2, also2), frame, oth, lo2, hi2, lo2 + 1, hi2 + 1, 4, 2)
    parcel2, block2, result, kept, tab = output(
        tab, *args, (0, 1), kept=kept, parts=(parcel1,), blocks=(block1,), blocks_at=((lo1 + 1, 1),)
    )
    early = lax.ppermute(parcel2, "tm", swap)
    args = (w_out, (mine3, theirs3), (got3, also3), frame, oth, lo3, hi3, lo3 + 1, hi3 + 1, 0, 2)
    parcel, tab = output(tab, *args, (0,), kept=kept, seam=(near, far))
    block3, result = output(
        tab, *args, (1,), kept=kept, seam=(near, far), blocks=(block2, early), blocks_at=((lo2 + 1, 1), (lo2 + 1, 0)),
        result=result,
    )
    return place(lax.ppermute(parcel, "tm", swap), block3, lo3 + 1, result)[None]


def solution(mesh):
    in_specs = (P("tm", "space", None, None), P(), P(), P(), P())
    out_specs = P("tm", "space", None, None)
    body = functools.partial(on_device, mesh.shape["tm"], mesh.shape["space"])
    return jax.shard_map(body, mesh=mesh, in_specs=in_specs, out_specs=out_specs, check_vma=False)
```

```python
import functools

import numpy as np
import jax
import jax.numpy as jnp
from jax import lax
from jax.experimental import pallas as pl
from jax.experimental.pallas import tpu as pltpu
from jax.sharding import PartitionSpec as P

F32 = jnp.float32
BF16 = jnp.bfloat16
VMEM = pl.BlockSpec(memory_space=pltpu.VMEM)
HBM = pl.BlockSpec(memory_space=pltpu.HBM)
PARAMS = pltpu.CompilerParams(vmem_limit_bytes=24 * 1024 * 1024)
SHORT = pl.CostEstimate(flops=1, bytes_accessed=1, transcendentals=0)
CLOSING = pl.CostEstimate(flops=4000000000, bytes_accessed=1, transcendentals=0)
LONG = pl.CostEstimate(flops=1, bytes_accessed=1, transcendentals=0)
SLOTS = 16


def cmul(coef, z):
    n = z.shape[-1] // 2
    re, im = z[..., :n], z[..., n:]
    cr, ci = coef
    return jnp.concatenate([cr * re - ci * im, cr * im + ci * re], axis=-1)


def coefficient(tab, i):
    return tab[i : i + 1, :], tab[SLOTS + i : SLOTS + i + 1, :]


def widen(row):
    w = row.shape[0]
    col = lax.broadcasted_iota(jnp.int32, row.shape, 0)
    left = jnp.where(col == 0, 0.0, pltpu.roll(row, 1, 0))
    right = jnp.where(col == w - 1, 0.0, pltpu.roll(row, w - 1, 0))
    return jnp.concatenate([left, row, right], axis=-1).astype(BF16)


def conv_block(wide, weights, start, count, order=(0, 1, 2)):
    w, k = wide.shape[1], wide.shape[2]
    lhs = jnp.concatenate(
        [wide[start + d : start + d + count].reshape(count * w, k) for d in range(3)], axis=-1
    )
    rhs = jnp.concatenate([weights[d] for d in order], axis=0)
    return jnp.dot(lhs, rhs, preferred_element_type=F32)


def load_weights(core, hbm, vmem, sem):
    copies = []
    for d in range(3):
        source = jnp.where(core == 1, 2 - d, d)
        copies.append(pltpu.make_async_copy(hbm.at[source], vmem.at[d], sem.at[d]))
        copies[-1].start()
    return copies


def my_core():
    return lax.rem(lax.axis_index("tm"), 2)


def convolve(weights, wide, row_of, n, step, finish):
    ready = 0
    for s in range(0, n, step):
        size = min(step, n - s)
        while ready < s + size + 2:
            wide[ready] = widen(row_of(ready))
            ready += 1
        finish(s, size, conv_block(wide, weights, s, size))


def lead_kernel(
    entries, lo, mid, hi, step, own, w_hbm, decay, phase, feed, feed_next, frame, weights, tab, factor, wide, dvec, sem
):
    core, chip = my_core(), lax.div(lax.axis_index("tm"), 2)
    rows = own.shape[0]
    n = hi - lo
    vectors = [pltpu.make_async_copy(ref, dvec.at[pl.ds(k, 1)], sem.at[3 + k]) for k, ref in enumerate((decay, phase))]
    for copy in vectors:
        copy.start()
    source = jnp.where(core == 1, rows - 1 - hi, lo - 1)
    near = pltpu.make_async_copy(own.at[pl.ds(source, n + 2)], frame.at[pl.ds(source, n + 2)], sem.at[5])
    near.start()
    wcopies = load_weights(core, w_hbm, weights, sem)
    for copy in vectors:
        copy.wait()
    expo, gate = [jnp.float32(0.0)] * SLOTS, [jnp.float32(0.0)] * SLOTS
    for q, slot, power in entries:
        expo[slot] = jnp.where(chip == q, jnp.float32(power), expo[slot])
        gate[slot] = jnp.where(chip == q, jnp.float32(1.0), gate[slot])
    for slot, power in ((8, 1), (9, 1 - core), (10, core)):
        expo[slot], gate[slot] = jnp.asarray(power).astype(F32), jnp.float32(1.0)
    spread = lambda values: jnp.concatenate([jnp.full((1, dvec.shape[1]), v, F32) for v in values], axis=0)
    expo = spread(expo)
    size = spread(gate) * jnp.exp(-expo * dvec[0:1])
    angle = expo * dvec[1:2]
    tab[...] = jnp.concatenate([size * jnp.cos(angle), size * jnp.sin(angle)], axis=0)
    mag = jnp.exp(-dvec[0:1])
    scale = jnp.sqrt(1.0 - mag * mag)
    factor[...] = jnp.concatenate([scale, scale], axis=-1)
    for copy in (*wcopies, near):
        copy.wait()
    rest = []
    for k, (begin, end) in enumerate(((0, lo - 1), (hi + 1, rows))):
        at = jnp.where(core == 1, rows - end, begin)
        rest.append(
            pltpu.make_async_copy(own.at[pl.ds(at, end - begin)], frame.at[pl.ds(at, end - begin)], sem.at[6 + k])
        )
        rest[-1].start()

    def row_of(p):
        return frame[source + jnp.where(core == 1, n + 1 - p, p)].astype(F32)

    def finish(s, count, acc):
        value = (acc * factor[...]).reshape((count,) + feed.shape[1:])
        for r in range(count):
            depth = lo + s + r
            if depth < mid:
                feed_next[depth - lo] = value[r]
            else:
                feed[depth - mid] = value[r]

    convolve(weights, wide, row_of, n, step, finish)
    for copy in rest:
        copy.wait()


def lead(entries, own, w_in, decay, phase, lo, mid, hi, step):
    rows, w, c = own.shape
    n = hi - lo
    return pl.pallas_call(
        functools.partial(lead_kernel, entries, lo, mid, hi, step),
        out_shape=[
            jax.ShapeDtypeStruct((hi - mid, w, c), F32),
            jax.ShapeDtypeStruct((mid - lo, w, c), F32),
            jax.ShapeDtypeStruct(own.shape, BF16),
            jax.ShapeDtypeStruct(w_in.shape, BF16),
            jax.ShapeDtypeStruct((2 * SLOTS, decay.shape[1]), F32),
            jax.ShapeDtypeStruct((1, 2 * decay.shape[1]), F32),
        ],
        in_specs=[HBM] * 4,
        out_specs=[VMEM] * 6,
        scratch_shapes=[
            pltpu.VMEM((n + 2, w, 3 * c), BF16),
            pltpu.VMEM((2, decay.shape[1]), F32),
            pltpu.SemaphoreType.DMA((8,)),
        ],
        compiler_params=PARAMS,
        cost_estimate=SHORT,
        name="lead",
    )(*(pltpu.with_memory_space_constraint(x, pltpu.HBM) for x in (own, w_in, decay, phase)))


def pair_kernel(lo, hi, step, oth, weights, tab, factor, feed_own, feed, pay, tab_next, wide):
    core = my_core()
    rows = oth.shape[0]
    n = hi - lo
    tab_next[...] = tab[...]
    source = jnp.where(core == 1, rows - 1 - hi, lo - 1)

    def row_of(p):
        return oth[source + jnp.where(core == 1, n + 1 - p, p)].astype(F32)

    def finish(s, count, acc):
        value = (acc * factor[...]).reshape((count,) + feed.shape[1:])
        feed[s : s + count] = value
        for r in range(count):
            pair = cmul(coefficient(tab, 9), feed_own[s + r]) + cmul(coefficient(tab, 10), value[r])
            pay[s + r] = pair.astype(BF16)

    convolve(weights, wide, row_of, n, step, finish)


def pair_up(oth, weights, tab, factor, feed_own, lo, hi, step):
    rows, w, c = oth.shape
    n = hi - lo
    return pl.pallas_call(
        functools.partial(pair_kernel, lo, hi, step),
        out_shape=[
            jax.ShapeDtypeStruct((n, w, c), F32),
            jax.ShapeDtypeStruct((n, w, c), BF16),
            jax.ShapeDtypeStruct(tab.shape, F32),
        ],
        in_specs=[VMEM] * 5,
        out_specs=[VMEM] * 3,
        scratch_shapes=[pltpu.VMEM((n + 2, w, 3 * c), BF16)],
        compiler_params=PARAMS,
        cost_estimate=SHORT,
        name="pair",
    )(oth, weights, tab, factor, feed_own)


def border_kernel(frame, oth, tab, border, tab_next):
    tab_next[...] = tab[...]
    at = my_core() * (frame.shape[0] - 2)
    for f, ref in enumerate((frame, oth)):
        for r in range(2):
            border[f, r] = ref[at + r]


def outer_rows(frame, oth, tab):
    return pl.pallas_call(
        border_kernel,
        out_shape=[
            jax.ShapeDtypeStruct((2, 2) + frame.shape[1:], BF16),
            jax.ShapeDtypeStruct(tab.shape, F32),
        ],
        in_specs=[VMEM] * 3,
        out_specs=[VMEM] * 2,
        compiler_params=PARAMS,
        cost_estimate=SHORT,
        name="border",
    )(frame, oth, tab)


def edge_kernel(
    lo, hi, step, frame, oth, weights, tab, factor, halo, feed_own, feed_oth, pay, tab_next, wide
):
    core = my_core()
    rows = frame.shape[0]
    n = hi - lo
    tab_next[...] = tab[...]
    outer = jnp.where(core == 1, lax.axis_size("space") - 1, 0)
    inside = jnp.where(lax.axis_index("space") == outer, 0.0, 1.0)
    for f, (ref, feed) in enumerate(((frame, feed_own), (oth, feed_oth))):

        def row_of(p):
            depth = lo - 1 + p
            if depth < 0:
                return halo[1 - f, jnp.where(core == 1, -1 - depth, 2 + depth)].astype(F32)
            return ref[jnp.where(core == 1, rows - 1 - depth, depth)].astype(F32)

        def finish(s, count, acc):
            value = (acc * factor[...]).reshape((count,) + feed.shape[1:])
            for r in range(count):
                row = value[r]
                if lo + s + r < 0:
                    row = row * inside
                feed[s + r] = row
                if f == 1:
                    pair = cmul(coefficient(tab, 9), feed_own[s + r]) + cmul(coefficient(tab, 10), row)
                    pay[s + r] = pair.astype(BF16)

        convolve(weights, wide.at[f], row_of, n, step, finish)


def edge_chunk(frame, oth, weights, tab, factor, halo, lo, hi, step):
    rows, w, c = frame.shape
    n = hi - lo
    return pl.pallas_call(
        functools.partial(edge_kernel, lo, hi, step),
        out_shape=[
            jax.ShapeDtypeStruct((n, w, c), F32),
            jax.ShapeDtypeStruct((n, w, c), F32),
            jax.ShapeDtypeStruct((n, w, c), BF16),
            jax.ShapeDtypeStruct(tab.shape, F32),
        ],
        in_specs=[VMEM] * 6,
        out_specs=[VMEM] * 4,
        scratch_shapes=[pltpu.VMEM((2, n + 2, w, 3 * c), BF16)],
        compiler_params=PARAMS,
        cost_estimate=pl.CostEstimate(flops=1, bytes_accessed=1, transcendentals=0),
        name="edge",
    )(frame, oth, weights, tab, factor, halo)


def relay_kernel(slot, tab, pair, got, pay, tab_next):
    tab_next[...] = tab[...]
    cp, cr = coefficient(tab, slot), coefficient(tab, slot + 1)
    for r in range(pair.shape[0]):
        pay[r] = (cmul(cp, pair[r].astype(F32)) + cmul(cr, got[r].astype(F32))).astype(BF16)


def relay(slot, tab, pair, got, hint=SHORT):
    return pl.pallas_call(
        functools.partial(relay_kernel, slot),
        out_shape=[jax.ShapeDtypeStruct(pair.shape, BF16), jax.ShapeDtypeStruct(tab.shape, F32)],
        in_specs=[VMEM] * 3,
        out_specs=[VMEM] * 2,
        compiler_params=PARAMS,
        cost_estimate=hint,
        name="relay",
    )(tab, pair, got)


def output_kernel(lo, hi, begin, end, slot, step, which, seam, closing, n_parts, blocks_at, more, *refs):
    refs = list(refs)
    take = lambda k: [refs.pop(0) for _ in range(k)]
    tab, weights, r1, r2, own, oth, feed_own, feed_oth = take(8)
    kept = take(1)[0] if not seam else None
    rim = take(1)[0] if closing else None
    parts = take(n_parts)
    blocks = take(len(blocks_at))
    take(1 if more else 0)
    parcel = take(1)[0] if 0 in which else None
    block = take(1)[0] if 1 in which else None
    result = take(1)[0] if blocks_at else None
    kept_out = take(1)[0] if not closing else None
    near_out, send = take(2) if seam else (None, None)
    tab_next = take(1)[0] if 0 in which else None
    wide = take(1)[0]
    core = my_core()
    first_core = core == 0
    order = [jnp.where(first_core, d, 2 - d) for d in range(3)]
    n, n_out = hi - lo, end - begin
    w, c = own.shape[1:]
    rows = own.shape[0]
    copies = []
    for ref, (depth, mine) in zip(blocks, blocks_at):
        copies.append(start_rows(ref, result, core if mine else 1 - core, depth, refs[0].at[len(copies)]))
    if tab_next is not None:
        tab_next[...] = tab[...]
    lam = coefficient(tab, 8)
    e1, e2 = coefficient(tab, slot + 2), coefficient(tab, slot + 3)
    for part in parts:
        parcel[pl.ds(jnp.where(first_core, n_out, 0), part.shape[0])] = part[...]

    def states(r):
        f_own, f_oth = feed_own[r], feed_oth[r]
        carry = cmul(e1, r1[r].astype(F32)) + cmul(e2, r2[r].astype(F32))
        s0 = cmul(lam, carry) + jnp.where(first_core, f_own, f_oth)
        s1 = cmul(lam, s0) + jnp.where(first_core, f_oth, f_own)
        return jnp.where(first_core, s1, s0), jnp.where(first_core, s0, s1)

    def emit(f, first_wide, size, depth, span):
        frame, dst = ((oth, parcel), (own, block))[f]
        mixed = conv_block(wide.at[f], weights, first_wide, size, order).reshape(size, w, c)
        act = 0.5 * mixed * (1.0 + lax.erf(mixed * np.float32(0.5**0.5)))
        for r in range(size):
            row = jnp.where(core == 1, rows - 1 - depth - r, depth + r)
            to = jnp.where(first_core, first_wide + r, span - 1 - first_wide - r)
            dst[to] = (frame[row].astype(F32) + act[r]).astype(BF16)

    if closing and 0 in which:
        parcel[parcel.shape[0] - 1] = rim[0]
    ready = 0
    for s in range(0, n_out, step):
        size = min(step, n_out - s)
        while ready < s + size + 2:
            if ready < n:
                pair = states(ready)
                for f in range(2):
                    if not closing and ready < 2:
                        kept_out[f, ready] = pair[f].astype(BF16)
                    if seam and ready >= n - 2:
                        near_out[f, ready - (n - 2)] = pair[f].astype(BF16)
                    if seam and ready == n - 1:
                        send[f] = pair[f].astype(BF16)
            else:
                pair = [kept[f, ready - n].astype(F32) for f in range(2)]
            for f in which:
                wide[f, ready] = widen(pair[f])
            ready += 1
        for f in which:
            emit(f, s, size, begin + s, parcel.shape[0] - (1 if closing else 0) if f == 0 else n_out)
    for copy in copies:
        copy.wait()


def start_rows(block, result, side, depth, sem):
    n = block.shape[0]
    start = jnp.where(side == 1, result.shape[0] - depth - n, depth)
    copy = pltpu.make_async_copy(block, result.at[pl.ds(start, n)], sem)
    copy.start()
    return copy


def output(
    tab, weights, feeds, arrived, own, oth, lo, hi, begin, end, slot, step, which, kept=None, seam=None, parts=(),
    blocks=(), blocks_at=(), result=None,
):
    rows, w, c = own.shape
    n, n_out = hi - lo, end - begin
    first, closing = kept is None, seam is not None
    args = [tab, weights, *arrived, own, oth, *feeds]
    args += ([] if first else [kept]) + (list(seam) if closing else []) + list(parts) + list(blocks)
    specs = [VMEM] * len(args)
    alias = {}
    shapes, out_specs = [], []
    extra = 1 if closing else 0
    if 0 in which:
        n_parcel = n_out + extra + sum(part.shape[0] for part in parts)
        shapes, out_specs = shapes + [jax.ShapeDtypeStruct((n_parcel, w, c), BF16)], out_specs + [VMEM]
    if 1 in which:
        shapes = shapes + [jax.ShapeDtypeStruct((n_out, w, c), BF16)]
        out_specs = out_specs + [VMEM]
    scratch = [pltpu.VMEM((2, n_out + 2, w, 3 * c), BF16)]
    if blocks:
        scratch += [pltpu.SemaphoreType.DMA((len(blocks),))]
        if result is not None:
            alias = {len(args): len(shapes)}
            args, specs = args + [result], specs + [HBM]
        shapes, out_specs = shapes + [jax.ShapeDtypeStruct(own.shape, BF16)], out_specs + [HBM]
    if not closing:
        shapes, out_specs = shapes + [jax.ShapeDtypeStruct((2, 2, w, c), BF16)], out_specs + [VMEM]
    if first:
        shapes = shapes + [jax.ShapeDtypeStruct((2, 2, w, c), BF16), jax.ShapeDtypeStruct((2, w, c), BF16)]
        out_specs = out_specs + [VMEM, VMEM]
    if 0 in which:
        shapes, out_specs = shapes + [jax.ShapeDtypeStruct(tab.shape, F32)], out_specs + [VMEM]
    return pl.pallas_call(
        functools.partial(
            output_kernel, lo, hi, begin, end, slot, step, which, first, closing, len(parts), blocks_at, result is not None
        ),
        out_shape=shapes,
        in_specs=specs,
        out_specs=out_specs,
        input_output_aliases=alias,
        scratch_shapes=scratch,
        compiler_params=PARAMS,
        cost_estimate=LONG if first else CLOSING if closing and 0 in which else SHORT,
        name="output",
    )(*args)


def rim_kernel(tab, weights, near, far, own, oth, rim, tab_next, wide):
    core = my_core()
    order = [jnp.where(core == 0, d, 2 - d) for d in range(3)]
    tab_next[...] = tab[...]
    depth = own.shape[0] // 2 - 1
    row = jnp.where(core == 1, own.shape[0] - 1 - depth, depth)
    for f, frame in enumerate((oth, own)):
        for k, z in enumerate((near[f, 0], near[f, 1], far[1 - f])):
            wide[f, k] = widen(z.astype(F32))
        mixed = conv_block(wide.at[f], weights, 0, 1, order)
        act = 0.5 * mixed * (1.0 + lax.erf(mixed * np.float32(0.5**0.5)))
        rim[f] = (frame[row].astype(F32) + act).astype(BF16)


def rim_rows(tab, weights, near, far, own, oth):
    w, c = own.shape[1:]
    return pl.pallas_call(
        rim_kernel,
        out_shape=[jax.ShapeDtypeStruct((2, w, c), BF16), jax.ShapeDtypeStruct(tab.shape, F32)],
        in_specs=[VMEM] * 6,
        out_specs=[VMEM] * 2,
        scratch_shapes=[pltpu.VMEM((2, 3, w, 3 * c), BF16)],
        compiler_params=PARAMS,
        cost_estimate=SHORT,
        name="rim",
    )(tab, weights, near, far, own, oth)


def place_kernel(depth, parcel, block, rim, _, result, sem):
    core = my_core()
    inner = result.shape[0] // 2 - 1
    n = parcel.shape[0] - 1
    copies = [
        start_rows(parcel.at[pl.ds(0, n)], result, 1 - core, depth, sem.at[0]),
        start_rows(parcel.at[pl.ds(n, 1)], result, 1 - core, inner, sem.at[1]),
        start_rows(block, result, core, depth, sem.at[2]),
        start_rows(rim.at[pl.ds(1, 1)], result, core, inner, sem.at[3]),
    ]
    for copy in copies:
        copy.wait()


def place(parcel, block, rim, depth, result):
    return pl.pallas_call(
        functools.partial(place_kernel, depth),
        out_shape=jax.ShapeDtypeStruct(result.shape, result.dtype),
        in_specs=[VMEM, VMEM, VMEM, HBM],
        out_specs=HBM,
        input_output_aliases={3: 0},
        scratch_shapes=[pltpu.SemaphoreType.DMA((4,))],
        compiler_params=PARAMS,
        name="place",
    )(parcel, block, rim, result)


ALONG_X = [(0, 1), (1, 0), (2, 3)], [(0, 2), (1, 3)]
ALONG_Y = [(0, 2), (1, 3)], [(0, 1), (2, 3), (3, 2)]


def roles(n):
    if n != 8:
        return [(q, slot, 0) for q in range(n // 2) for slot in (2, 6)]
    along_x = [(0, 0, 2), (0, 1, 0), (1, 0, 0), (1, 1, 2), (1, 2, 0), (2, 3, 0), (3, 2, 0), (3, 3, 2)]
    along_y = [(0, 4, 0), (2, 4, 0), (2, 5, 4), (3, 5, 0), (1, 7, 0), (2, 6, 2), (2, 7, 0), (3, 6, 2), (3, 7, 0)]
    return along_x + along_y


def both_cores(pairs):
    return [(2 * a + k, 2 * b + k) for a, b in pairs for k in range(2)]


def first_stage(n, slot, pair, decay, phase):
    if n == 8:
        return lax.ppermute(pair, "tm", both_cores((ALONG_X if slot == 0 else ALONG_Y)[0]))
    chips, stride, total = n // 2, 1, pair.astype(F32)
    while stride < chips:
        steps = both_cores([(i, i + stride) for i in range(chips - stride)])
        moved = lax.ppermute(total.astype(BF16), "tm", steps).astype(F32)
        size, angle = jnp.exp(-2.0 * stride * decay), 2.0 * stride * phase
        total = total + cmul((size * jnp.cos(angle), size * jnp.sin(angle)), moved)
        stride *= 2
    return lax.ppermute(total.astype(BF16), "tm", both_cores([(i, i + 1) for i in range(chips - 1)]))


def second_stage(n, slot, tab, pair, got, hint=SHORT):
    if n != 8:
        return jnp.zeros_like(got), tab
    pay, tab = relay(slot, tab, pair, got, hint)
    return lax.ppermute(pay, "tm", both_cores((ALONG_X if slot == 0 else ALONG_Y)[1])), tab


def on_device(n, n_space, frames_in, w_input, decay_rate, phase, w_output):
    own = frames_in[0]
    rows, w, c = own.shape
    decay, phase = decay_rate[None], phase[None]
    w_in = w_input.reshape(3, 3 * c, -1)
    w_out = w_output.reshape(3, -1, c)
    swap = [(i, i ^ 1) for i in range(n)]
    step = 3
    oth = lax.ppermute(own, "tm", swap)

    half = rows // 2
    total = half + 1
    last = max(3, total * 5 // 17)
    middle = max(2, total * 5 // 17)
    spans = [(last - 1 + middle, half), (last - 1, last - 1 + middle), (-1, last - 1)]
    links = [
        ((t ^ 1) * n_space + s, t * n_space + s + 1) if t % 2 == 0 else ((t ^ 1) * n_space + s + 1, t * n_space + s)
        for t in range(n)
        for s in range(n_space - 1)
    ]
    (lo1, hi1), (lo2, hi2), (lo3, hi3) = spans
    mine1, mine2, frame, weights, tab, factor = lead(roles(n), own, w_in, decay, phase, lo2, lo1, hi1, step)
    border, tab = outer_rows(frame, oth, tab)
    halo = lax.ppermute(border, ("tm", "space"), links)
    theirs1, pair1, tab = pair_up(oth, weights, tab, factor, mine1, lo1, hi1, step)
    got1 = first_stage(n, 0, pair1, decay, phase)
    theirs2, pair2, tab = pair_up(oth, weights, tab, factor, mine2, lo2, hi2, step)
    got2 = first_stage(n, 4, pair2, decay, phase)
    mine3, theirs3, pair3, tab = edge_chunk(frame, oth, weights, tab, factor, halo, lo3, hi3, step)
    got3 = first_stage(n, 0, pair3, decay, phase)
    also1, tab = second_stage(n, 0, tab, pair1, got1)
    also2, tab = second_stage(n, 4, tab, pair2, got2)
    also3, tab = second_stage(n, 0, tab, pair3, got3, pl.CostEstimate(flops=1, bytes_accessed=1, transcendentals=0))
    args = (w_out, (mine1, theirs1), (got1, also1), frame, oth, lo1, hi1, lo1 + 1, half - 1, 0, 2)
    parcel1, block1, kept, near, send, tab = output(tab, *args, (0, 1))
    far = lax.ppermute(send, "tm", swap)
    args = (w_out, (mine2, theirs2), (got2, also2), frame, oth, lo2, hi2, lo2 + 1, hi2 + 1, 4, 2)
    parcel2, block2, result, kept, tab = output(
        tab, *args, (0, 1), kept=kept, parts=(parcel1,), blocks=(block1,), blocks_at=((lo1 + 1, 1),)
    )
    early = lax.ppermute(parcel2, "tm", swap)
    rim, tab = rim_rows(tab, w_out, near, far, frame, oth)
    args = (w_out, (mine3, theirs3), (got3, also3), frame, oth, lo3, hi3, lo3 + 1, hi3 + 1, 0, 2)
    parcel, tab = output(tab, *args, (0,), kept=kept, seam=(rim,))
    block3, result = output(
        tab, *args, (1,), kept=kept, seam=(rim,), blocks=(block2, early), blocks_at=((lo2 + 1, 1), (lo2 + 1, 0)),
        result=result,
    )
    return place(lax.ppermute(parcel, "tm", swap), block3, rim, lo3 + 1, result)[None]


def solution(mesh):
    in_specs = (P("tm", "space", None, None), P(), P(), P(), P())
    out_specs = P("tm", "space", None, None)
    body = functools.partial(on_device, mesh.shape["tm"], mesh.shape["space"])
    return jax.shard_map(body, mesh=mesh, in_specs=in_specs, out_specs=out_specs, check_vma=False)
```

```python
import functools

import numpy as np
import jax
import jax.numpy as jnp
from jax import lax
from jax.experimental import pallas as pl
from jax.experimental.pallas import tpu as pltpu
from jax.sharding import PartitionSpec as P

F32 = jnp.float32
BF16 = jnp.bfloat16
VMEM = pl.BlockSpec(memory_space=pltpu.VMEM)
HBM = pl.BlockSpec(memory_space=pltpu.HBM)
PARAMS = pltpu.CompilerParams(vmem_limit_bytes=24 * 1024 * 1024)
SHORT = pl.CostEstimate(flops=1, bytes_accessed=1, transcendentals=0)
CLOSING = pl.CostEstimate(flops=4000000000, bytes_accessed=1, transcendentals=0)
LONG = pl.CostEstimate(flops=1, bytes_accessed=1, transcendentals=0)
SLOTS = 16


def cmul(coef, z):
    n = z.shape[-1] // 2
    re, im = z[..., :n], z[..., n:]
    cr, ci = coef
    return jnp.concatenate([cr * re - ci * im, cr * im + ci * re], axis=-1)


def coefficient(tab, i):
    return tab[i : i + 1, :], tab[SLOTS + i : SLOTS + i + 1, :]


def widen(row):
    w = row.shape[0]
    col = lax.broadcasted_iota(jnp.int32, row.shape, 0)
    left = jnp.where(col == 0, 0.0, pltpu.roll(row, 1, 0))
    right = jnp.where(col == w - 1, 0.0, pltpu.roll(row, w - 1, 0))
    return jnp.concatenate([left, row, right], axis=-1).astype(BF16)


def conv_block(wide, weights, start, count, order=(0, 1, 2)):
    w, k = wide.shape[1], wide.shape[2]
    lhs = jnp.concatenate(
        [wide[start + d : start + d + count].reshape(count * w, k) for d in range(3)], axis=-1
    )
    rhs = jnp.concatenate([weights[d] for d in order], axis=0)
    return jnp.dot(lhs, rhs, preferred_element_type=F32)


def load_weights(core, hbm, vmem, sem):
    copies = []
    for d in range(3):
        source = jnp.where(core == 1, 2 - d, d)
        copies.append(pltpu.make_async_copy(hbm.at[source], vmem.at[d], sem.at[d]))
        copies[-1].start()
    return copies


def my_core():
    return lax.rem(lax.axis_index("tm"), 2)


def convolve(weights, wide, row_of, n, step, finish):
    ready = 0
    for s in range(0, n, step):
        size = min(step, n - s)
        while ready < s + size + 2:
            wide[ready] = widen(row_of(ready))
            ready += 1
        finish(s, size, conv_block(wide, weights, s, size))


def lead_kernel(
    entries, lo, mid, hi, step, own, w_hbm, decay, phase, feed, feed_next, frame, weights, tab, factor, wide, dvec, sem
):
    core, chip = my_core(), lax.div(lax.axis_index("tm"), 2)
    rows = own.shape[0]
    n = hi - lo
    vectors = [pltpu.make_async_copy(ref, dvec.at[pl.ds(k, 1)], sem.at[3 + k]) for k, ref in enumerate((decay, phase))]
    for copy in vectors:
        copy.start()
    source = jnp.where(core == 1, rows - 1 - hi, lo - 1)
    near = pltpu.make_async_copy(own.at[pl.ds(source, n + 2)], frame.at[pl.ds(source, n + 2)], sem.at[5])
    near.start()
    wcopies = load_weights(core, w_hbm, weights, sem)
    for copy in vectors:
        copy.wait()
    expo, gate = [jnp.float32(0.0)] * SLOTS, [jnp.float32(0.0)] * SLOTS
    for q, slot, power in entries:
        expo[slot] = jnp.where(chip == q, jnp.float32(power), expo[slot])
        gate[slot] = jnp.where(chip == q, jnp.float32(1.0), gate[slot])
    for slot, power in ((8, 1), (9, 1 - core), (10, core)):
        expo[slot], gate[slot] = jnp.asarray(power).astype(F32), jnp.float32(1.0)
    spread = lambda values: jnp.concatenate([jnp.full((1, dvec.shape[1]), v, F32) for v in values], axis=0)
    expo = spread(expo)
    size = spread(gate) * jnp.exp(-expo * dvec[0:1])
    angle = expo * dvec[1:2]
    tab[...] = jnp.concatenate([size * jnp.cos(angle), size * jnp.sin(angle)], axis=0)
    mag = jnp.exp(-dvec[0:1])
    scale = jnp.sqrt(1.0 - mag * mag)
    factor[...] = jnp.concatenate([scale, scale], axis=-1)
    for copy in (*wcopies, near):
        copy.wait()
    rest = []
    for k, (begin, end) in enumerate(((0, lo - 1), (hi + 1, rows))):
        at = jnp.where(core == 1, rows - end, begin)
        rest.append(
            pltpu.make_async_copy(own.at[pl.ds(at, end - begin)], frame.at[pl.ds(at, end - begin)], sem.at[6 + k])
        )
        rest[-1].start()

    def row_of(p):
        return frame[source + jnp.where(core == 1, n + 1 - p, p)].astype(F32)

    def finish(s, count, acc):
        value = (acc * factor[...]).reshape((count,) + feed.shape[1:])
        for r in range(count):
            depth = lo + s + r
            if depth < mid:
                feed_next[depth - lo] = value[r]
            else:
                feed[depth - mid] = value[r]

    convolve(weights, wide, row_of, n, step, finish)
    for copy in rest:
        copy.wait()


def lead(entries, own, w_in, decay, phase, lo, mid, hi, step):
    rows, w, c = own.shape
    n = hi - lo
    return pl.pallas_call(
        functools.partial(lead_kernel, entries, lo, mid, hi, step),
        out_shape=[
            jax.ShapeDtypeStruct((hi - mid, w, c), F32),
            jax.ShapeDtypeStruct((mid - lo, w, c), F32),
            jax.ShapeDtypeStruct(own.shape, BF16),
            jax.ShapeDtypeStruct(w_in.shape, BF16),
            jax.ShapeDtypeStruct((2 * SLOTS, decay.shape[1]), F32),
            jax.ShapeDtypeStruct((1, 2 * decay.shape[1]), F32),
        ],
        in_specs=[HBM] * 4,
        out_specs=[VMEM] * 6,
        scratch_shapes=[
            pltpu.VMEM((n + 2, w, 3 * c), BF16),
            pltpu.VMEM((2, decay.shape[1]), F32),
            pltpu.SemaphoreType.DMA((8,)),
        ],
        compiler_params=PARAMS,
        cost_estimate=SHORT,
        name="lead",
    )(*(pltpu.with_memory_space_constraint(x, pltpu.HBM) for x in (own, w_in, decay, phase)))


def pair_kernel(lo, hi, step, oth, weights, tab, factor, feed_own, feed, pay, tab_next, wide):
    core = my_core()
    rows = oth.shape[0]
    n = hi - lo
    tab_next[...] = tab[...]
    source = jnp.where(core == 1, rows - 1 - hi, lo - 1)

    def row_of(p):
        return oth[source + jnp.where(core == 1, n + 1 - p, p)].astype(F32)

    def finish(s, count, acc):
        value = (acc * factor[...]).reshape((count,) + feed.shape[1:])
        feed[s : s + count] = value
        for r in range(count):
            pair = cmul(coefficient(tab, 9), feed_own[s + r]) + cmul(coefficient(tab, 10), value[r])
            pay[s + r] = pair.astype(BF16)

    convolve(weights, wide, row_of, n, step, finish)


def pair_up(oth, weights, tab, factor, feed_own, lo, hi, step):
    rows, w, c = oth.shape
    n = hi - lo
    return pl.pallas_call(
        functools.partial(pair_kernel, lo, hi, step),
        out_shape=[
            jax.ShapeDtypeStruct((n, w, c), F32),
            jax.ShapeDtypeStruct((n, w, c), BF16),
            jax.ShapeDtypeStruct(tab.shape, F32),
        ],
        in_specs=[VMEM] * 5,
        out_specs=[VMEM] * 3,
        scratch_shapes=[pltpu.VMEM((n + 2, w, 3 * c), BF16)],
        compiler_params=PARAMS,
        cost_estimate=SHORT,
        name="pair",
    )(oth, weights, tab, factor, feed_own)


def border_kernel(frame, oth, tab, border, tab_next):
    tab_next[...] = tab[...]
    at = my_core() * (frame.shape[0] - 2)
    for f, ref in enumerate((frame, oth)):
        for r in range(2):
            border[f, r] = ref[at + r]


def outer_rows(frame, oth, tab):
    return pl.pallas_call(
        border_kernel,
        out_shape=[
            jax.ShapeDtypeStruct((2, 2) + frame.shape[1:], BF16),
            jax.ShapeDtypeStruct(tab.shape, F32),
        ],
        in_specs=[VMEM] * 3,
        out_specs=[VMEM] * 2,
        compiler_params=PARAMS,
        cost_estimate=SHORT,
        name="border",
    )(frame, oth, tab)


def edge_kernel(
    lo, hi, step, frame, oth, weights, tab, factor, halo, feed_own, feed_oth, pay, tab_next, wide
):
    core = my_core()
    rows = frame.shape[0]
    n = hi - lo
    tab_next[...] = tab[...]
    outer = jnp.where(core == 1, lax.axis_size("space") - 1, 0)
    inside = jnp.where(lax.axis_index("space") == outer, 0.0, 1.0)
    for f, (ref, feed) in enumerate(((frame, feed_own), (oth, feed_oth))):

        def row_of(p):
            depth = lo - 1 + p
            if depth < 0:
                return halo[1 - f, jnp.where(core == 1, -1 - depth, 2 + depth)].astype(F32)
            return ref[jnp.where(core == 1, rows - 1 - depth, depth)].astype(F32)

        def finish(s, count, acc):
            value = (acc * factor[...]).reshape((count,) + feed.shape[1:])
            for r in range(count):
                row = value[r]
                if lo + s + r < 0:
                    row = row * inside
                feed[s + r] = row
                if f == 1:
                    pair = cmul(coefficient(tab, 9), feed_own[s + r]) + cmul(coefficient(tab, 10), row)
                    pay[s + r] = pair.astype(BF16)

        convolve(weights, wide.at[f], row_of, n, step, finish)


def edge_chunk(frame, oth, weights, tab, factor, halo, lo, hi, step):
    rows, w, c = frame.shape
    n = hi - lo
    return pl.pallas_call(
        functools.partial(edge_kernel, lo, hi, step),
        out_shape=[
            jax.ShapeDtypeStruct((n, w, c), F32),
            jax.ShapeDtypeStruct((n, w, c), F32),
            jax.ShapeDtypeStruct((n, w, c), BF16),
            jax.ShapeDtypeStruct(tab.shape, F32),
        ],
        in_specs=[VMEM] * 6,
        out_specs=[VMEM] * 4,
        scratch_shapes=[pltpu.VMEM((2, n + 2, w, 3 * c), BF16)],
        compiler_params=PARAMS,
        cost_estimate=pl.CostEstimate(flops=1, bytes_accessed=1, transcendentals=0),
        name="edge",
    )(frame, oth, weights, tab, factor, halo)


def relay_kernel(slot, tab, pair, got, pay, tab_next):
    tab_next[...] = tab[...]
    cp, cr = coefficient(tab, slot), coefficient(tab, slot + 1)
    for r in range(pair.shape[0]):
        pay[r] = (cmul(cp, pair[r].astype(F32)) + cmul(cr, got[r].astype(F32))).astype(BF16)


def relay(slot, tab, pair, got, hint=SHORT):
    return pl.pallas_call(
        functools.partial(relay_kernel, slot),
        out_shape=[jax.ShapeDtypeStruct(pair.shape, BF16), jax.ShapeDtypeStruct(tab.shape, F32)],
        in_specs=[VMEM] * 3,
        out_specs=[VMEM] * 2,
        compiler_params=PARAMS,
        cost_estimate=hint,
        name="relay",
    )(tab, pair, got)


def output_kernel(lo, hi, begin, end, slot, step, which, seam, closing, n_parts, blocks_at, more, *refs):
    refs = list(refs)
    take = lambda k: [refs.pop(0) for _ in range(k)]
    tab, weights, r1, r2, own, oth, feed_own, feed_oth = take(8)
    kept = take(1)[0] if not seam else None
    rim = take(1)[0] if closing else None
    parts = take(n_parts)
    blocks = take(len(blocks_at))
    take(1 if more else 0)
    parcel = take(1)[0] if 0 in which else None
    block = take(1)[0] if 1 in which else None
    result = take(1)[0] if blocks_at else None
    kept_out = take(1)[0] if not closing else None
    near_out, send = take(2) if seam else (None, None)
    tab_next = take(1)[0] if 0 in which else None
    wide = take(1)[0]
    core = my_core()
    first_core = core == 0
    order = [jnp.where(first_core, d, 2 - d) for d in range(3)]
    n, n_out = hi - lo, end - begin
    w, c = own.shape[1:]
    rows = own.shape[0]
    copies = []
    for ref, (depth, mine) in zip(blocks, blocks_at):
        copies.append(start_rows(ref, result, core if mine else 1 - core, depth, refs[0].at[len(copies)]))
    if tab_next is not None:
        tab_next[...] = tab[...]
    lam = coefficient(tab, 8)
    e1, e2 = coefficient(tab, slot + 2), coefficient(tab, slot + 3)
    for part in parts:
        parcel[pl.ds(jnp.where(first_core, n_out, 0), part.shape[0])] = part[...]

    def states(r):
        f_own, f_oth = feed_own[r], feed_oth[r]
        carry = cmul(e1, r1[r].astype(F32)) + cmul(e2, r2[r].astype(F32))
        s0 = cmul(lam, carry) + jnp.where(first_core, f_own, f_oth)
        s1 = cmul(lam, s0) + jnp.where(first_core, f_oth, f_own)
        return jnp.where(first_core, s1, s0), jnp.where(first_core, s0, s1)

    def emit(f, first_wide, size, depth, span):
        frame, dst = ((oth, parcel), (own, block))[f]
        mixed = conv_block(wide.at[f], weights, first_wide, size, order).reshape(size, w, c)
        act = 0.5 * mixed * (1.0 + lax.erf(mixed * np.float32(0.5**0.5)))
        for r in range(size):
            row = jnp.where(core == 1, rows - 1 - depth - r, depth + r)
            to = jnp.where(first_core, first_wide + r, span - 1 - first_wide - r)
            dst[to] = (frame[row].astype(F32) + act[r]).astype(BF16)

    if closing and 0 in which:
        parcel[parcel.shape[0] - 1] = rim[0]
    ready = 0
    for s in range(0, n_out, step):
        size = min(step, n_out - s)
        while ready < s + size + 2:
            if ready < n:
                pair = states(ready)
                for f in range(2):
                    if not closing and ready < 2:
                        kept_out[f, ready] = pair[f].astype(BF16)
                    if seam and ready >= n - 2:
                        near_out[f, ready - (n - 2)] = pair[f].astype(BF16)
                    if seam and ready == n - 1:
                        send[f] = pair[f].astype(BF16)
            else:
                pair = [kept[f, ready - n].astype(F32) for f in range(2)]
            for f in which:
                wide[f, ready] = widen(pair[f])
            ready += 1
        for f in which:
            emit(f, s, size, begin + s, parcel.shape[0] - (1 if closing else 0) if f == 0 else n_out)
    for copy in copies:
        copy.wait()


def start_rows(block, result, side, depth, sem):
    n = block.shape[0]
    start = jnp.where(side == 1, result.shape[0] - depth - n, depth)
    copy = pltpu.make_async_copy(block, result.at[pl.ds(start, n)], sem)
    copy.start()
    return copy


def output(
    tab, weights, feeds, arrived, own, oth, lo, hi, begin, end, slot, step, which, kept=None, seam=None, parts=(),
    blocks=(), blocks_at=(), result=None,
):
    rows, w, c = own.shape
    n, n_out = hi - lo, end - begin
    first, closing = kept is None, seam is not None
    args = [tab, weights, *arrived, own, oth, *feeds]
    args += ([] if first else [kept]) + (list(seam) if closing else []) + list(parts) + list(blocks)
    specs = [VMEM] * len(args)
    alias = {}
    shapes, out_specs = [], []
    extra = 1 if closing else 0
    if 0 in which:
        n_parcel = n_out + extra + sum(part.shape[0] for part in parts)
        shapes, out_specs = shapes + [jax.ShapeDtypeStruct((n_parcel, w, c), BF16)], out_specs + [VMEM]
    if 1 in which:
        shapes = shapes + [jax.ShapeDtypeStruct((n_out, w, c), BF16)]
        out_specs = out_specs + [VMEM]
    scratch = [pltpu.VMEM((2, n_out + 2, w, 3 * c), BF16)]
    if blocks:
        scratch += [pltpu.SemaphoreType.DMA((len(blocks),))]
        if result is not None:
            alias = {len(args): len(shapes)}
            args, specs = args + [result], specs + [HBM]
        shapes, out_specs = shapes + [jax.ShapeDtypeStruct(own.shape, BF16)], out_specs + [HBM]
    if not closing:
        shapes, out_specs = shapes + [jax.ShapeDtypeStruct((2, 2, w, c), BF16)], out_specs + [VMEM]
    if first:
        shapes = shapes + [jax.ShapeDtypeStruct((2, 2, w, c), BF16), jax.ShapeDtypeStruct((2, w, c), BF16)]
        out_specs = out_specs + [VMEM, VMEM]
    if 0 in which:
        shapes, out_specs = shapes + [jax.ShapeDtypeStruct(tab.shape, F32)], out_specs + [VMEM]
    return pl.pallas_call(
        functools.partial(
            output_kernel, lo, hi, begin, end, slot, step, which, first, closing, len(parts), blocks_at, result is not None
        ),
        out_shape=shapes,
        in_specs=specs,
        out_specs=out_specs,
        input_output_aliases=alias,
        scratch_shapes=scratch,
        compiler_params=PARAMS,
        cost_estimate=LONG if first else CLOSING if closing and 0 in which else SHORT,
        name="output",
    )(*args)


def rim_kernel(tab, weights, near, far, own, oth, rim, tab_next, wide):
    core = my_core()
    order = [jnp.where(core == 0, d, 2 - d) for d in range(3)]
    tab_next[...] = tab[...]
    depth = own.shape[0] // 2 - 1
    row = jnp.where(core == 1, own.shape[0] - 1 - depth, depth)
    for f, frame in enumerate((oth, own)):
        for k, z in enumerate((near[f, 0], near[f, 1], far[1 - f])):
            wide[f, k] = widen(z.astype(F32))
        mixed = conv_block(wide.at[f], weights, 0, 1, order)
        act = 0.5 * mixed * (1.0 + lax.erf(mixed * np.float32(0.5**0.5)))
        rim[f] = (frame[row].astype(F32) + act).astype(BF16)


def rim_rows(tab, weights, near, far, own, oth):
    w, c = own.shape[1:]
    return pl.pallas_call(
        rim_kernel,
        out_shape=[jax.ShapeDtypeStruct((2, w, c), BF16), jax.ShapeDtypeStruct(tab.shape, F32)],
        in_specs=[VMEM] * 6,
        out_specs=[VMEM] * 2,
        scratch_shapes=[pltpu.VMEM((2, 3, w, 3 * c), BF16)],
        compiler_params=PARAMS,
        cost_estimate=SHORT,
        name="rim",
    )(tab, weights, near, far, own, oth)


def place_kernel(depth, above, parcel, block, rim, early, earlier, _, result, sem):
    core = my_core()
    inner = result.shape[0] // 2 - 1
    n = parcel.shape[0] - 1
    copies = [
        start_rows(parcel.at[pl.ds(0, n)], result, 1 - core, depth, sem.at[0]),
        start_rows(parcel.at[pl.ds(n, 1)], result, 1 - core, inner, sem.at[1]),
        start_rows(block, result, core, depth, sem.at[2]),
        start_rows(rim.at[pl.ds(1, 1)], result, core, inner, sem.at[3]),
        start_rows(early, result, 1 - core, above, sem.at[4]),
        start_rows(earlier, result, core, above, sem.at[5]),
    ]
    for copy in copies:
        copy.wait()


def place(parcel, block, rim, early, earlier, depth, above, result):
    return pl.pallas_call(
        functools.partial(place_kernel, depth, above),
        out_shape=jax.ShapeDtypeStruct(result.shape, result.dtype),
        in_specs=[VMEM] * 5 + [HBM],
        out_specs=HBM,
        input_output_aliases={5: 0},
        scratch_shapes=[pltpu.SemaphoreType.DMA((6,))],
        compiler_params=PARAMS,
        name="place",
    )(parcel, block, rim, early, earlier, result)


ALONG_X = [(0, 1), (1, 0), (2, 3)], [(0, 2), (1, 3)]
ALONG_Y = [(0, 2), (1, 3)], [(0, 1), (2, 3), (3, 2)]


def roles(n):
    if n != 8:
        return [(q, slot, 0) for q in range(n // 2) for slot in (2, 6)]
    along_x = [(0, 0, 2), (0, 1, 0), (1, 0, 0), (1, 1, 2), (1, 2, 0), (2, 3, 0), (3, 2, 0), (3, 3, 2)]
    along_y = [(0, 4, 0), (2, 4, 0), (2, 5, 4), (3, 5, 0), (1, 7, 0), (2, 6, 2), (2, 7, 0), (3, 6, 2), (3, 7, 0)]
    return along_x + along_y


def both_cores(pairs):
    return [(2 * a + k, 2 * b + k) for a, b in pairs for k in range(2)]


def first_stage(n, slot, pair, decay, phase):
    if n == 8:
        return lax.ppermute(pair, "tm", both_cores((ALONG_X if slot == 0 else ALONG_Y)[0]))
    chips, stride, total = n // 2, 1, pair.astype(F32)
    while stride < chips:
        steps = both_cores([(i, i + stride) for i in range(chips - stride)])
        moved = lax.ppermute(total.astype(BF16), "tm", steps).astype(F32)
        size, angle = jnp.exp(-2.0 * stride * decay), 2.0 * stride * phase
        total = total + cmul((size * jnp.cos(angle), size * jnp.sin(angle)), moved)
        stride *= 2
    return lax.ppermute(total.astype(BF16), "tm", both_cores([(i, i + 1) for i in range(chips - 1)]))


def second_stage(n, slot, tab, pair, got, hint=SHORT):
    if n != 8:
        return jnp.zeros_like(got), tab
    pay, tab = relay(slot, tab, pair, got, hint)
    return lax.ppermute(pay, "tm", both_cores((ALONG_X if slot == 0 else ALONG_Y)[1])), tab


def on_device(n, n_space, frames_in, w_input, decay_rate, phase, w_output):
    own = frames_in[0]
    rows, w, c = own.shape
    decay, phase = decay_rate[None], phase[None]
    w_in = w_input.reshape(3, 3 * c, -1)
    w_out = w_output.reshape(3, -1, c)
    swap = [(i, i ^ 1) for i in range(n)]
    step = 3
    oth = lax.ppermute(own, "tm", swap)

    half = rows // 2
    total = half + 1
    last = max(3, total * 5 // 17)
    middle = max(2, total * 5 // 17)
    spans = [(last - 1 + middle, half), (last - 1, last - 1 + middle), (-1, last - 1)]
    links = [
        ((t ^ 1) * n_space + s, t * n_space + s + 1) if t % 2 == 0 else ((t ^ 1) * n_space + s + 1, t * n_space + s)
        for t in range(n)
        for s in range(n_space - 1)
    ]
    (lo1, hi1), (lo2, hi2), (lo3, hi3) = spans
    mine1, mine2, frame, weights, tab, factor = lead(roles(n), own, w_in, decay, phase, lo2, lo1, hi1, step)
    border, tab = outer_rows(frame, oth, tab)
    halo = lax.ppermute(border, ("tm", "space"), links)
    theirs1, pair1, tab = pair_up(oth, weights, tab, factor, mine1, lo1, hi1, step)
    got1 = first_stage(n, 0, pair1, decay, phase)
    theirs2, pair2, tab = pair_up(oth, weights, tab, factor, mine2, lo2, hi2, step)
    got2 = first_stage(n, 4, pair2, decay, phase)
    mine3, theirs3, pair3, tab = edge_chunk(frame, oth, weights, tab, factor, halo, lo3, hi3, step)
    got3 = first_stage(n, 0, pair3, decay, phase)
    also1, tab = second_stage(n, 0, tab, pair1, got1)
    also2, tab = second_stage(n, 4, tab, pair2, got2)
    also3, tab = second_stage(n, 0, tab, pair3, got3, pl.CostEstimate(flops=1, bytes_accessed=1, transcendentals=0))
    args = (w_out, (mine1, theirs1), (got1, also1), frame, oth, lo1, hi1, lo1 + 1, half - 1, 0, 2)
    parcel1, block1, kept, near, send, tab = output(tab, *args, (0, 1))
    far = lax.ppermute(send, "tm", swap)
    args = (w_out, (mine2, theirs2), (got2, also2), frame, oth, lo2, hi2, lo2 + 1, hi2 + 1, 4, 2)
    parcel2, block2, result, kept, tab = output(
        tab, *args, (0, 1), kept=kept, parts=(parcel1,), blocks=(block1,), blocks_at=((lo1 + 1, 1),)
    )
    early = lax.ppermute(parcel2, "tm", swap)
    rim, tab = rim_rows(tab, w_out, near, far, frame, oth)
    args = (w_out, (mine3, theirs3), (got3, also3), frame, oth, lo3, hi3, lo3 + 1, hi3 + 1, 0, 2)
    parcel, tab = output(tab, *args, (0,), kept=kept, seam=(rim,))
    (block3,) = output(tab, *args, (1,), kept=kept, seam=(rim,))
    return place(lax.ppermute(parcel, "tm", swap), block3, rim, early, block2, lo3 + 1, lo2 + 1, result)[None]


def solution(mesh):
    in_specs = (P("tm", "space", None, None), P(), P(), P(), P())
    out_specs = P("tm", "space", None, None)
    body = functools.partial(on_device, mesh.shape["tm"], mesh.shape["space"])
    return jax.shard_map(body, mesh=mesh, in_specs=in_specs, out_specs=out_specs, check_vma=False)
```

```python
import functools

import numpy as np
import jax
import jax.numpy as jnp
from jax import lax
from jax.experimental import pallas as pl
from jax.experimental.pallas import tpu as pltpu
from jax.sharding import PartitionSpec as P

F32 = jnp.float32
BF16 = jnp.bfloat16
VMEM = pl.BlockSpec(memory_space=pltpu.VMEM)
HBM = pl.BlockSpec(memory_space=pltpu.HBM)
PARAMS = pltpu.CompilerParams(vmem_limit_bytes=24 * 1024 * 1024)
SHORT = pl.CostEstimate(flops=1, bytes_accessed=1, transcendentals=0)
CLOSING = pl.CostEstimate(flops=4000000000, bytes_accessed=1, transcendentals=0)
LONG = pl.CostEstimate(flops=1, bytes_accessed=1, transcendentals=0)
SLOTS = 16


def cmul(coef, z):
    n = z.shape[-1] // 2
    re, im = z[..., :n], z[..., n:]
    cr, ci = coef
    return jnp.concatenate([cr * re - ci * im, cr * im + ci * re], axis=-1)


def coefficient(tab, i):
    return tab[i : i + 1, :], tab[SLOTS + i : SLOTS + i + 1, :]


def widen(row):
    w = row.shape[0]
    col = lax.broadcasted_iota(jnp.int32, row.shape, 0)
    left = jnp.where(col == 0, 0.0, pltpu.roll(row, 1, 0))
    right = jnp.where(col == w - 1, 0.0, pltpu.roll(row, w - 1, 0))
    return jnp.concatenate([left, row, right], axis=-1).astype(BF16)


def conv_block(wide, weights, start, count, order=(0, 1, 2)):
    w, k = wide.shape[1], wide.shape[2]
    lhs = jnp.concatenate(
        [wide[start + d : start + d + count].reshape(count * w, k) for d in range(3)], axis=-1
    )
    rhs = jnp.concatenate([weights[d] for d in order], axis=0)
    return jnp.dot(lhs, rhs, preferred_element_type=F32)


def load_weights(core, hbm, vmem, sem):
    copies = []
    for d in range(3):
        source = jnp.where(core == 1, 2 - d, d)
        copies.append(pltpu.make_async_copy(hbm.at[source], vmem.at[d], sem.at[d]))
        copies[-1].start()
    return copies


def my_core():
    return lax.rem(lax.axis_index("tm"), 2)


def convolve(weights, wide, row_of, n, step, finish):
    ready = 0
    for s in range(0, n, step):
        size = min(step, n - s)
        while ready < s + size + 2:
            wide[ready] = widen(row_of(ready))
            ready += 1
        finish(s, size, conv_block(wide, weights, s, size))


def lead_kernel(
    entries, lo, mid, hi, step, own, w_hbm, decay, phase, feed, feed_next, frame, weights, tab, factor, wide, dvec, sem
):
    core, chip = my_core(), lax.div(lax.axis_index("tm"), 2)
    rows = own.shape[0]
    n = hi - lo
    vectors = [pltpu.make_async_copy(ref, dvec.at[pl.ds(k, 1)], sem.at[3 + k]) for k, ref in enumerate((decay, phase))]
    for copy in vectors:
        copy.start()
    source = jnp.where(core == 1, rows - 1 - hi, lo - 1)
    near = pltpu.make_async_copy(own.at[pl.ds(source, n + 2)], frame.at[pl.ds(source, n + 2)], sem.at[5])
    near.start()
    wcopies = load_weights(core, w_hbm, weights, sem)
    for copy in vectors:
        copy.wait()
    expo, gate = [jnp.float32(0.0)] * SLOTS, [jnp.float32(0.0)] * SLOTS
    for q, slot, power in entries:
        expo[slot] = jnp.where(chip == q, jnp.float32(power), expo[slot])
        gate[slot] = jnp.where(chip == q, jnp.float32(1.0), gate[slot])
    for slot, power in ((8, 1), (9, 1 - core), (10, core)):
        expo[slot], gate[slot] = jnp.asarray(power).astype(F32), jnp.float32(1.0)
    spread = lambda values: jnp.concatenate([jnp.full((1, dvec.shape[1]), v, F32) for v in values], axis=0)
    expo = spread(expo)
    size = spread(gate) * jnp.exp(-expo * dvec[0:1])
    angle = expo * dvec[1:2]
    tab[...] = jnp.concatenate([size * jnp.cos(angle), size * jnp.sin(angle)], axis=0)
    mag = jnp.exp(-dvec[0:1])
    scale = jnp.sqrt(1.0 - mag * mag)
    factor[...] = jnp.concatenate([scale, scale], axis=-1)
    for copy in (*wcopies, near):
        copy.wait()
    rest = []
    for k, (begin, end) in enumerate(((0, lo - 1), (hi + 1, rows))):
        at = jnp.where(core == 1, rows - end, begin)
        rest.append(
            pltpu.make_async_copy(own.at[pl.ds(at, end - begin)], frame.at[pl.ds(at, end - begin)], sem.at[6 + k])
        )
        rest[-1].start()

    def row_of(p):
        return frame[source + jnp.where(core == 1, n + 1 - p, p)].astype(F32)

    def finish(s, count, acc):
        value = (acc * factor[...]).reshape((count,) + feed.shape[1:])
        for r in range(count):
            depth = lo + s + r
            if depth < mid:
                feed_next[depth - lo] = value[r]
            else:
                feed[depth - mid] = value[r]

    convolve(weights, wide, row_of, n, step, finish)
    for copy in rest:
        copy.wait()


def lead(entries, own, w_in, decay, phase, lo, mid, hi, step):
    rows, w, c = own.shape
    n = hi - lo
    return pl.pallas_call(
        functools.partial(lead_kernel, entries, lo, mid, hi, step),
        out_shape=[
            jax.ShapeDtypeStruct((hi - mid, w, c), F32),
            jax.ShapeDtypeStruct((mid - lo, w, c), F32),
            jax.ShapeDtypeStruct(own.shape, BF16),
            jax.ShapeDtypeStruct(w_in.shape, BF16),
            jax.ShapeDtypeStruct((2 * SLOTS, decay.shape[1]), F32),
            jax.ShapeDtypeStruct((1, 2 * decay.shape[1]), F32),
        ],
        in_specs=[HBM] * 4,
        out_specs=[VMEM] * 6,
        scratch_shapes=[
            pltpu.VMEM((n + 2, w, 3 * c), BF16),
            pltpu.VMEM((2, decay.shape[1]), F32),
            pltpu.SemaphoreType.DMA((8,)),
        ],
        compiler_params=PARAMS,
        cost_estimate=SHORT,
        name="lead",
    )(*(pltpu.with_memory_space_constraint(x, pltpu.HBM) for x in (own, w_in, decay, phase)))


def pair_kernel(lo, hi, step, oth, weights, tab, factor, feed_own, feed, pay, tab_next, wide):
    core = my_core()
    rows = oth.shape[0]
    n = hi - lo
    tab_next[...] = tab[...]
    source = jnp.where(core == 1, rows - 1 - hi, lo - 1)

    def row_of(p):
        return oth[source + jnp.where(core == 1, n + 1 - p, p)].astype(F32)

    def finish(s, count, acc):
        value = (acc * factor[...]).reshape((count,) + feed.shape[1:])
        feed[s : s + count] = value
        for r in range(count):
            pair = cmul(coefficient(tab, 9), feed_own[s + r]) + cmul(coefficient(tab, 10), value[r])
            pay[s + r] = pair.astype(BF16)

    convolve(weights, wide, row_of, n, step, finish)


def pair_up(oth, weights, tab, factor, feed_own, lo, hi, step):
    rows, w, c = oth.shape
    n = hi - lo
    return pl.pallas_call(
        functools.partial(pair_kernel, lo, hi, step),
        out_shape=[
            jax.ShapeDtypeStruct((n, w, c), F32),
            jax.ShapeDtypeStruct((n, w, c), BF16),
            jax.ShapeDtypeStruct(tab.shape, F32),
        ],
        in_specs=[VMEM] * 5,
        out_specs=[VMEM] * 3,
        scratch_shapes=[pltpu.VMEM((n + 2, w, 3 * c), BF16)],
        compiler_params=PARAMS,
        cost_estimate=SHORT,
        name="pair",
    )(oth, weights, tab, factor, feed_own)


def border_kernel(frame, oth, tab, border, tab_next):
    tab_next[...] = tab[...]
    at = my_core() * (frame.shape[0] - 2)
    for f, ref in enumerate((frame, oth)):
        for r in range(2):
            border[f, r] = ref[at + r]


def outer_rows(frame, oth, tab):
    return pl.pallas_call(
        border_kernel,
        out_shape=[
            jax.ShapeDtypeStruct((2, 2) + frame.shape[1:], BF16),
            jax.ShapeDtypeStruct(tab.shape, F32),
        ],
        in_specs=[VMEM] * 3,
        out_specs=[VMEM] * 2,
        compiler_params=PARAMS,
        cost_estimate=SHORT,
        name="border",
    )(frame, oth, tab)


def edge_kernel(
    lo, hi, step, frame, oth, weights, tab, factor, halo, feed_own, feed_oth, pay, tab_next, wide
):
    core = my_core()
    rows = frame.shape[0]
    n = hi - lo
    tab_next[...] = tab[...]
    outer = jnp.where(core == 1, lax.axis_size("space") - 1, 0)
    inside = jnp.where(lax.axis_index("space") == outer, 0.0, 1.0)
    for f, (ref, feed) in enumerate(((frame, feed_own), (oth, feed_oth))):

        def row_of(p):
            depth = lo - 1 + p
            if depth < 0:
                return halo[1 - f, jnp.where(core == 1, -1 - depth, 2 + depth)].astype(F32)
            return ref[jnp.where(core == 1, rows - 1 - depth, depth)].astype(F32)

        def finish(s, count, acc):
            value = (acc * factor[...]).reshape((count,) + feed.shape[1:])
            for r in range(count):
                row = value[r]
                if lo + s + r < 0:
                    row = row * inside
                feed[s + r] = row
                if f == 1:
                    pair = cmul(coefficient(tab, 9), feed_own[s + r]) + cmul(coefficient(tab, 10), row)
                    pay[s + r] = pair.astype(BF16)

        convolve(weights, wide.at[f], row_of, n, step, finish)


def edge_chunk(frame, oth, weights, tab, factor, halo, lo, hi, step):
    rows, w, c = frame.shape
    n = hi - lo
    return pl.pallas_call(
        functools.partial(edge_kernel, lo, hi, step),
        out_shape=[
            jax.ShapeDtypeStruct((n, w, c), F32),
            jax.ShapeDtypeStruct((n, w, c), F32),
            jax.ShapeDtypeStruct((n, w, c), BF16),
            jax.ShapeDtypeStruct(tab.shape, F32),
        ],
        in_specs=[VMEM] * 6,
        out_specs=[VMEM] * 4,
        scratch_shapes=[pltpu.VMEM((2, n + 2, w, 3 * c), BF16)],
        compiler_params=PARAMS,
        cost_estimate=pl.CostEstimate(flops=1, bytes_accessed=1, transcendentals=0),
        name="edge",
    )(frame, oth, weights, tab, factor, halo)


def relay_kernel(slot, tab, pair, got, pay, tab_next):
    tab_next[...] = tab[...]
    cp, cr = coefficient(tab, slot), coefficient(tab, slot + 1)
    for r in range(pair.shape[0]):
        pay[r] = (cmul(cp, pair[r].astype(F32)) + cmul(cr, got[r].astype(F32))).astype(BF16)


def relay(slot, tab, pair, got, hint=SHORT):
    return pl.pallas_call(
        functools.partial(relay_kernel, slot),
        out_shape=[jax.ShapeDtypeStruct(pair.shape, BF16), jax.ShapeDtypeStruct(tab.shape, F32)],
        in_specs=[VMEM] * 3,
        out_specs=[VMEM] * 2,
        compiler_params=PARAMS,
        cost_estimate=hint,
        name="relay",
    )(tab, pair, got)


def output_kernel(lo, hi, begin, end, slot, step, which, seam, closing, n_parts, blocks_at, more, *refs):
    refs = list(refs)
    take = lambda k: [refs.pop(0) for _ in range(k)]
    tab, weights, r1, r2, own, oth, feed_own, feed_oth = take(8)
    kept = take(1)[0] if not seam else None
    rim = take(1)[0] if closing else None
    parts = take(n_parts)
    blocks = take(len(blocks_at))
    take(1 if more else 0)
    parcel = take(1)[0] if 0 in which else None
    block = take(1)[0] if 1 in which else None
    result = take(1)[0] if blocks_at else None
    kept_out = take(1)[0] if not closing else None
    near_out, send = take(2) if seam else (None, None)
    tab_next = take(1)[0] if 0 in which else None
    wide = take(1)[0]
    core = my_core()
    first_core = core == 0
    order = [jnp.where(first_core, d, 2 - d) for d in range(3)]
    n, n_out = hi - lo, end - begin
    w, c = own.shape[1:]
    rows = own.shape[0]
    copies = []
    for ref, (depth, mine) in zip(blocks, blocks_at):
        copies.append(start_rows(ref, result, core if mine else 1 - core, depth, refs[0].at[len(copies)]))
    if tab_next is not None:
        tab_next[...] = tab[...]
    lam = coefficient(tab, 8)
    e1, e2 = coefficient(tab, slot + 2), coefficient(tab, slot + 3)
    for part in parts:
        parcel[pl.ds(jnp.where(first_core, n_out, 0), part.shape[0])] = part[...]

    def states(r):
        f_own, f_oth = feed_own[r], feed_oth[r]
        carry = cmul(e1, r1[r].astype(F32)) + cmul(e2, r2[r].astype(F32))
        s0 = cmul(lam, carry) + jnp.where(first_core, f_own, f_oth)
        s1 = cmul(lam, s0) + jnp.where(first_core, f_oth, f_own)
        return jnp.where(first_core, s1, s0), jnp.where(first_core, s0, s1)

    def emit(f, first_wide, size, depth, span):
        frame, dst = ((oth, parcel), (own, block))[f]
        mixed = conv_block(wide.at[f], weights, first_wide, size, order).reshape(size, w, c)
        act = 0.5 * mixed * (1.0 + lax.erf(mixed * np.float32(0.5**0.5)))
        for r in range(size):
            row = jnp.where(core == 1, rows - 1 - depth - r, depth + r)
            to = jnp.where(first_core, first_wide + r, span - 1 - first_wide - r)
            dst[to] = (frame[row].astype(F32) + act[r]).astype(BF16)

    if closing and 0 in which:
        parcel[parcel.shape[0] - 1] = rim[0]
    ready = 0
    for s in range(0, n_out, step):
        size = min(step, n_out - s)
        while ready < s + size + 2:
            if ready < n:
                pair = states(ready)
                for f in range(2):
                    if not closing and ready < 2:
                        kept_out[f, ready] = pair[f].astype(BF16)
                    if seam and ready >= n - 2:
                        near_out[f, ready - (n - 2)] = pair[f].astype(BF16)
                    if seam and ready == n - 1:
                        send[f] = pair[f].astype(BF16)
            else:
                pair = [kept[f, ready - n].astype(F32) for f in range(2)]
            for f in which:
                wide[f, ready] = widen(pair[f])
            ready += 1
        for f in which:
            emit(f, s, size, begin + s, parcel.shape[0] - (1 if closing else 0) if f == 0 else n_out)
    for copy in copies:
        copy.wait()


def start_rows(block, result, side, depth, sem):
    n = block.shape[0]
    start = jnp.where(side == 1, result.shape[0] - depth - n, depth)
    copy = pltpu.make_async_copy(block, result.at[pl.ds(start, n)], sem)
    copy.start()
    return copy


def output(
    tab, weights, feeds, arrived, own, oth, lo, hi, begin, end, slot, step, which, kept=None, seam=None, parts=(),
    blocks=(), blocks_at=(), result=None,
):
    rows, w, c = own.shape
    n, n_out = hi - lo, end - begin
    first, closing = kept is None, seam is not None
    args = [tab, weights, *arrived, own, oth, *feeds]
    args += ([] if first else [kept]) + (list(seam) if closing else []) + list(parts) + list(blocks)
    specs = [VMEM] * len(args)
    alias = {}
    shapes, out_specs = [], []
    extra = 1 if closing else 0
    if 0 in which:
        n_parcel = n_out + extra + sum(part.shape[0] for part in parts)
        shapes, out_specs = shapes + [jax.ShapeDtypeStruct((n_parcel, w, c), BF16)], out_specs + [VMEM]
    if 1 in which:
        shapes = shapes + [jax.ShapeDtypeStruct((n_out, w, c), BF16)]
        out_specs = out_specs + [VMEM]
    scratch = [pltpu.VMEM((2, n_out + 2, w, 3 * c), BF16)]
    if blocks:
        scratch += [pltpu.SemaphoreType.DMA((len(blocks),))]
        if result is not None:
            alias = {len(args): len(shapes)}
            args, specs = args + [result], specs + [HBM]
        shapes, out_specs = shapes + [jax.ShapeDtypeStruct(own.shape, BF16)], out_specs + [HBM]
    if not closing:
        shapes, out_specs = shapes + [jax.ShapeDtypeStruct((2, 2, w, c), BF16)], out_specs + [VMEM]
    if first:
        shapes = shapes + [jax.ShapeDtypeStruct((2, 2, w, c), BF16), jax.ShapeDtypeStruct((2, w, c), BF16)]
        out_specs = out_specs + [VMEM, VMEM]
    if 0 in which:
        shapes, out_specs = shapes + [jax.ShapeDtypeStruct(tab.shape, F32)], out_specs + [VMEM]
    return pl.pallas_call(
        functools.partial(
            output_kernel, lo, hi, begin, end, slot, step, which, first, closing, len(parts), blocks_at, result is not None
        ),
        out_shape=shapes,
        in_specs=specs,
        out_specs=out_specs,
        input_output_aliases=alias,
        scratch_shapes=scratch,
        compiler_params=PARAMS,
        cost_estimate=LONG if first else CLOSING if closing and 0 in which else SHORT,
        name="output",
    )(*args)


def rim_kernel(tab, weights, near, far, own, oth, rim, tab_next, wide):
    core = my_core()
    order = [jnp.where(core == 0, d, 2 - d) for d in range(3)]
    tab_next[...] = tab[...]
    depth = own.shape[0] // 2 - 1
    row = jnp.where(core == 1, own.shape[0] - 1 - depth, depth)
    for f, frame in enumerate((oth, own)):
        for k, z in enumerate((near[f, 0], near[f, 1], far[1 - f])):
            wide[f, k] = widen(z.astype(F32))
        mixed = conv_block(wide.at[f], weights, 0, 1, order)
        act = 0.5 * mixed * (1.0 + lax.erf(mixed * np.float32(0.5**0.5)))
        rim[f] = (frame[row].astype(F32) + act).astype(BF16)


def rim_rows(tab, weights, near, far, own, oth):
    w, c = own.shape[1:]
    return pl.pallas_call(
        rim_kernel,
        out_shape=[jax.ShapeDtypeStruct((2, w, c), BF16), jax.ShapeDtypeStruct(tab.shape, F32)],
        in_specs=[VMEM] * 6,
        out_specs=[VMEM] * 2,
        scratch_shapes=[pltpu.VMEM((2, 3, w, 3 * c), BF16)],
        compiler_params=PARAMS,
        cost_estimate=SHORT,
        name="rim",
    )(tab, weights, near, far, own, oth)


def place_kernel(depth, above, parcel, block, rim, early, _, result, sem):
    core = my_core()
    inner = result.shape[0] // 2 - 1
    n = parcel.shape[0] - 1
    copies = [
        start_rows(parcel.at[pl.ds(0, n)], result, 1 - core, depth, sem.at[0]),
        start_rows(parcel.at[pl.ds(n, 1)], result, 1 - core, inner, sem.at[1]),
        start_rows(block, result, core, depth, sem.at[2]),
        start_rows(rim.at[pl.ds(1, 1)], result, core, inner, sem.at[3]),
        start_rows(early, result, 1 - core, above, sem.at[4]),
    ]
    for copy in copies:
        copy.wait()


def place(parcel, block, rim, early, depth, above, result):
    return pl.pallas_call(
        functools.partial(place_kernel, depth, above),
        out_shape=jax.ShapeDtypeStruct(result.shape, result.dtype),
        in_specs=[VMEM] * 4 + [HBM],
        out_specs=HBM,
        input_output_aliases={4: 0},
        scratch_shapes=[pltpu.SemaphoreType.DMA((5,))],
        compiler_params=PARAMS,
        name="place",
    )(parcel, block, rim, early, result)


ALONG_X = [(0, 1), (1, 0), (2, 3)], [(0, 2), (1, 3)]
ALONG_Y = [(0, 2), (1, 3)], [(0, 1), (2, 3), (3, 2)]


def roles(n):
    if n != 8:
        return [(q, slot, 0) for q in range(n // 2) for slot in (2, 6)]
    along_x = [(0, 0, 2), (0, 1, 0), (1, 0, 0), (1, 1, 2), (1, 2, 0), (2, 3, 0), (3, 2, 0), (3, 3, 2)]
    along_y = [(0, 4, 0), (2, 4, 0), (2, 5, 4), (3, 5, 0), (1, 7, 0), (2, 6, 2), (2, 7, 0), (3, 6, 2), (3, 7, 0)]
    return along_x + along_y


def both_cores(pairs):
    return [(2 * a + k, 2 * b + k) for a, b in pairs for k in range(2)]


def first_stage(n, slot, pair, decay, phase):
    if n == 8:
        return lax.ppermute(pair, "tm", both_cores((ALONG_X if slot == 0 else ALONG_Y)[0]))
    chips, stride, total = n // 2, 1, pair.astype(F32)
    while stride < chips:
        steps = both_cores([(i, i + stride) for i in range(chips - stride)])
        moved = lax.ppermute(total.astype(BF16), "tm", steps).astype(F32)
        size, angle = jnp.exp(-2.0 * stride * decay), 2.0 * stride * phase
        total = total + cmul((size * jnp.cos(angle), size * jnp.sin(angle)), moved)
        stride *= 2
    return lax.ppermute(total.astype(BF16), "tm", both_cores([(i, i + 1) for i in range(chips - 1)]))


def second_stage(n, slot, tab, pair, got, hint=SHORT):
    if n != 8:
        return jnp.zeros_like(got), tab
    pay, tab = relay(slot, tab, pair, got, hint)
    return lax.ppermute(pay, "tm", both_cores((ALONG_X if slot == 0 else ALONG_Y)[1])), tab


def on_device(n, n_space, frames_in, w_input, decay_rate, phase, w_output):
    own = frames_in[0]
    rows, w, c = own.shape
    decay, phase = decay_rate[None], phase[None]
    w_in = w_input.reshape(3, 3 * c, -1)
    w_out = w_output.reshape(3, -1, c)
    swap = [(i, i ^ 1) for i in range(n)]
    step = 3
    oth = lax.ppermute(own, "tm", swap)

    half = rows // 2
    total = half + 1
    last = max(3, total * 5 // 17)
    middle = max(2, total * 5 // 17)
    spans = [(last - 1 + middle, half), (last - 1, last - 1 + middle), (-1, last - 1)]
    links = [
        ((t ^ 1) * n_space + s, t * n_space + s + 1) if t % 2 == 0 else ((t ^ 1) * n_space + s + 1, t * n_space + s)
        for t in range(n)
        for s in range(n_space - 1)
    ]
    (lo1, hi1), (lo2, hi2), (lo3, hi3) = spans
    mine1, mine2, frame, weights, tab, factor = lead(roles(n), own, w_in, decay, phase, lo2, lo1, hi1, step)
    border, tab = outer_rows(frame, oth, tab)
    halo = lax.ppermute(border, ("tm", "space"), links)
    theirs1, pair1, tab = pair_up(oth, weights, tab, factor, mine1, lo1, hi1, step)
    got1 = first_stage(n, 0, pair1, decay, phase)
    theirs2, pair2, tab = pair_up(oth, weights, tab, factor, mine2, lo2, hi2, step)
    got2 = first_stage(n, 4, pair2, decay, phase)
    mine3, theirs3, pair3, tab = edge_chunk(frame, oth, weights, tab, factor, halo, lo3, hi3, step)
    got3 = first_stage(n, 0, pair3, decay, phase)
    also1, tab = second_stage(n, 0, tab, pair1, got1)
    also2, tab = second_stage(n, 4, tab, pair2, got2)
    also3, tab = second_stage(n, 0, tab, pair3, got3, pl.CostEstimate(flops=1, bytes_accessed=1, transcendentals=0))
    args = (w_out, (mine1, theirs1), (got1, also1), frame, oth, lo1, hi1, lo1 + 1, half - 1, 0, 2)
    parcel1, block1, kept, near, send, tab = output(tab, *args, (0, 1))
    far = lax.ppermute(send, "tm", swap)
    args = (w_out, (mine2, theirs2), (got2, also2), frame, oth, lo2, hi2, lo2 + 1, hi2 + 1, 4, 2)
    parcel2, block2, result, kept, tab = output(
        tab, *args, (0, 1), kept=kept, parts=(parcel1,), blocks=(block1,), blocks_at=((lo1 + 1, 1),)
    )
    early = lax.ppermute(parcel2, "tm", swap)
    rim, tab = rim_rows(tab, w_out, near, far, frame, oth)
    args = (w_out, (mine3, theirs3), (got3, also3), frame, oth, lo3, hi3, lo3 + 1, hi3 + 1, 0, 2)
    parcel, tab = output(tab, *args, (0,), kept=kept, seam=(rim,))
    block3, result = output(
        tab, *args, (1,), kept=kept, seam=(rim,), blocks=(block2,), blocks_at=((lo2 + 1, 1),), result=result
    )
    return place(lax.ppermute(parcel, "tm", swap), block3, rim, early, lo3 + 1, lo2 + 1, result)[None]


def solution(mesh):
    in_specs = (P("tm", "space", None, None), P(), P(), P(), P())
    out_specs = P("tm", "space", None, None)
    body = functools.partial(on_device, mesh.shape["tm"], mesh.shape["space"])
    return jax.shard_map(body, mesh=mesh, in_specs=in_specs, out_specs=out_specs, check_vma=False)
```
